32 devices in a mesh: gx: 8 (over z, core), gy: 4 (over y, x).
Axes of the slice: x: 2, y: 2, z: 4, core: 2. Of those that a mesh axis runs over, the one named last changes fastest.
Arguments:
- particles: float32 [8, 262144], P(None, ('gx', 'gy'))
- old_density: float32 [262144], P(('gx', 'gy')), may hold values from 0.5 to 4
- active: int32 [262144], P(('gx', 'gy')), may hold values 0 or 1
- send_rows: int32 [4, 65536], P(None, ('gx', 'gy')), may hold values from 0 to 8191, as said below
- send_count: int32 [4, 32], P(None, ('gx', 'gy')), may hold values from 682 to 2048, as said below
- export_rows: int32 [8, 32768], P(None, ('gx', 'gy')), may hold values from 0 to 8191
- pair_tiles: int32 [2, 16384], P(None, ('gx', 'gy')), may hold values from 0 to 255, as said below
- pair_count: int32 [32], P(('gx', 'gy')), may hold values from 128 to 512, as said below
Outputs:
- density: float32 [262144], P(('gx', 'gy'))
- acceleration: float32 [3, 262144], P(None, ('gx', 'gy'))
- heating: float32 [262144], P(('gx', 'gy'))
The draws below stay inside these ranges and needn't reach their ends.
Inputs may be any that keep to these rules, and one draw needn't show every extreme that they name: `send_rows`: within one level and one device the 2048 offered rows are distinct local rows. `send_count`: the two devices that a level pairs have the same count; at every level some pair exchanges all 2048 offered rows. `pair_tiles`: a pair's source tile differs from its target tile; target tiles are below 128. `pair_count`: some device uses all 512 slots.
All inputs are finite; a program needn't handle non-finite values. No bound on the sum of `active` on one device may be relied on, other than what follows from the above.
Results may differ from the reference program's by a relative error of at most 0.0003.
Values sent between devices are 32-bit elements; how exact they have to be, the bound alone decides.
No kernel may reach another device: no remote copies, remote signals or barrier semaphores. Data moves between devices by JAX's collectives and lax.ppermute only.
A program may use at most 64 MiB of HBM per device.

```python
import math
import jax
import jax.numpy as jnp
from jax import lax

ROWS = 8192
NPAIR = 512
LEVELS = 4
FIELDS = 8
TILE = 64
SEND = 2048
GHOSTS = 1024
NTILE = 128
POOLT = 256
PARTS_SIZE = 262144
N_GX = 8
N_GY = 4


def draw_particles(key, part):
    keys = jax.random.split(key, 4)
    position = jax.random.uniform(keys[0], (3, PARTS_SIZE), jnp.float32)
    velocity = jax.random.normal(keys[1], (3, PARTS_SIZE), jnp.float32)
    smooth = jax.random.uniform(keys[2], (1, PARTS_SIZE), jnp.float32, 0.12, 0.25)
    energy = jnp.exp(jax.random.uniform(keys[3], (1, PARTS_SIZE), jnp.float32, jnp.log(0.5), jnp.log(2.0)))
    return jnp.concatenate([position, velocity, smooth, energy], axis=0)


def draw_send_rows(key, part):
    devices = N_GX * N_GY
    keys = jax.random.split(key, LEVELS * devices)
    chosen = jax.vmap(lambda k: jax.random.permutation(k, ROWS)[:SEND])(keys)
    return chosen.reshape(LEVELS, devices * SEND).astype(jnp.int32)


def draw_send_count(key, part):
    devices = N_GX * N_GY
    bits_x = N_GX.bit_length() - 1
    bits_y = N_GY.bit_length() - 1
    masks = (1 << bits_y + bits_x - 1, 1 << bits_y + bits_x - 2, 1 << bits_y - 1, 1 << bits_y - 2)
    raw = jax.random.randint(key, (LEVELS, devices), SEND // 3, SEND + 1, dtype=jnp.int32)
    raw = raw.at[:, 0].set(SEND)
    ranks = jnp.arange(devices, dtype=jnp.int32)
    result = []
    for section_level in range(LEVELS):
        lower = jnp.bitwise_and(ranks, devices - 1 - masks[section_level])
        result.append(raw[section_level][lower])
    return jnp.stack(result, axis=0)


def draw_pair_tiles(key, part):
    devices = N_GX * N_GY
    keys = jax.random.split(jax.random.fold_in(key, 11), 2)
    targets = jax.random.randint(keys[0], (devices * NPAIR,), 0, NTILE, dtype=jnp.int32)
    raw = jax.random.randint(keys[1], (devices * NPAIR,), 0, POOLT - 1, dtype=jnp.int32)
    sources = raw + (raw >= targets).astype(jnp.int32)
    return jnp.stack([targets, sources], axis=0)


def draw_pair_count(key, part):
    devices = N_GX * N_GY
    counts = jax.random.randint(jax.random.fold_in(key, 23), (devices,), NPAIR // 4, NPAIR + 1, dtype=jnp.int32)
    return counts.at[0].set(NPAIR)


def plant(values, own_key, smallest, high):
    shape = values.shape
    place = [jax.random.randint(jax.random.fold_in(own_key, axis), (), 0, shape[axis]) for axis in range(len(shape))]
    values = values.at[tuple(place)].set(smallest)
    longest = shape.index(max(shape))
    place[longest] = (place[longest] + 1) % shape[longest]
    return values.at[tuple(place)].set(high)


def shard_levels(key, shape, cuts, smallest, top_value):
    def one(axis_at, blocks):
        draws = jax.random.uniform(jax.random.fold_in(jax.random.fold_in(key, 6), axis_at), (blocks,), jnp.float32, smallest / len(cuts), top_value / len(cuts))
        return jnp.repeat(jnp.exp(draws), shape[axis_at] // blocks).reshape((-1,) + (1,) * (len(shape) - axis_at - 1))

    loudness = one(*cuts[0])
    for cut in cuts[1:]:
        loudness = loudness * one(*cut)
    return loudness


def setup_inputs(seed: int = 0) -> dict:
    key_list = jax.random.split(jax.random.key(seed), 9)
    return {
        "particles": draw_particles(jax.random.fold_in(key_list[8], 71), 0),
        "old_density": jnp.clip(jnp.exp(math.log(4.0) - 2.0794415 * jax.random.uniform(key_list[1], (PARTS_SIZE,), jnp.float32) ** shard_levels(key_list[1], (PARTS_SIZE,), ((0, 32),), -0.2, 0.2)), 0.5, 4.0),
        "active": plant((jax.random.randint(key_list[2], (PARTS_SIZE,), 0, 4) < 1).astype(jnp.int32), jax.random.fold_in(key_list[2], 1), 0, 1),
        "send_rows": draw_send_rows(jax.random.fold_in(key_list[8], 71), 0),
        "send_count": draw_send_count(jax.random.fold_in(key_list[8], 71), 0),
        "export_rows": plant(jax.random.randint(key_list[5], (8, GHOSTS * N_GX * N_GY), 0, ROWS), jax.random.fold_in(key_list[5], 1), 0, ROWS - 1).astype(jnp.int32),
        "pair_tiles": draw_pair_tiles(jax.random.fold_in(key_list[8], 71), 0),
        "pair_count": draw_pair_count(jax.random.fold_in(key_list[8], 71), 0),
    }


PARTICLE_MASS = 1.0 / 512.0
ADIABATIC = 5.0 / 3.0
directions = ((-1, -1), (-1, 0), (-1, 1), (0, -1), (0, 1), (1, -1), (1, 0), (1, 1))

def kernel_value(dist_sq, smooth):
    q = jnp.sqrt(dist_sq) / smooth
    inner_part = 1.0 - 1.5 * q * q + 0.75 * q * q * q
    outer_part = 0.25 * (2.0 - q) ** 3
    profile = jnp.where(q < 1.0, inner_part, jnp.where(q < 2.0, outer_part, 0.0))
    return profile / (jnp.pi * smooth * smooth * smooth)

def kernel_slope(dist_sq, smooth):
    q = jnp.sqrt(dist_sq) / smooth
    inner_part = -3.0 + 2.25 * q
    outer_part = -0.75 * (2.0 - q) ** 2 / jnp.maximum(q, 1.0)
    profile = jnp.where(q < 1.0, inner_part, jnp.where(q < 2.0, outer_part, 0.0))
    return profile / (jnp.pi * smooth ** 5)

def separation(target_rows, source_rows):
    offset = target_rows[0:3, :, :, None] - source_rows[0:3, :, None, :]
    offset = offset - jnp.floor(offset + 0.5)
    return (offset, lax.optimization_barrier(jnp.sum(offset * offset, axis=0)))

def tile_select(targets, in_list, tile_count):
    return ((targets[:, None] == jnp.arange(tile_count)[None, :]) & in_list[:, None]).astype(jnp.float32)

def density_block(tile_view, targets, sources, in_list, tile_count):
    target_rows = jnp.take(tile_view, targets, axis=1)
    source_rows = jnp.take(tile_view, sources, axis=1)
    offset, dist_sq = separation(target_rows, source_rows)
    terms = PARTICLE_MASS * lax.optimization_barrier(jnp.sum(kernel_value(dist_sq, target_rows[6][:, :, None]), axis=2))
    onehot = tile_select(targets, in_list, tile_count)
    return jnp.einsum('bt,br->tr', onehot, terms, precision=lax.Precision.HIGHEST)

def force_block(tile_view, press_view, targets, sources, in_list, tile_count):
    target_rows = jnp.take(tile_view, targets, axis=1)
    source_rows = jnp.take(tile_view, sources, axis=1)
    target_press = jnp.take(press_view, targets, axis=0)
    source_press = jnp.take(press_view, sources, axis=0)
    offset, dist_sq = separation(target_rows, source_rows)
    slope = 0.5 * (kernel_slope(dist_sq, target_rows[6][:, :, None]) + kernel_slope(dist_sq, source_rows[6][:, None, :]))
    weight_pair = PARTICLE_MASS * (target_press[:, :, None] + source_press[:, None, :]) * slope
    acceleration = -lax.optimization_barrier(jnp.sum(weight_pair[None] * offset, axis=3))
    velocity_gap = target_rows[3:6, :, :, None] - source_rows[3:6, :, None, :]
    heating = 0.5 * lax.optimization_barrier(jnp.sum(weight_pair * lax.optimization_barrier(jnp.sum(velocity_gap * offset, axis=0)), axis=2))
    terms = jnp.concatenate([acceleration, heating[None]], axis=0)
    onehot = tile_select(targets, in_list, tile_count)
    return jnp.einsum('bt,kbr->ktr', onehot, terms, precision=lax.Precision.HIGHEST)

def device_density(pooled, pair_lists, used):
    tile_view = pooled.reshape(FIELDS, -1, TILE)
    tile_count = ROWS // TILE
    block_size = math.gcd(NPAIR, 64)

    def advance(running, which):
        begin = which * block_size
        targets = lax.dynamic_slice_in_dim(pair_lists[0], begin, block_size)
        sources = lax.dynamic_slice_in_dim(pair_lists[1], begin, block_size)
        in_list = begin + jnp.arange(block_size) < used
        return (running + density_block(tile_view, targets, sources, in_list, tile_count), None)
    start = jnp.zeros((tile_count, TILE), jnp.float32)
    total, _ = lax.scan(advance, start, jnp.arange(NPAIR // block_size))
    return total.reshape(ROWS)

def device_force(pooled, press_pool, pair_lists, used):
    tile_view = pooled.reshape(FIELDS, -1, TILE)
    press_view = press_pool.reshape(-1, TILE)
    tile_count = ROWS // TILE
    block_size = math.gcd(NPAIR, 64)

    def advance(running, which):
        begin = which * block_size
        targets = lax.dynamic_slice_in_dim(pair_lists[0], begin, block_size)
        sources = lax.dynamic_slice_in_dim(pair_lists[1], begin, block_size)
        in_list = begin + jnp.arange(block_size) < used
        return (running + force_block(tile_view, press_view, targets, sources, in_list, tile_count), None)
    start = jnp.zeros((4, tile_count, TILE), jnp.float32)
    total, _ = lax.scan(advance, start, jnp.arange(NPAIR // block_size))
    return total.reshape(4, ROWS)

def reference(particles, old_density, active, send_rows, send_count, export_rows, pair_tiles, pair_count):
    size_x = N_GX
    size_y = N_GY
    devices = size_x * size_y
    fields = particles.reshape(FIELDS, size_x, size_y, ROWS).transpose(1, 2, 0, 3)
    density_rows = old_density.reshape(size_x, size_y, ROWS)
    active_rows = active.reshape(size_x, size_y, ROWS)
    bits_x = size_x.bit_length() - 1
    bits_y = size_y.bit_length() - 1
    bisections = ((0, bits_x - 1), (0, bits_x - 2), (1, bits_y - 1), (1, bits_y - 2))
    for section_level in range(LEVELS):
        which_axis, bit_number = bisections[section_level]
        slots = send_rows[section_level].reshape(size_x, size_y, SEND)
        offered = send_count[section_level].reshape(size_x, size_y)
        taken = jnp.arange(SEND)[None, None, :] < offered[:, :, None]
        out_fields = jnp.take_along_axis(fields, slots[:, :, None, :], axis=3)
        out_density = jnp.take_along_axis(density_rows, slots, axis=2)
        out_active = jnp.take_along_axis(active_rows, slots, axis=2)
        extent = size_x if which_axis == 0 else size_y
        partner = jnp.bitwise_xor(jnp.arange(extent, dtype=jnp.int32), 1 << bit_number)
        in_fields = jnp.take(out_fields, partner, axis=which_axis)
        in_density = jnp.take(out_density, partner, axis=which_axis)
        in_active = jnp.take(out_active, partner, axis=which_axis)
        new_fields = jnp.where(taken[:, :, None, :], in_fields, out_fields)
        new_density = jnp.where(taken, in_density, out_density)
        new_active = jnp.where(taken, in_active, out_active)
        fields = jax.vmap(jax.vmap(lambda a, i, v: a.at[:, i].set(v)))(fields, slots, new_fields)
        density_rows = jax.vmap(jax.vmap(lambda a, i, v: a.at[i].set(v)))(density_rows, slots, new_density)
        active_rows = jax.vmap(jax.vmap(lambda a, i, v: a.at[i].set(v)))(active_rows, slots, new_active)
    exports = export_rows.reshape(8, size_x, size_y, GHOSTS)
    ghost_blocks = []
    for number in range(8):
        step_x, step_y = directions[number]
        portion = jnp.take_along_axis(fields, exports[number][:, :, None, :], axis=3)
        ghost_blocks.append(jnp.roll(portion, (step_x, step_y), axis=(0, 1)))
    pooled = jnp.concatenate([fields] + ghost_blocks, axis=3).reshape(devices, FIELDS, -1)
    pair_lists = pair_tiles.reshape(2, devices, NPAIR).transpose(1, 0, 2)
    kernel_sums = lax.map(lambda item: device_density(item[0], item[1], item[2]), (pooled, pair_lists, pair_count))
    smooth = fields[:, :, 6, :].reshape(devices, ROWS)
    recomputed = PARTICLE_MASS * kernel_value(jnp.zeros_like(smooth), smooth) + kernel_sums
    flat_active = active_rows.reshape(devices, ROWS)
    density_new = jnp.where(flat_active == 1, recomputed, density_rows.reshape(devices, ROWS))
    density_grid = density_new.reshape(size_x, size_y, ROWS)
    ghost_density = []
    for number in range(8):
        step_x, step_y = directions[number]
        portion = jnp.take_along_axis(density_grid, exports[number], axis=2)
        ghost_density.append(jnp.roll(portion, (step_x, step_y), axis=(0, 1)))
    pool_density = jnp.concatenate([density_grid] + ghost_density, axis=2).reshape(devices, -1)
    press_pool = (ADIABATIC - 1.0) * pooled[:, 7, :] / pool_density
    forces = lax.map(lambda item: device_force(item[0], item[1], item[2], item[3]), (pooled, press_pool, pair_lists, pair_count))
    forces = forces * flat_active.astype(jnp.float32)[:, None, :]
    acceleration = forces[:, 0:3, :].transpose(1, 0, 2).reshape(3, devices * ROWS)
    heating = forces[:, 3, :].reshape(devices * ROWS)
    return (density_new.reshape(devices * ROWS), acceleration, heating)
```

```python
import math

import jax
import jax.numpy as jnp
from jax import lax
from jax.experimental import pallas as pl
from jax.experimental.pallas import tpu as pltpu
from jax.sharding import PartitionSpec as P

TILE = 64
LANES = 128
UNROLL = 8

PARTICLE_MASS = 1.0 / 512.0
ADIABATIC = 5.0 / 3.0
F32 = jnp.float32
I32 = jnp.int32


def from_behind(value, axis, steps):
    count = lax.axis_size(axis)
    pairs = [(source, (source + steps) % count) for source in range(count)]
    return lax.ppermute(value, axis, pairs)


def from_partner(block, axis, bit):
    count = lax.axis_size(axis)
    route = []
    for low in range(count):
        high = low | 1 << bit
        if high != low and high < count:
            route += [(low, high), (high, low)]
    return lax.ppermute(block, axis, route)


def to_neighbours(low, middle, high, unit):
    low = from_behind(low, "gx", -1)
    high = from_behind(high, "gx", 1)
    down = jnp.concatenate([low[:unit], middle[:unit], high[:unit]], axis=0)
    up = jnp.concatenate([low[2 * unit :], middle[unit:], high[2 * unit :]], axis=0)
    down = from_behind(down, "gy", -1)
    up = from_behind(up, "gy", 1)
    return low, high, down, up


def ghost_place(unit):
    return ((2, 0), (0, unit), (3, 0), (2, unit), (3, unit), (2, 2 * unit), (1, unit), (3, 2 * unit))


def export_place(unit):
    return ((0, 0), (0, unit), (0, 2 * unit), (1, 0), (1, unit), (2, 0), (2, unit), (2, 2 * unit))


def lane_pick(table, index):
    return jnp.take_along_axis(table, index, axis=1, mode="promise_in_bounds")


def spread(row, rows=8):
    return jnp.broadcast_to(row, (rows, LANES))


def iota(shape, axis):
    return lax.broadcasted_iota(I32, shape, axis)


def aligned(value, size=8):
    return pl.multiple_of(value, size)


def gather_fields(field_ref, rows, block_count):
    high = [spread(row >> 7) for row in rows]
    low = [spread(row & 127) for row in rows]
    found = [jnp.zeros((8, LANES), F32) for _ in rows]
    for block in range(block_count):
        table = field_ref[:, LANES * block : LANES * (block + 1)]
        for u in range(len(rows)):
            found[u] = jnp.where(high[u] == block, lane_pick(table, low[u]), found[u])
    return found


def gather_outgoing(field_ref, flag_ref, send_ref, level, index_ref, out_ref):
    row_count = index_ref.shape[0]
    block_count = field_ref.shape[1] // LANES
    for j in range(row_count):
        index_ref[j : j + 1, :] = send_ref[level : level + 1, LANES * j : LANES * (j + 1)]

    def body(step, carry):
        rows = [index_ref[pl.ds(2 * step + u, 1), :] for u in range(2)]
        found = gather_fields(field_ref, rows, block_count)
        for u in range(2):
            out_ref[pl.ds(aligned((2 * step + u) * 8), 8), :] = found[u]
        return carry

    lax.fori_loop(0, row_count // 2, body, 0)
    base = 8 * row_count
    for part in range(row_count // 8):
        index = index_ref[8 * part : 8 * part + 8, :]
        high, low = index >> 7, index & 127
        found = jnp.zeros((8, LANES), F32)
        for block in range(block_count):
            table = spread(flag_ref[block : block + 1, :])
            found = jnp.where(high == block, lane_pick(table, low), found)
        out_ref[base + 8 * part : base + 8 * part + 8, :] = jnp.abs(found)
        out_ref[base + row_count + 8 * part : base + row_count + 8 * part + 8, :] = jnp.where(
            found > 0, 1.0, 0.0
        )


def apply_incoming(field_ref, flag_ref, inverse_ref, level, in_ref, new_field_ref, new_flag_ref, flag_in_ref):
    tile_rows = flag_ref.shape[0]
    in_blocks = flag_in_ref.shape[0]
    base = 8 * in_blocks
    density_in = in_ref[base : base + in_blocks, :]
    flag_in_ref[...] = jnp.where(
        in_ref[base + in_blocks : base + 2 * in_blocks, :] > 0.5, density_in, -density_in
    )
    first = level * tile_rows

    def body(step, carry):
        rows = [2 * step + u for u in range(2)]
        which = [inverse_ref[pl.ds(first + row, 1), :] - 1 for row in rows]
        high = [spread(w >> 7) for w in which]
        low = [spread(w & 127) for w in which]
        found = [field_ref[:, pl.ds(aligned(row * LANES, LANES), LANES)] for row in rows]
        for block in range(in_blocks):
            table = in_ref[8 * block : 8 * block + 8, :]
            for u in range(2):
                found[u] = jnp.where(high[u] == block, lane_pick(table, low[u]), found[u])
        for u in range(2):
            new_field_ref[:, pl.ds(aligned(rows[u] * LANES, LANES), LANES)] = found[u]
        return carry

    lax.fori_loop(0, tile_rows // 2, body, 0)

    for part in range(tile_rows // 8):
        which = inverse_ref[first + 8 * part : first + 8 * part + 8, :] - 1
        high, low = which >> 7, which & 127
        found = flag_ref[8 * part : 8 * part + 8, :]
        for block in range(in_blocks):
            table = spread(flag_in_ref[block : block + 1, :])
            found = jnp.where(high == block, lane_pick(table, low), found)
        new_flag_ref[8 * part : 8 * part + 8, :] = found


def first_kernel(field_ref, flag_ref, send_ref, out_ref, index_ref):
    gather_outgoing(field_ref, flag_ref, send_ref, 0, index_ref, out_ref)


def level_kernel(level, field_ref, flag_ref, inverse_ref, in_ref, send_ref, new_field_ref, new_flag_ref, out_ref, index_ref, flag_in_ref):
    apply_incoming(
        field_ref, flag_ref, inverse_ref, level, in_ref, new_field_ref, new_flag_ref, flag_in_ref
    )
    gather_outgoing(new_field_ref, new_flag_ref, send_ref, level + 1, index_ref, out_ref)


def last_kernel(level, field_ref, flag_ref, inverse_ref, in_ref, export_ref, new_field_ref, new_flag_ref, low_ref, middle_ref, high_ref, flag_in_ref):
    apply_incoming(
        field_ref, flag_ref, inverse_ref, level, in_ref, new_field_ref, new_flag_ref, flag_in_ref
    )
    outs = (low_ref, middle_ref, high_ref)
    blocks = export_ref.shape[1] // LANES
    block_count = field_ref.shape[1] // LANES
    place = export_place(8 * blocks)
    for number in range(8):
        target, start = place[number]

        def body(step, carry, number=number, target=target, start=start):
            rows = [
                export_ref[number : number + 1, pl.ds(aligned((2 * step + u) * LANES, LANES), LANES)]
                for u in range(2)
            ]
            found = gather_fields(new_field_ref, rows, block_count)
            for u in range(2):
                outs[target][pl.ds(aligned(start + (2 * step + u) * 8), 8), :] = found[u]
            return carry

        lax.fori_loop(0, blocks // 2, body, 0)


def inverse_kernel(count_ref, send_ref, inverse_ref):
    levels, slots = send_ref.shape
    tile_rows = inverse_ref.shape[0] // levels
    slot = iota((1, slots), 1)
    for level in range(levels):
        rows = send_ref[level : level + 1, :]
        taken = slot < count_ref[level]
        high = jnp.where(taken, rows >> 7, -1)
        low = rows & 127
        number = slot + 1
        hit = jnp.broadcast_to(high, (tile_rows, slots)) == iota((tile_rows, slots), 0)
        coarse = jnp.where(hit, jnp.broadcast_to((number >> 6).astype(F32), hit.shape), 0.0)
        fine = jnp.where(hit, jnp.broadcast_to((number & 63).astype(F32), hit.shape), 0.0)
        left = jnp.concatenate([coarse, fine], axis=0).astype(jnp.bfloat16)
        right = jnp.where(
            jnp.broadcast_to(low, (LANES, slots)) == iota((LANES, slots), 0), 1.0, 0.0
        ).astype(jnp.bfloat16)
        both = lax.dot_general(left, right, (((1,), (1,)), ((), ())), preferred_element_type=F32)
        total = both[:tile_rows] * 64.0 + both[tile_rows:]
        inverse_ref[level * tile_rows : (level + 1) * tile_rows, :] = total.astype(I32)


def target_kernel(field_ref, flag_ref, compact_ref, rank_ref, order_ref, chunks_ref, stack_ref):
    tile_rows = flag_ref.shape[0]
    groups = tile_rows // 16
    active = flag_ref[...] > 0
    ones = jnp.where(active, 1.0, 0.0).astype(jnp.bfloat16)
    a = iota((LANES, LANES), 0)
    b = iota((LANES, LANES), 1)
    same = (a >> 6) == (b >> 6)
    before = jnp.where(same & (a < b), 1.0, 0.0).astype(jnp.bfloat16)
    whole = jnp.where(same, 1.0, 0.0).astype(jnp.bfloat16)
    rank = jnp.dot(ones, before, preferred_element_type=F32).astype(I32)
    total = jnp.dot(ones, whole, preferred_element_type=F32)
    rank_ref[...] = rank
    chunks_ref[0] = (jnp.max(total).astype(I32) + 15) >> 4
    lane = iota((tile_rows, LANES), 1)
    code = jnp.where(active, lane + 128 * ((lane & 63) - rank), -1)
    for bit in range(6):
        moved = pltpu.roll(code, LANES - (1 << bit), 1)
        take = (moved >= 0) & (((moved >> (7 + bit)) & 1) == 1)
        keep = (code >= 0) & (((code >> (7 + bit)) & 1) == 0)
        code = jnp.where(take, moved, jnp.where(keep, code, -1))
    order_ref[...] = jnp.where(code >= 0, code & 127, lane)
    left_half = iota((8, LANES), 1) < 64
    for group in range(groups):
        for inner in range(16):
            row = group * 16 + inner
            stack_ref[8 * inner : 8 * inner + 8, :] = lane_pick(
                field_ref[:, LANES * row : LANES * (row + 1)], spread(order_ref[row : row + 1, :])
            )
        turned = jnp.transpose(stack_ref[...])
        for half in range(2):
            for chunk in range(4):
                first = half * 64 + chunk * 16
                near, far = turned[first : first + 8], turned[first + 8 : first + 16]
                for section in range(2):
                    if section == 0:
                        mixed = jnp.where(left_half, near, pltpu.roll(far, 64, 1))
                    else:
                        mixed = jnp.where(left_half, pltpu.roll(near, 64, 1), far)
                    place = (((chunk * groups + group) * 2 + section) * 2 + half) * 8
                    compact_ref[place : place + 8, :] = mixed


def expand_targets(compact_ref, chunk, groups, fields, emit):
    lane = iota((8, LANES), 1)
    half_base = jnp.where(lane < 64, 0, 64)
    for inner in range(8):
        for field in fields:
            index = half_base + (inner * 8 + field)
            for group in range(groups):
                for section in range(2):
                    for half in range(2):
                        place = ((group * 2 + section) * 2 + half) * 8
                        start = aligned(chunk * (groups * 32) + place)
                        tile = 2 * (group * 16 + section * 8 + inner) + half
                        emit(field, tile, lane_pick(compact_ref[pl.ds(start, 8), :], index))


def reduce_targets(sum_ref, first, tile_count, chunk, out_ref):
    lane = iota((8, LANES), 1)
    sub = iota((8, LANES), 0)
    left = lane < 64
    for block in range(tile_count // 16):
        near = jnp.zeros((8, LANES), F32)
        far = jnp.zeros((8, LANES), F32)
        for inner in range(16):
            place = first + (block * 16 + inner) * 8
            value = sum_ref[place : place + 8, :]
            here = lane == sub + inner * 8
            near_sum = jnp.sum(jnp.where(left, value, 0.0), axis=1, keepdims=True)
            far_sum = jnp.sum(jnp.where(left, 0.0, value), axis=1, keepdims=True)
            near = jnp.where(here, near_sum, near)
            far = jnp.where(here, far_sum, far)
        blocks = tile_count // 16
        out_ref[pl.ds((chunk * 2) * blocks + block, 1), :] = jnp.sum(near, axis=0, keepdims=True)
        out_ref[pl.ds((chunk * 2 + 1) * blocks + block, 1), :] = jnp.sum(far, axis=0, keepdims=True)


def place_results(red_ref, blocks, part, rank):
    row = iota((8, LANES), 0)
    half = iota((8, LANES), 1) >> 6
    index = (2 * row + half) * 8 + (rank & 7)
    which = rank >> 3
    found = jnp.zeros((8, LANES), F32)
    for section in range(8):
        table = spread(red_ref[section * blocks + part : section * blocks + part + 1, :])
        found = jnp.where(which == section, lane_pick(table, index), found)
    return found


def density_kernel(count_ref, chunks_ref, target_ref, source_ref, compact_ref, rank_ref, field_ref, flag_ref, low_ref, high_ref, down_ref, up_ref, export_ref,
                   density_ref, low_out, middle_out, high_out, pool_ref,
                   expanded_ref, sum_ref, red_ref, height_ref):
    tile_rows = flag_ref.shape[0]
    tile_count = 2 * tile_rows
    groups = tile_rows // 16
    region = (tile_count + 1) * 8
    left = iota((8, LANES), 1) < 64

    def write_doubled(row, value):
        other = pltpu.roll(value, 64, 1)
        pool_ref[pl.ds(aligned(row * 16), 8), :] = jnp.where(left, value, other)
        pool_ref[pl.ds(aligned(row * 16 + 8), 8), :] = jnp.where(left, other, value)

    for row in range(tile_rows):
        write_doubled(row, field_ref[:, LANES * row : LANES * (row + 1)])
        height_ref[row : row + 1, :] = field_ref[6:7, LANES * row : LANES * (row + 1)]
    ghosts = (low_ref, high_ref, down_ref, up_ref)
    unit = low_ref.shape[0] // 3
    place = ghost_place(unit)
    for number in range(8):
        which, start = place[number]
        for block in range(unit // 8):
            write_doubled(
                tile_rows + number * (unit // 8) + block,
                ghosts[which][start + 8 * block : start + 8 * block + 8, :],
            )

    def one_chunk(chunk, carry):
        order = {0: 0, 1: 1, 2: 2, 6: 3}

        def emit(field, tile, value):
            if field == 6:
                value = 1.0 / value
            first = order[field] * region + tile * 8
            expanded_ref[first : first + 8, :] = value

        expand_targets(compact_ref, chunk, groups, (0, 1, 2, 6), emit)
        for tile in range(tile_count):
            sum_ref[8 * tile : 8 * tile + 8, :] = jnp.zeros((8, LANES), F32)

        def step(number, inner_carry):
            results = []
            for u in range(UNROLL):
                target = aligned(target_ref[number * UNROLL + u])
                source = source_ref[number * UNROLL + u]

                def at(field, target=target):
                    return expanded_ref[pl.ds(aligned(target + field * region), 8), :]

                def source_row(field, source=source):
                    return pool_ref[pl.ds(source + field, 1), :]

                square = None
                for axis in range(3):
                    gap = at(axis) - source_row(axis)
                    gap = gap - jnp.floor(gap + 0.5)
                    square = gap * gap if square is None else square + gap * gap
                safe = jnp.maximum(square, 1.2e-38)
                ratio = safe * lax.rsqrt(safe) * at(3)
                outer = jnp.maximum(2.0 - ratio, 0.0)
                inner = jnp.maximum(1.0 - ratio, 0.0)
                results.append((target, 0.25 * (outer * outer * outer) - inner * inner * inner))
            for target, value in results:
                sum_ref[pl.ds(target, 8), :] += value
            return inner_carry

        lax.fori_loop(0, (count_ref[0] + UNROLL - 1) // UNROLL, step, 0)
        reduce_targets(sum_ref, 0, tile_count, chunk, red_ref)
        return carry

    lax.fori_loop(0, chunks_ref[0], one_chunk, 0)

    for part in range(tile_rows // 8):
        rank = rank_ref[8 * part : 8 * part + 8, :]
        found = place_results(red_ref, tile_count // 16, part, rank)
        height = height_ref[8 * part : 8 * part + 8, :]
        flag = flag_ref[8 * part : 8 * part + 8, :]
        norm = PARTICLE_MASS / (math.pi * height * height * height)
        density_ref[8 * part : 8 * part + 8, :] = jnp.where(
            flag > 0, norm * (1.0 + found), jnp.abs(flag)
        )
    outs = (low_out, middle_out, high_out)
    blocks = unit // 8
    place = export_place(blocks)
    for block in range(blocks):
        index = export_ref[:, LANES * block : LANES * (block + 1)]
        high, low = index >> 7, index & 127
        found = jnp.zeros((8, LANES), F32)
        for row in range(tile_rows):
            found = jnp.where(high == row, lane_pick(spread(density_ref[row : row + 1, :]), low), found)
        for number in range(8):
            which, start = place[number]
            outs[which][start + block : start + block + 1, :] = found[number : number + 1, :]


def force_kernel(count_ref, chunks_ref, target_ref, source_ref, compact_ref, rank_ref, order_ref, field_ref, flag_ref, density_ref, pool_ref, low_ref, high_ref, down_ref, up_ref,
                 accel_ref, heat_ref,
                 first_ref, second_ref, expanded_ref, sum_ref, red_ref, energy_ref, press_ref, press_compact_ref):
    tile_rows = flag_ref.shape[0]
    tile_count = 2 * tile_rows
    groups = tile_rows // 16
    region = (tile_count + 1) * 8
    left = iota((8, LANES), 1) < 64
    sub = iota((8, LANES), 0)
    slope_norm = 0.5 * PARTICLE_MASS / math.pi

    def derived(height):
        inverse = 1.0 / height
        square = inverse * inverse
        return inverse, slope_norm * (square * square * inverse)

    def sources(row, density_row):
        wide = spread(density_row)
        other = pltpu.roll(wide, 64, 1)
        for half in range(2):
            doubled = jnp.where(left, wide, other) if half == 0 else jnp.where(left, other, wide)
            start = aligned(row * 16 + half * 8)
            value = pool_ref[pl.ds(start, 8), :]
            inverse, norm = derived(value)
            first_ref[pl.ds(start, 8), :] = jnp.where(
                sub == 7, (ADIABATIC - 1.0) * value / doubled, jnp.where(sub == 6, inverse, value)
            )
            second_ref[pl.ds(start, 8), :] = jnp.where(
                sub == 6, norm, -0.75 * pltpu.roll(value, 1, 0)
            )

    for row in range(tile_rows):
        sources(row, density_ref[row : row + 1, :])
        energy_ref[row : row + 1, :] = field_ref[7:8, LANES * row : LANES * (row + 1)]
    ghosts = (low_ref, high_ref, down_ref, up_ref)
    unit = low_ref.shape[0] // 3
    place = ghost_place(unit)
    for number in range(8):
        which, start = place[number]
        for block in range(unit):
            sources(tile_rows + number * unit + block, ghosts[which][start + block : start + block + 1, :])

    for part in range(tile_rows // 8):
        rows = slice(8 * part, 8 * part + 8)
        press = (ADIABATIC - 1.0) * energy_ref[rows, :] / density_ref[rows, :]
        press_ref[rows, :] = lane_pick(press, order_ref[rows, :])
    press_ref[tile_rows:, :] = jnp.zeros((LANES - tile_rows, LANES), F32)
    turned = jnp.transpose(press_ref[...])
    for half in range(2):
        for chunk in range(4):
            first = half * 64 + chunk * 16
            near, far = turned[first : first + 8], turned[first + 8 : first + 16]
            place_at = (chunk * 2 + half) * 8
            press_compact_ref[place_at : place_at + 8, :] = jnp.where(left, near, pltpu.roll(far, 64, 1))

    half_base = jnp.where(left, 0, 64)

    def one_chunk(chunk, carry):
        def emit(field, tile, value):
            first = field * region + tile * 8
            if field == 6:
                inverse, norm = derived(value)
                expanded_ref[first : first + 8, :] = inverse
                expanded_ref[2 * region + first : 2 * region + first + 8, :] = norm
                expanded_ref[3 * region + first : 3 * region + first + 8, :] = -0.75 * value
            else:
                expanded_ref[first : first + 8, :] = value

        expand_targets(compact_ref, chunk, groups, range(7), emit)
        for row in range(tile_rows):
            for half in range(2):
                start = aligned(chunk * 16 + half * 8)
                first = 7 * region + (2 * row + half) * 8
                expanded_ref[first : first + 8, :] = lane_pick(
                    press_compact_ref[pl.ds(start, 8), :], half_base + row
                )
        for quantity in range(4):
            for tile in range(tile_count):
                first = quantity * region + 8 * tile
                sum_ref[first : first + 8, :] = jnp.zeros((8, LANES), F32)

        def step(number, inner_carry):
            results = []
            for u in range(UNROLL):
                target = aligned(target_ref[number * UNROLL + u])
                source = source_ref[number * UNROLL + u]

                def at(field, target=target):
                    return expanded_ref[pl.ds(aligned(target + field * region), 8), :]

                def source_row(field, source=source):
                    return first_ref[pl.ds(source + field, 1), :]

                def source_more(field, source=source):
                    return second_ref[pl.ds(source + field, 1), :]

                gaps = []
                square = None
                approach = None
                for axis in range(3):
                    gap = at(axis) - source_row(axis)
                    gap = gap - jnp.floor(gap + 0.5)
                    gaps.append(gap)
                    square = gap * gap if square is None else square + gap * gap
                    part = (at(3 + axis) - source_row(3 + axis)) * gap
                    approach = part if approach is None else approach + part
                safe = jnp.maximum(square, 1.2e-38)
                inverse_distance = lax.rsqrt(safe)
                distance = safe * inverse_distance

                def slope(inverse_height, norm, scaled_height):
                    ratio = distance * inverse_height
                    outer = jnp.maximum(2.0 - ratio, 0.0)
                    far = (outer * outer) * (inverse_distance * scaled_height)
                    return norm * jnp.where(ratio < 1.0, 2.25 * ratio - 3.0, far)

                total = slope(at(6), at(8), at(9)) + slope(
                    source_row(6), source_more(6), source_more(7)
                )
                weight = (at(7) + source_row(7)) * total
                results.append((target, [weight * gap for gap in gaps] + [weight * approach]))
            for target, values in results:
                for quantity in range(4):
                    sum_ref[pl.ds(aligned(target + quantity * region), 8), :] += values[quantity]
            return inner_carry

        lax.fori_loop(0, (count_ref[0] + UNROLL - 1) // UNROLL, step, 0)
        for quantity in range(4):
            reduce_targets(sum_ref, quantity * region, tile_count, chunk + 4 * quantity, red_ref)
        return carry

    lax.fori_loop(0, chunks_ref[0], one_chunk, 0)
    blocks = tile_count // 16
    for part in range(tile_rows // 8):
        rank = rank_ref[8 * part : 8 * part + 8, :]
        flag = flag_ref[8 * part : 8 * part + 8, :]
        for quantity in range(4):
            found = place_results(red_ref.at[pl.ds(quantity * 8 * blocks, 8 * blocks)], blocks, part, rank)
            if quantity == 3:
                heat_ref[8 * part : 8 * part + 8, :] = jnp.where(flag > 0, 0.5 * found, 0.0)
            else:
                found = jnp.where(flag > 0, -found, 0.0)
                for row in range(8):
                    at = LANES * (8 * part + row)
                    accel_ref[quantity : quantity + 1, at : at + LANES] = found[row : row + 1, :]


def call(kernel, outs, scratch, operands, scalars=0, scalar_outs=()):
    smem = pl.BlockSpec(memory_space=pltpu.SMEM)
    vmem = pl.BlockSpec(memory_space=pltpu.VMEM)
    return pl.pallas_call(
        kernel,
        out_shape=[jax.ShapeDtypeStruct(shape, dtype) for shape, dtype in outs],
        in_specs=[smem if i < scalars else vmem for i in range(len(operands))],
        out_specs=[smem if i in scalar_outs else vmem for i in range(len(outs))],
        scratch_shapes=[pltpu.VMEM(shape, dtype) for shape, dtype in scratch],
        compiler_params=pltpu.CompilerParams(vmem_limit_bytes=40 * 2**20),
    )(*operands)


def on_device(
    particles, old_density, active, send_rows, send_count, export_rows, pair_tiles, pair_count
):
    row_count = particles.shape[1]
    levels, slots = send_rows.shape
    ghosts = export_rows.shape[1]
    pair_total = pair_tiles.shape[1]
    tile_rows = row_count // LANES
    tile_count = 2 * tile_rows
    in_blocks = slots // LANES
    out_rows = 10 * in_blocks
    unit = 8 * (ghosts // LANES)
    dense_unit = ghosts // LANES
    bits_x = lax.axis_size("gx").bit_length() - 1
    bits_y = lax.axis_size("gy").bit_length() - 1

    flag = jnp.where(active == 1, old_density, -old_density).reshape(tile_rows, LANES)
    used = jnp.arange(pair_total) < pair_count[0]
    targets = jnp.where(used, pair_tiles[0], tile_count) * 8
    sources = pair_tiles[1] * 8
    state_shapes = [((8, row_count), F32), ((tile_rows, LANES), F32)]
    index_scratch = ((in_blocks, LANES), I32)
    flag_scratch = ((in_blocks, LANES), F32)

    fields = particles
    (outgoing,) = call(
        first_kernel, [((out_rows, LANES), F32)], [index_scratch], [fields, flag, send_rows]
    )
    (inverse,) = call(
        inverse_kernel,
        [((levels * tile_rows, LANES), I32)],
        [],
        [send_count[:, 0], send_rows],
        scalars=1,
    )
    for level in range(4):
        if level < 2:
            incoming = from_partner(outgoing, "gx", bits_x - 1 - level)
        else:
            incoming = from_partner(outgoing, "gy", bits_y + 1 - level)
        if level < 3:
            fields, flag, outgoing = call(
                lambda *refs, level=level: level_kernel(level, *refs),
                state_shapes + [((out_rows, LANES), F32)],
                [index_scratch, flag_scratch],
                [fields, flag, inverse, incoming, send_rows],
            )
        else:
            fields, flag, low, middle, high = call(
                lambda *refs, level=level: last_kernel(level, *refs),
                state_shapes
                + [((3 * unit, LANES), F32), ((2 * unit, LANES), F32), ((3 * unit, LANES), F32)],
                [flag_scratch],
                [fields, flag, inverse, incoming, export_rows],
            )
    low, high, down, up = to_neighbours(low, middle, high, unit)
    compact, rank, order, chunks = call(
        target_kernel,
        [
            ((4 * tile_count * 4, LANES), F32),
            ((tile_rows, LANES), I32),
            ((tile_rows, LANES), I32),
            ((1,), I32),
        ],
        [((LANES, LANES), F32)],
        [fields, flag],
        scalar_outs=(3,),
    )
    region = (tile_count + 1) * 8
    density, low_d, middle_d, high_d, pool = call(
        density_kernel,
        [
            ((tile_rows, LANES), F32),
            ((3 * dense_unit, LANES), F32),
            ((2 * dense_unit, LANES), F32),
            ((3 * dense_unit, LANES), F32),
            ((2 * (tile_rows + 8 * dense_unit) * 8, LANES), F32),
        ],
        [
            ((4 * region, LANES), F32),
            ((region, LANES), F32),
            ((8 * (tile_count // 16), LANES), F32),
            ((tile_rows, LANES), F32),
        ],
        [
            pair_count, chunks, targets, sources,
            compact, rank, fields, flag, low, high, down, up, export_rows,
        ],
        scalars=4,
    )
    low_d, high_d, down_d, up_d = to_neighbours(low_d, middle_d, high_d, dense_unit)
    pool_shape = ((2 * (tile_rows + 8 * dense_unit) * 8, LANES), F32)
    accel, heat = call(
        force_kernel,
        [((3, row_count), F32), ((tile_rows, LANES), F32)],
        [
            pool_shape,
            pool_shape,
            ((10 * region, LANES), F32),
            ((4 * region, LANES), F32),
            ((32 * (tile_count // 16), LANES), F32),
            ((tile_rows, LANES), F32),
            ((LANES, LANES), F32),
            ((64, LANES), F32),
        ],
        [
            pair_count, chunks, targets, sources,
            compact, rank, order, fields, flag, density, pool, low_d, high_d, down_d, up_d,
        ],
        scalars=4,
    )
    return (density.reshape(row_count), accel, heat.reshape(row_count))


def solution(mesh):
    in_specs = (
        P(None, ("gx", "gy")),
        P(("gx", "gy")),
        P(("gx", "gy")),
        P(None, ("gx", "gy")),
        P(None, ("gx", "gy")),
        P(None, ("gx", "gy")),
        P(None, ("gx", "gy")),
        P(("gx", "gy")),
    )
    out_specs = (P(("gx", "gy")), P(None, ("gx", "gy")), P(("gx", "gy")))
    return jax.shard_map(
        on_device, mesh=mesh, in_specs=in_specs, out_specs=out_specs, check_vma=False
    )
```

```python
import math

import jax
import jax.numpy as jnp
from jax import lax
from jax.experimental import pallas as pl
from jax.experimental.pallas import tpu as pltpu
from jax.sharding import PartitionSpec as P

TILE = 64
LANES = 128
UNROLL = 8

PARTICLE_MASS = 1.0 / 512.0
ADIABATIC = 5.0 / 3.0
F32 = jnp.float32
I32 = jnp.int32


def from_behind(value, axis, steps):
    count = lax.axis_size(axis)
    pairs = [(source, (source + steps) % count) for source in range(count)]
    return lax.ppermute(value, axis, pairs)


def from_partner(block, axis, bit):
    count = lax.axis_size(axis)
    route = []
    for low in range(count):
        high = low | 1 << bit
        if high != low and high < count:
            route += [(low, high), (high, low)]
    return lax.ppermute(block, axis, route)


def along_x(low, high):
    return from_behind(low, "gx", -1), from_behind(high, "gx", 1)


def along_y(low, middle, high, unit):
    down = jnp.concatenate([low[:unit], middle[:unit], high[:unit]], axis=0)
    up = jnp.concatenate([low[2 * unit :], middle[unit:], high[2 * unit :]], axis=0)
    return from_behind(down, "gy", -1), from_behind(up, "gy", 1)


def ghost_place(unit):
    return ((2, 0), (0, unit), (3, 0), (2, unit), (3, unit), (2, 2 * unit), (1, unit), (3, 2 * unit))


def export_place(unit):
    return ((0, 0), (0, unit), (0, 2 * unit), (1, 0), (1, unit), (2, 0), (2, unit), (2, 2 * unit))


def lane_pick(table, index):
    return jnp.take_along_axis(table, index, axis=1, mode="promise_in_bounds")


def spread(row, rows=8):
    return jnp.broadcast_to(row, (rows, row.shape[1]))


def iota(shape, axis):
    return lax.broadcasted_iota(I32, shape, axis)


def aligned(value, size=8):
    return pl.multiple_of(value, size)


def pick_fields(tables, row, start):
    high, low = spread(row >> 7), spread(row & 127)
    found = start
    for block, table in enumerate(tables):
        found = jnp.where(high == block, lane_pick(table, low), found)
    return found


def pick_rows(table_refs, index, starts):
    high, low = index >> 7, index & 127
    found = list(starts)
    for block in range(table_refs[0].shape[0]):
        here = high == block
        for n, ref in enumerate(table_refs):
            found[n] = jnp.where(here, lane_pick(spread(ref[block : block + 1, :]), low), found[n])
    return found


def lane_blocks(ref):
    return [ref[:, LANES * b : LANES * (b + 1)] for b in range(ref.shape[1] // LANES)]


def row_blocks(ref, count):
    return [ref[8 * b : 8 * b + 8, :] for b in range(count)]


def stage_index(send_ref, level, index_ref):
    for j in range(index_ref.shape[0]):
        index_ref[j : j + 1, :] = send_ref[level : level + 1, LANES * j : LANES * (j + 1)]


def gather_outgoing(field_ref, flag_ref, index_ref, out_ref, inverse_ref=None, pick_ref=None):
    count = index_ref.shape[0]

    def body(step, carry):
        found = pick_fields(
            lane_blocks(field_ref), index_ref[pl.ds(step, 1), :], jnp.zeros((8, LANES), F32)
        )
        out_ref[pl.ds(aligned(step * 8), 8), :] = found
        return carry

    lax.fori_loop(0, count, body, 0, unroll=True)
    zero = jnp.zeros((8, LANES), F32)
    for part in range(count // 8):
        rows = slice(8 * part, 8 * part + 8)
        refs = [flag_ref] if inverse_ref is None else [flag_ref, inverse_ref]
        found = pick_rows(refs, index_ref[rows, :], [zero] * len(refs))
        first = 8 * count + 8 * part
        out_ref[first : first + 8, :] = jnp.abs(found[0])
        out_ref[first + count : first + count + 8, :] = jnp.where(found[0] > 0, 1.0, 0.0)
        if pick_ref is not None:
            pick_ref[rows, :] = found[1].astype(I32)


def apply_incoming(field_ref, flag_ref, inverse_ref, in_ref, new_field_ref, new_flag_ref, flag_in_ref):
    tile_rows = flag_ref.shape[0]
    count = flag_in_ref.shape[0]
    base = 8 * count
    density_in = in_ref[base : base + count, :]
    flag_in_ref[...] = jnp.where(in_ref[base + count : base + 2 * count, :] > 0.5, density_in, -density_in)

    def body(row, carry):
        where = pl.ds(aligned(row * LANES, LANES), LANES)
        slot = inverse_ref[pl.ds(row, 1), :].astype(I32) - 1
        new_field_ref[:, where] = pick_fields(row_blocks(in_ref, count), slot, field_ref[:, where])
        return carry

    lax.fori_loop(0, tile_rows, body, 0, unroll=16)
    for part in range(tile_rows // 8):
        rows = slice(8 * part, 8 * part + 8)
        slot = inverse_ref[rows, :].astype(I32) - 1
        new_flag_ref[rows, :] = pick_rows([flag_in_ref], slot, [flag_ref[rows, :]])[0]


def first_kernel(particle_ref, flag_ref, send_in_ref, field_ref, out_ref, send_ref, index_ref):
    stage_index(send_in_ref, 0, index_ref)
    gather_outgoing(particle_ref, flag_ref, index_ref, out_ref)
    field_ref[...] = particle_ref[...]
    send_ref[...] = send_in_ref[...]


def inverse_kernel(count_ref, send_ref, *inverse_refs):
    slots = send_ref.shape[1]
    slot = iota((1, slots), 1)
    for level, inverse_ref in enumerate(inverse_refs):
        tile_rows = inverse_ref.shape[0]
        rows = send_ref[level : level + 1, :]
        taken = slot < count_ref[level]
        high = jnp.where(taken, rows >> 7, -1)
        low = rows & 127
        number = slot + 1
        hit = spread(high, tile_rows) == iota((tile_rows, slots), 0)
        coarse = jnp.where(hit, spread((number >> 6).astype(F32), tile_rows), 0.0)
        fine = jnp.where(hit, spread((number & 63).astype(F32), tile_rows), 0.0)
        left = jnp.concatenate([coarse, fine], axis=0).astype(jnp.bfloat16)
        right = jnp.where(spread(low, LANES) == iota((LANES, slots), 0), 1.0, 0.0).astype(jnp.bfloat16)
        both = lax.dot_general(left, right, (((1,), (1,)), ((), ())), preferred_element_type=F32)
        inverse_ref[...] = both[:tile_rows] * 64.0 + both[tile_rows:]


def ahead_first_kernel(field_ref, flag_ref, inverse_ref, send_ref, partial_ref, pick_ref, index_ref):
    stage_index(send_ref, 1, index_ref)
    gather_outgoing(field_ref, flag_ref, index_ref, partial_ref, inverse_ref, pick_ref)


def ahead_kernel(level, field_ref, flag_ref, before_ref, in_ref, inverse_ref, send_ref, new_field_ref, new_flag_ref, partial_ref, pick_ref, index_ref, flag_in_ref):
    apply_incoming(field_ref, flag_ref, before_ref, in_ref, new_field_ref, new_flag_ref, flag_in_ref)
    stage_index(send_ref, level + 1, index_ref)
    gather_outgoing(new_field_ref, new_flag_ref, index_ref, partial_ref, inverse_ref, pick_ref)


def fix_kernel(partial_ref, pick_ref, in_ref, out_ref):
    count = pick_ref.shape[0]

    def body(step, carry):
        where = pl.ds(aligned(step * 8), 8)
        slot = pick_ref[pl.ds(step, 1), :] - 1
        out_ref[where, :] = pick_fields(row_blocks(in_ref, count), slot, partial_ref[where, :])
        return carry

    lax.fori_loop(0, count, body, 0, unroll=True)
    base = 8 * count
    for part in range(count // 8):
        slot = pick_ref[8 * part : 8 * part + 8, :] - 1
        tables = [in_ref.at[pl.ds(base, count)], in_ref.at[pl.ds(base + count, count)]]
        places = [slice(base + n * count + 8 * part, base + n * count + 8 * part + 8) for n in range(2)]
        found = pick_rows(tables, slot, [partial_ref[place, :] for place in places])
        for place, value in zip(places, found):
            out_ref[place, :] = value


def ahead_export_kernel(field_ref, flag_ref, before_ref, in_ref, inverse_ref, send_ref, last_ref, export_ref, new_field_ref, new_flag_ref, partial_ref, pick_ref, export_pick_ref, export_index_ref, index_ref, flag_in_ref):
    ahead_kernel(1, field_ref, flag_ref, before_ref, in_ref, inverse_ref, send_ref, new_field_ref, new_flag_ref, partial_ref, pick_ref, index_ref, flag_in_ref)
    zero = jnp.zeros((8, LANES), F32)
    blocks = export_ref.shape[1] // LANES
    for block in range(blocks):
        index = export_ref[:, LANES * block : LANES * (block + 1)]
        export_pick_ref[8 * block : 8 * block + 8, :] = pick_rows([last_ref], index, [zero])[0].astype(I32)
        for number in range(8):
            at = number * blocks + block
            export_index_ref[at : at + 1, :] = index[number : number + 1, :]


def ahead_last_kernel(field_ref, flag_ref, before_ref, in_ref, export_index_ref, new_field_ref, new_flag_ref, *rest):
    outs, flag_in_ref = rest[:3], rest[3]
    apply_incoming(field_ref, flag_ref, before_ref, in_ref, new_field_ref, new_flag_ref, flag_in_ref)
    blocks = export_index_ref.shape[0] // 8
    for target, (first, count) in enumerate(((0, 3), (3, 2), (5, 3))):

        def body(step, carry, target=target, first=first):
            row = export_index_ref[pl.ds(first * blocks + step, 1), :]
            outs[target][pl.ds(aligned(step * 8), 8), :] = pick_fields(
                lane_blocks(new_field_ref), row, jnp.zeros((8, LANES), F32)
            )
            return carry

        lax.fori_loop(0, count * blocks, body, 0, unroll=8)


def fix_last_kernel(low_ref, middle_ref, high_ref, pick_ref, in_ref, *outs):
    parts = (low_ref, middle_ref, high_ref)
    blocks = pick_ref.shape[0] // 8
    count = in_ref.shape[0] // 10
    for number, (target, start) in enumerate(export_place(8 * blocks)):
        for block in range(blocks):
            slot = pick_ref[8 * block + number : 8 * block + number + 1, :] - 1
            rows = slice(start + 8 * block, start + 8 * block + 8)
            outs[target][rows, :] = pick_fields(row_blocks(in_ref, count), slot, parts[target][rows, :])


EXPANDED = 9
SLOPE_NORM = 0.5 * PARTICLE_MASS / math.pi


def derived(height):
    inverse = 1.0 / height
    square = inverse * inverse
    return inverse, SLOPE_NORM * (square * square * inverse)


def expand_targets(compact_ref, chunk, base, expanded_ref):
    groups = compact_ref.shape[0] // (4 * 32)
    region = (groups * 32 + 1) * 8
    half_base = jnp.where(iota((8, LANES), 1) < 64, 0, 64)
    for inner in range(8):
        for field in range(7):
            index = half_base + (inner * 8 + field)
            for group in range(groups):
                for section in range(2):
                    for half in range(2):
                        place = ((group * 2 + section) * 2 + half) * 8
                        start = aligned(chunk * (groups * 32) + place)
                        tile = 2 * (group * 16 + section * 8 + inner) + half
                        value = lane_pick(compact_ref[pl.ds(start, 8), :], index)
                        first = base + field * region + tile * 8
                        if field == 6:
                            inverse, norm = derived(value)
                            expanded_ref[pl.ds(aligned(first), 8), :] = inverse
                            expanded_ref[pl.ds(aligned(first + region), 8), :] = norm
                            expanded_ref[pl.ds(aligned(first + 2 * region), 8), :] = -0.75 * value
                        else:
                            expanded_ref[pl.ds(aligned(first), 8), :] = value


def target_kernel(count_ref, field_ref, flag_ref, inverse_ref, in_ref, pair_ref,
                  new_field_ref, new_flag_ref, compact_ref, rank_ref, order_ref, list_ref, length_ref, expanded_ref,
                  flag_in_ref, stack_ref):
    apply_incoming(field_ref, flag_ref, inverse_ref, in_ref, new_field_ref, new_flag_ref, flag_in_ref)
    tile_rows = flag_ref.shape[0]
    groups = tile_rows // 16
    tile_count = 2 * tile_rows
    region = (tile_count + 1) * 8
    active = new_flag_ref[...] > 0
    ones = jnp.where(active, 1.0, 0.0).astype(jnp.bfloat16)
    a = iota((LANES, LANES), 0)
    b = iota((LANES, LANES), 1)
    same = (a >> 6) == (b >> 6)
    before = jnp.where(same & (a < b), 1.0, 0.0).astype(jnp.bfloat16)
    whole = jnp.where(same, 1.0, 0.0).astype(jnp.bfloat16)
    rank = jnp.dot(ones, before, preferred_element_type=F32).astype(I32)
    total = jnp.dot(ones, whole, preferred_element_type=F32)
    rank_ref[...] = rank
    lane = iota((tile_rows, LANES), 1)
    code = jnp.where(active, lane + 128 * ((lane & 63) - rank), -1)
    for bit in range(6):
        moved = pltpu.roll(code, LANES - (1 << bit), 1)
        take = (moved >= 0) & (((moved >> (7 + bit)) & 1) == 1)
        keep = (code >= 0) & (((code >> (7 + bit)) & 1) == 0)
        code = jnp.where(take, moved, jnp.where(keep, code, -1))
    order_ref[...] = jnp.where(code >= 0, code & 127, lane)
    left_half = iota((8, LANES), 1) < 64
    for group in range(groups):
        for inner in range(16):
            row = group * 16 + inner
            stack_ref[8 * inner : 8 * inner + 8, :] = lane_pick(
                new_field_ref[:, LANES * row : LANES * (row + 1)], spread(order_ref[row : row + 1, :])
            )
        turned = jnp.transpose(stack_ref[...])
        for half in range(2):
            for chunk in range(4):
                first = half * 64 + chunk * 16
                near, far = turned[first : first + 8], turned[first + 8 : first + 16]
                for section in range(2):
                    if section == 0:
                        mixed = jnp.where(left_half, near, pltpu.roll(far, 64, 1))
                    else:
                        mixed = jnp.where(left_half, pltpu.roll(near, 64, 1), far)
                    place = (((chunk * groups + group) * 2 + section) * 2 + half) * 8
                    compact_ref[place : place + 8, :] = mixed

    pairs = pair_ref.shape[1]
    slots = list_ref.shape[1]
    target, source = pair_ref[0:1, :], pair_ref[1:2, :]
    folded = jnp.where((lane & 63) == iota((tile_rows, LANES), 0), total, 0.0)
    totals = spread(jnp.sum(folded, axis=0, keepdims=True))
    place = spread((target & 1) * 64 + (target >> 1))
    need = jnp.concatenate(
        [lane_pick(totals, place[:, LANES * q : LANES * (q + 1)]) for q in range(pairs // LANES)], axis=1
    )
    sub = iota((8, pairs), 0)
    is_ghost = spread(source) >= tile_count
    member = (
        (iota((8, pairs), 1) < count_ref[0])
        & (need > (16 * (sub & 3)).astype(F32))
        & (is_ghost == (sub >= 4))
    )
    member_value = jnp.where(member, 1.0, 0.0)
    earlier = jnp.where(iota((pairs, pairs), 0) < iota((pairs, pairs), 1), 1.0, 0.0).astype(jnp.bfloat16)
    position = jnp.dot(member_value.astype(jnp.bfloat16), earlier, preferred_element_type=F32).astype(I32)
    length = jnp.broadcast_to(jnp.sum(member_value, axis=1, keepdims=True), (8, LANES)).astype(I32)
    length_ref[...] = length
    own_steps = ((length + (UNROLL - 1)) // UNROLL) * UNROLL
    base = jnp.where(iota((8, LANES), 0) >= 4, pltpu.roll(own_steps, 4, 0), 0)
    position = position + jnp.concatenate([base] * (pairs // LANES), axis=1)
    position = jnp.where(member, position, -1)
    local = jnp.where(source >= tile_count, source - tile_count, source)
    values = jnp.where(
        sub == 0, spread(target + 1), jnp.where(sub == 1, spread(local + 1), 0)
    ).astype(F32).astype(jnp.bfloat16)

    def make_list(chunk):
        row = jnp.maximum(position[chunk : chunk + 1, :], position[chunk + 4 : chunk + 5, :])
        hit = jnp.where(spread(row, slots) == iota((slots, pairs), 0), 1.0, 0.0).astype(jnp.bfloat16)
        found = lax.dot_general(
            values, hit, (((1,), (1,)), ((), ())), preferred_element_type=F32
        ).astype(I32)
        list_ref[chunk : chunk + 1, :] = jnp.where(found[0:1] > 0, found[0:1] - 1, tile_count) * 8
        list_ref[4 + chunk : 5 + chunk, :] = jnp.maximum(found[1:2] - 1, 0) * 8

    make_list(0)
    make_list(1)

    @pl.when(jnp.max(total) > 32.0)
    def _():
        make_list(2)
        make_list(3)

    def one_chunk(chunk, carry):
        expand_targets(compact_ref, chunk, aligned(chunk * (EXPANDED * region)), expanded_ref)
        return carry

    lax.fori_loop(0, 2, one_chunk, 0)


def reduce_targets(sum_ref, first, tile_count, section, out_ref):
    lane = iota((8, LANES), 1)
    sub = iota((8, LANES), 0)
    left = lane < 64
    blocks = tile_count // 16
    for block in range(blocks):
        near = jnp.zeros((8, LANES), F32)
        far = jnp.zeros((8, LANES), F32)
        for inner in range(16):
            place = first + (block * 16 + inner) * 8
            value = sum_ref[place : place + 8, :]
            here = lane == sub + inner * 8
            near_sum = jnp.sum(jnp.where(left, value, 0.0), axis=1, keepdims=True)
            far_sum = jnp.sum(jnp.where(left, 0.0, value), axis=1, keepdims=True)
            near = jnp.where(here, near_sum, near)
            far = jnp.where(here, far_sum, far)
        out_ref[pl.ds((section * 2) * blocks + block, 1), :] = jnp.sum(near, axis=0, keepdims=True)
        out_ref[pl.ds((section * 2 + 1) * blocks + block, 1), :] = jnp.sum(far, axis=0, keepdims=True)


def place_results(red_ref, blocks, part, rank):
    row = iota((8, LANES), 0)
    half = iota((8, LANES), 1) >> 6
    index = (2 * row + half) * 8 + (rank & 7)
    which = rank >> 3
    found = jnp.zeros((8, LANES), F32)
    for section in range(8):
        table = spread(red_ref[section * blocks + part : section * blocks + part + 1, :])
        found = jnp.where(which == section, lane_pick(table, index), found)
    return found


def clear(sum_ref, first, rows):
    for at in range(0, rows, 8):
        sum_ref[first + at : first + at + 8, :] = jnp.zeros((8, LANES), F32)


def steps_of(length):
    return (length + (UNROLL - 1)) // UNROLL


def span(length_ref, chunk, ghost):
    own = steps_of(length_ref[chunk, 0])
    if not ghost:
        return 0, own
    return own, own + steps_of(length_ref[chunk + 4, 0])


def double_into(pool_ref, row, value):
    left = iota((8, LANES), 1) < 64
    other = pltpu.roll(value, 64, 1)
    pool_ref[16 * row : 16 * row + 8, :] = jnp.where(left, value, other)
    pool_ref[16 * row + 8 : 16 * row + 16, :] = jnp.where(left, other, value)


def density_pairs(list_ref, length_ref, chunk, ghost, expanded_ref, base, region, pool_ref, sum_ref, sum_base):
    def step(number, carry):
        results = []
        for u in range(UNROLL):
            target = list_ref[chunk, number * UNROLL + u]
            source = list_ref[chunk + 4, number * UNROLL + u]

            def at(field, target=target):
                return expanded_ref[pl.ds(aligned(target + (base + field * region)), 8), :]

            square = None
            for axis in range(3):
                gap = at(axis) - pool_ref[pl.ds(source + axis, 1), :]
                gap = gap - jnp.floor(gap + 0.5)
                square = gap * gap if square is None else square + gap * gap
            safe = jnp.maximum(square, 1.2e-38)
            ratio = safe * lax.rsqrt(safe) * at(6)
            outer = jnp.maximum(2.0 - ratio, 0.0)
            inner = jnp.maximum(1.0 - ratio, 0.0)
            results.append((target, 0.25 * (outer * outer * outer) - inner * inner * inner))
        for target, value in results:
            sum_ref[pl.ds(aligned(target + sum_base), 8), :] += value
        return carry

    first, last = span(length_ref, chunk, ghost)
    lax.fori_loop(first, last, step, 0)


def density_own_kernel(list_ref, length_ref, field_ref, expanded_ref, pool_ref, sum_ref):
    tile_rows = field_ref.shape[1] // LANES
    region = (2 * tile_rows + 1) * 8
    for row in range(tile_rows):
        double_into(pool_ref, row, field_ref[:, LANES * row : LANES * (row + 1)])
    clear(sum_ref, 0, 2 * region)
    for chunk in range(2):
        density_pairs(
            list_ref, length_ref, chunk, False, expanded_ref, chunk * EXPANDED * region, region,
            pool_ref, sum_ref, chunk * region,
        )


def density_kernel(list_ref, length_ref, compact_ref, expanded_ref, own_pool_ref, own_sum_ref, rank_ref, field_ref, flag_ref, low_ref, high_ref, down_ref, up_ref, export_ref,
                   density_ref, low_out, middle_out, high_out, pool_ref,
                   sum_ref, red_ref, height_ref, spare_ref):
    tile_rows = flag_ref.shape[0]
    tile_count = 2 * tile_rows
    region = (tile_count + 1) * 8
    ghosts = (low_ref, high_ref, down_ref, up_ref)
    unit = low_ref.shape[0] // 3
    blocks = unit // 8
    for number, (which, start) in enumerate(ghost_place(unit)):
        for block in range(blocks):
            first = start + 8 * block
            double_into(pool_ref, number * blocks + block, ghosts[which][first : first + 8, :])
    sum_ref[...] = own_sum_ref[...]
    for chunk in range(2):
        density_pairs(
            list_ref, length_ref, chunk, True, expanded_ref, chunk * EXPANDED * region, region,
            pool_ref, sum_ref, chunk * region,
        )
        reduce_targets(sum_ref, chunk * region, tile_count, chunk, red_ref)
    for row in range(4 * (tile_count // 16), 8 * (tile_count // 16), 8):
        red_ref[row : row + 8, :] = jnp.zeros((8, LANES), F32)

    def rare_chunk(chunk, carry):
        @pl.when(length_ref[chunk, 0] + length_ref[chunk + 4, 0] > 0)
        def _():
            expand_targets(compact_ref, chunk, 0, spare_ref)
            clear(sum_ref, 0, region)
            density_pairs(list_ref, length_ref, chunk, False, spare_ref, 0, region, own_pool_ref, sum_ref, 0)
            density_pairs(list_ref, length_ref, chunk, True, spare_ref, 0, region, pool_ref, sum_ref, 0)
            reduce_targets(sum_ref, 0, tile_count, chunk, red_ref)

        return carry

    lax.fori_loop(2, 4, rare_chunk, 0)
    for row in range(tile_rows):
        height_ref[row : row + 1, :] = field_ref[6:7, LANES * row : LANES * (row + 1)]
    for part in range(tile_rows // 8):
        rows = slice(8 * part, 8 * part + 8)
        found = place_results(red_ref, tile_count // 16, part, rank_ref[rows, :])
        height = height_ref[rows, :]
        flag = flag_ref[rows, :]
        norm = PARTICLE_MASS / (math.pi * height * height * height)
        density_ref[rows, :] = jnp.where(flag > 0, norm * (1.0 + found), jnp.abs(flag))
    outs = (low_out, middle_out, high_out)
    zero = jnp.zeros((8, LANES), F32)
    for block in range(blocks):
        index = export_ref[:, LANES * block : LANES * (block + 1)]
        found = pick_rows([density_ref], index, [zero])[0]
        for number, (which, start) in enumerate(export_place(blocks)):
            outs[which][start + block : start + block + 1, :] = found[number : number + 1, :]


def source_tables(pool_ref, tile, first_ref, second_ref, density=None):
    sub = iota((8, LANES), 0)
    rows = slice(8 * tile, 8 * tile + 8)
    value = pool_ref[rows, :]
    inverse, norm = derived(value)
    press = (ADIABATIC - 1.0) * value
    if density is not None:
        press = press / density
    first_ref[rows, :] = jnp.where(sub == 7, press, jnp.where(sub == 6, inverse, value))
    second_ref[rows, :] = jnp.where(sub == 6, norm, -0.75 * pltpu.roll(value, 1, 0))


def doubled_halves(row):
    left = iota((8, LANES), 1) < 64
    wide = spread(row)
    other = pltpu.roll(wide, 64, 1)
    return jnp.where(left, wide, other), jnp.where(left, other, wide)


def force_pairs(list_ref, length_ref, chunk, ghost, expanded_ref, base, region, press_ref, press_base, first_ref, second_ref, sum_ref):
    def step(number, carry):
        results = []
        for u in range(UNROLL):
            target = list_ref[chunk, number * UNROLL + u]
            source = list_ref[chunk + 4, number * UNROLL + u]

            def at(field, target=target):
                return expanded_ref[pl.ds(aligned(target + (base + field * region)), 8), :]

            def source_row(field, source=source):
                return first_ref[pl.ds(source + field, 1), :]

            def source_more(field, source=source):
                return second_ref[pl.ds(source + field, 1), :]

            gaps = []
            square = None
            approach = None
            for axis in range(3):
                gap = at(axis) - source_row(axis)
                gap = gap - jnp.floor(gap + 0.5)
                gaps.append(gap)
                square = gap * gap if square is None else square + gap * gap
                part = (at(3 + axis) - source_row(3 + axis)) * gap
                approach = part if approach is None else approach + part
            safe = jnp.maximum(square, 1.2e-38)
            inverse_distance = lax.rsqrt(safe)
            distance = safe * inverse_distance

            def slope(inverse_height, norm, scaled_height):
                ratio = distance * inverse_height
                outer = jnp.maximum(2.0 - ratio, 0.0)
                far = (outer * outer) * (inverse_distance * scaled_height)
                return norm * jnp.where(ratio < 1.0, 2.25 * ratio - 3.0, far)

            total = slope(at(6), at(7), at(8)) + slope(source_row(6), source_more(6), source_more(7))
            press = press_ref[pl.ds(aligned(target + press_base), 8), :] + source_row(7)
            weight = press * total
            results.append((target, [weight * gap for gap in gaps] + [weight * approach]))
        for target, values in results:
            for quantity in range(4):
                sum_ref[pl.ds(aligned(target + quantity * region), 8), :] += values[quantity]
        return carry

    first, last = span(length_ref, chunk, ghost)
    lax.fori_loop(first, last, step, 0)


def expand_press(press_compact_ref, chunk, tile_rows, press_ref, base):
    half_base = jnp.where(iota((8, LANES), 1) < 64, 0, 64)
    for row in range(tile_rows):
        for half in range(2):
            start = aligned(chunk * 16 + half * 8)
            first = base + (2 * row + half) * 8
            press_ref[first : first + 8, :] = lane_pick(
                press_compact_ref[pl.ds(start, 8), :], half_base + row
            )


def force_own_kernel(list_ref, length_ref, density_ref, field_ref, order_ref, expanded_ref, pool_ref,
                     first_ref, second_ref, press_compact_ref, press_ref, sum_ref,
                     energy_ref, ordered_ref):
    tile_rows = density_ref.shape[0]
    tile_count = 2 * tile_rows
    region = (tile_count + 1) * 8
    left = iota((8, LANES), 1) < 64
    for row in range(tile_rows):
        near, far = doubled_halves(density_ref[row : row + 1, :])
        source_tables(pool_ref, 2 * row, first_ref, second_ref, near)
        source_tables(pool_ref, 2 * row + 1, first_ref, second_ref, far)
        energy_ref[row : row + 1, :] = field_ref[7:8, LANES * row : LANES * (row + 1)]
    for part in range(tile_rows // 8):
        rows = slice(8 * part, 8 * part + 8)
        press = (ADIABATIC - 1.0) * energy_ref[rows, :] / density_ref[rows, :]
        ordered_ref[rows, :] = lane_pick(press, order_ref[rows, :])
    ordered_ref[tile_rows:, :] = jnp.zeros((LANES - tile_rows, LANES), F32)
    turned = jnp.transpose(ordered_ref[...])
    for half in range(2):
        for chunk in range(4):
            first = half * 64 + chunk * 16
            near, far = turned[first : first + 8], turned[first + 8 : first + 16]
            place_at = (chunk * 2 + half) * 8
            press_compact_ref[place_at : place_at + 8, :] = jnp.where(left, near, pltpu.roll(far, 64, 1))
    for chunk in range(2):
        expand_press(press_compact_ref, chunk, tile_rows, press_ref, chunk * region)
    clear(sum_ref, 0, 4 * region)
    force_pairs(
        list_ref, length_ref, 0, False, expanded_ref, 0, region, press_ref, 0, first_ref, second_ref, sum_ref
    )


def force_own_more_kernel(list_ref, length_ref, expanded_ref, press_ref, own_first_ref, own_second_ref, pool_ref,
                          sum_ref, first_ref, second_ref):
    region = sum_ref.shape[0] // 4
    for tile in range(pool_ref.shape[0] // 8):
        source_tables(pool_ref, tile, first_ref, second_ref)
    clear(sum_ref, 0, 4 * region)
    force_pairs(
        list_ref, length_ref, 1, False, expanded_ref, EXPANDED * region, region, press_ref, region,
        own_first_ref, own_second_ref, sum_ref,
    )


def force_kernel(list_ref, length_ref, compact_ref, expanded_ref, press_compact_ref, press_ref, rank_ref, flag_ref, own_first_ref, own_second_ref, half_ref, second_ref, zero_sum_ref, one_sum_ref, low_ref, high_ref, down_ref, up_ref,
                 accel_ref, heat_ref,
                 first_ref, sum_ref, red_ref, spare_ref, spare_press_ref):
    tile_rows = flag_ref.shape[0]
    tile_count = 2 * tile_rows
    region = (tile_count + 1) * 8
    blocks = tile_count // 16
    is_press = iota((8, LANES), 0) == 7
    ghosts = (low_ref, high_ref, down_ref, up_ref)
    unit = low_ref.shape[0] // 3
    for number, (which, start) in enumerate(ghost_place(unit)):
        for block in range(unit):
            row = number * unit + block
            for half, density in enumerate(doubled_halves(ghosts[which][start + block : start + block + 1, :])):
                rows = slice(16 * row + 8 * half, 16 * row + 8 * half + 8)
                value = half_ref[rows, :]
                first_ref[rows, :] = jnp.where(is_press, value / density, value)
    for chunk in range(2):
        sum_ref[...] = (zero_sum_ref if chunk == 0 else one_sum_ref)[...]
        force_pairs(
            list_ref, length_ref, chunk, True, expanded_ref, chunk * EXPANDED * region, region,
            press_ref, chunk * region, first_ref, second_ref, sum_ref,
        )
        for quantity in range(4):
            reduce_targets(sum_ref, quantity * region, tile_count, chunk + 4 * quantity, red_ref)
    for quantity in range(4):
        for row in range(4 * blocks, 8 * blocks, 8):
            at = quantity * 8 * blocks + row
            red_ref[at : at + 8, :] = jnp.zeros((8, LANES), F32)

    def rare_chunk(chunk, carry):
        @pl.when(length_ref[chunk, 0] + length_ref[chunk + 4, 0] > 0)
        def _():
            expand_targets(compact_ref, chunk, 0, spare_ref)
            expand_press(press_compact_ref, chunk, tile_rows, spare_press_ref, 0)
            clear(sum_ref, 0, 4 * region)
            force_pairs(
                list_ref, length_ref, chunk, False, spare_ref, 0, region, spare_press_ref, 0,
                own_first_ref, own_second_ref, sum_ref,
            )
            force_pairs(
                list_ref, length_ref, chunk, True, spare_ref, 0, region, spare_press_ref, 0,
                first_ref, second_ref, sum_ref,
            )
            for quantity in range(4):
                reduce_targets(sum_ref, quantity * region, tile_count, chunk + 4 * quantity, red_ref)

        return carry

    lax.fori_loop(2, 4, rare_chunk, 0)
    for part in range(tile_rows // 8):
        rank = rank_ref[8 * part : 8 * part + 8, :]
        flag = flag_ref[8 * part : 8 * part + 8, :]
        for quantity in range(4):
            found = place_results(red_ref.at[pl.ds(quantity * 8 * blocks, 8 * blocks)], blocks, part, rank)
            if quantity == 3:
                heat_ref[8 * part : 8 * part + 8, :] = jnp.where(flag > 0, 0.5 * found, 0.0)
            else:
                found = jnp.where(flag > 0, -found, 0.0)
                for row in range(8):
                    at = LANES * (8 * part + row)
                    accel_ref[quantity : quantity + 1, at : at + LANES] = found[row : row + 1, :]


def call(kernel, outs, scratch, operands, scalars=0):
    smem = pl.BlockSpec(memory_space=pltpu.SMEM)
    vmem = pl.BlockSpec(memory_space=pltpu.VMEM)
    return pl.pallas_call(
        kernel,
        out_shape=[jax.ShapeDtypeStruct(shape, dtype) for shape, dtype in outs],
        in_specs=[smem if i < scalars else vmem for i in range(len(operands))],
        out_specs=[vmem] * len(outs),
        scratch_shapes=[pltpu.VMEM(shape, dtype) for shape, dtype in scratch],
        compiler_params=pltpu.CompilerParams(vmem_limit_bytes=24 * 2**20),
    )(*operands)


def on_device(
    particles, old_density, active, send_rows, send_count, export_rows, pair_tiles, pair_count
):
    row_count = particles.shape[1]
    levels, slots = send_rows.shape
    ghosts = export_rows.shape[1]
    pair_total = pair_tiles.shape[1]
    tile_rows = row_count // LANES
    tile_count = 2 * tile_rows
    in_blocks = slots // LANES
    unit = 8 * (ghosts // LANES)
    dense_unit = ghosts // LANES
    region = (tile_count + 1) * 8
    list_slots = -(-(pair_total + 2 * UNROLL) // LANES) * LANES
    bits_x = lax.axis_size("gx").bit_length() - 1
    bits_y = lax.axis_size("gy").bit_length() - 1

    row = ((tile_rows, LANES), F32)
    whole = ((8, row_count), F32)
    offered = ((10 * in_blocks, LANES), F32)
    picked = ((in_blocks, LANES), I32)
    index_scratch = ((in_blocks, LANES), I32)
    flag_scratch = ((in_blocks, LANES), F32)
    exported = [((3 * unit, LANES), F32), ((2 * unit, LANES), F32), ((3 * unit, LANES), F32)]

    def swap(block, level):
        if level < 2:
            return from_partner(block, "gx", bits_x - 1 - level)
        return from_partner(block, "gy", bits_y + 1 - level)

    flag = jnp.where(active == 1, old_density, -old_density).reshape(tile_rows, LANES)
    fields, outgoing, send_rows = call(
        first_kernel,
        [whole, offered, (send_rows.shape, I32)],
        [index_scratch],
        [particles, flag, send_rows],
    )
    incoming = swap(outgoing, 0)
    inverse = call(inverse_kernel, [row] * levels, [], [send_count[:, 0], send_rows], scalars=1)
    partial, pick = call(
        ahead_first_kernel, [offered, picked], [index_scratch], [fields, flag, inverse[0], send_rows]
    )
    (outgoing,) = call(fix_kernel, [offered], [], [partial, pick, incoming])
    before = incoming
    incoming = swap(outgoing, 1)
    fields, flag, partial, pick, export_pick, export_index = call(
        ahead_export_kernel,
        [whole, row, offered, picked, ((8 * dense_unit, LANES), I32), ((8 * dense_unit, LANES), I32)],
        [index_scratch, flag_scratch],
        [fields, flag, inverse[0], before, inverse[1], send_rows, inverse[3], export_rows],
    )
    (outgoing,) = call(fix_kernel, [offered], [], [partial, pick, incoming])
    before = incoming
    incoming = swap(outgoing, 2)
    fields, flag, partial, pick = call(
        lambda *refs: ahead_kernel(2, *refs),
        [whole, row, offered, picked],
        [index_scratch, flag_scratch],
        [fields, flag, inverse[1], before, inverse[2], send_rows],
    )
    (outgoing,) = call(fix_kernel, [offered], [], [partial, pick, incoming])
    before = incoming
    incoming = swap(outgoing, 3)
    fields, flag, low, middle, high = call(
        ahead_last_kernel,
        [whole, row] + exported,
        [flag_scratch],
        [fields, flag, inverse[2], before, export_index],
    )
    low, middle, high = call(
        fix_last_kernel, exported, [], [low, middle, high, export_pick, incoming]
    )
    low, high = along_x(low, high)
    fields, flag, compact, rank, order, lists, lengths, expanded = call(
        target_kernel,
        [
            whole,
            row,
            ((8 * tile_rows, LANES), F32),
            ((tile_rows, LANES), I32),
            ((tile_rows, LANES), I32),
            ((8, list_slots), I32),
            ((8, LANES), I32),
            ((2 * EXPANDED * region, LANES), F32),
        ],
        [flag_scratch, ((LANES, LANES), F32)],
        [pair_count, fields, flag, inverse[3], incoming, pair_tiles],
        scalars=1,
    )
    low, high, lengths = lax.optimization_barrier((low, high, lengths))
    down, up = along_y(low, middle, high, unit)
    pool_shape = ((tile_count * 8, LANES), F32)
    ghost_pool_shape = ((2 * 8 * dense_unit * 8, LANES), F32)
    own_pool, own_sum = call(
        density_own_kernel,
        [pool_shape, ((2 * region, LANES), F32)],
        [],
        [lists, lengths, fields, expanded],
        scalars=2,
    )
    density, low_d, middle_d, high_d, ghost_pool = call(
        density_kernel,
        [
            row,
            ((3 * dense_unit, LANES), F32),
            ((2 * dense_unit, LANES), F32),
            ((3 * dense_unit, LANES), F32),
            ghost_pool_shape,
        ],
        [
            ((2 * region, LANES), F32),
            ((8 * (tile_count // 16), LANES), F32),
            row,
            ((EXPANDED * region, LANES), F32),
        ],
        [
            lists, lengths, compact, expanded, own_pool, own_sum,
            rank, fields, flag, low, high, down, up, export_rows,
        ],
        scalars=2,
    )
    low_d, high_d = along_x(low_d, high_d)
    sums = ((4 * region, LANES), F32)
    own_first, own_second, press_compact, press, zero_sum = call(
        force_own_kernel,
        [pool_shape, pool_shape, ((64, LANES), F32), ((2 * region, LANES), F32), sums],
        [row, ((LANES, LANES), F32)],
        [lists, lengths, density, fields, order, expanded, own_pool],
        scalars=2,
    )
    low_d, high_d, press = lax.optimization_barrier((low_d, high_d, press))
    down_d, up_d = along_y(low_d, middle_d, high_d, dense_unit)
    one_sum, ghost_first, ghost_second = call(
        force_own_more_kernel,
        [sums, ghost_pool_shape, ghost_pool_shape],
        [],
        [lists, lengths, expanded, press, own_first, own_second, ghost_pool],
        scalars=2,
    )
    accel, heat = call(
        force_kernel,
        [((3, row_count), F32), row],
        [
            ghost_pool_shape,
            sums,
            ((32 * (tile_count // 16), LANES), F32),
            ((EXPANDED * region, LANES), F32),
            ((region, LANES), F32),
        ],
        [
            lists, lengths, compact, expanded, press_compact, press, rank, flag,
            own_first, own_second, ghost_first, ghost_second, zero_sum, one_sum,
            low_d, high_d, down_d, up_d,
        ],
        scalars=2,
    )
    return (density.reshape(row_count), accel, heat.reshape(row_count))


def solution(mesh):
    in_specs = (
        P(None, ("gx", "gy")),
        P(("gx", "gy")),
        P(("gx", "gy")),
        P(None, ("gx", "gy")),
        P(None, ("gx", "gy")),
        P(None, ("gx", "gy")),
        P(None, ("gx", "gy")),
        P(("gx", "gy")),
    )
    out_specs = (P(("gx", "gy")), P(None, ("gx", "gy")), P(("gx", "gy")))
    return jax.shard_map(
        on_device, mesh=mesh, in_specs=in_specs, out_specs=out_specs, check_vma=False
    )
```

```python
import math

import jax
import jax.numpy as jnp
from jax import lax
from jax.experimental import pallas as pl
from jax.experimental.pallas import tpu as pltpu
from jax.sharding import PartitionSpec as P

TILE = 64
LANES = 128
UNROLL = 8

PARTICLE_MASS = 1.0 / 512.0
ADIABATIC = 5.0 / 3.0
F32 = jnp.float32
I32 = jnp.int32


def from_behind(value, axis, steps):
    count = lax.axis_size(axis)
    pairs = [(source, (source + steps) % count) for source in range(count)]
    return lax.ppermute(value, axis, pairs)


def from_partner(block, axis, bit):
    count = lax.axis_size(axis)
    route = []
    for low in range(count):
        high = low | 1 << bit
        if high != low and high < count:
            route += [(low, high), (high, low)]
    return lax.ppermute(block, axis, route)


def along_x(low, high):
    count = lax.axis_size("gx")
    if count % 2:
        return from_behind(low, "gx", -1), from_behind(high, "gx", 1)
    even = lax.axis_index("gx") % 2 == 0
    first = [(i, i ^ 1) for i in range(count)]
    second = [(i, (i + 1) % count if i % 2 else (i - 1) % count) for i in range(count)]
    after = lax.ppermute(jnp.where(even, high, low), "gx", first)
    before = lax.ppermute(jnp.where(even, low, high), "gx", second)
    return jnp.where(even, after, before), jnp.where(even, before, after)


def along_y(low, middle, high, unit):
    down = jnp.concatenate([low[:unit], middle[:unit], high[:unit]], axis=0)
    up = jnp.concatenate([low[2 * unit :], middle[unit:], high[2 * unit :]], axis=0)
    return from_behind(down, "gy", -1), from_behind(up, "gy", 1)


def ghost_place(unit):
    return ((2, 0), (0, unit), (3, 0), (2, unit), (3, unit), (2, 2 * unit), (1, unit), (3, 2 * unit))


def export_place(unit):
    return ((0, 0), (0, unit), (0, 2 * unit), (1, 0), (1, unit), (2, 0), (2, unit), (2, 2 * unit))


def lane_pick(table, index):
    return jnp.take_along_axis(table, index, axis=1, mode="promise_in_bounds")


def spread(row, rows=8):
    return jnp.broadcast_to(row, (rows, row.shape[1]))


def iota(shape, axis):
    return lax.broadcasted_iota(I32, shape, axis)


def aligned(value, size=8):
    return pl.multiple_of(value, size)


def pick_fields(tables, row, start):
    high, low = spread(row >> 7), spread(row & 127)
    found = start
    for block, table in enumerate(tables):
        found = jnp.where(high == block, lane_pick(table, low), found)
    return found


def pick_rows(table_refs, index, starts):
    high, low = index >> 7, index & 127
    found = list(starts)
    for block in range(table_refs[0].shape[0]):
        here = high == block
        for n, ref in enumerate(table_refs):
            found[n] = jnp.where(here, lane_pick(spread(ref[block : block + 1, :]), low), found[n])
    return found


def lane_blocks(ref):
    return [ref[:, LANES * b : LANES * (b + 1)] for b in range(ref.shape[1] // LANES)]


def row_blocks(ref, count):
    return [ref[8 * b : 8 * b + 8, :] for b in range(count)]


def stage_index(send_ref, level, index_ref):
    for j in range(index_ref.shape[0]):
        index_ref[j : j + 1, :] = send_ref[level : level + 1, LANES * j : LANES * (j + 1)]


def gather_outgoing(field_ref, flag_ref, index_ref, out_ref, inverse_ref=None, pick_ref=None):
    count = index_ref.shape[0]

    def body(step, carry):
        found = pick_fields(
            lane_blocks(field_ref), index_ref[pl.ds(step, 1), :], jnp.zeros((8, LANES), F32)
        )
        out_ref[pl.ds(aligned(step * 8), 8), :] = found
        return carry

    lax.fori_loop(0, count, body, 0, unroll=True)
    zero = jnp.zeros((8, LANES), F32)
    for part in range(count // 8):
        rows = slice(8 * part, 8 * part + 8)
        refs = [flag_ref] if inverse_ref is None else [flag_ref, inverse_ref]
        found = pick_rows(refs, index_ref[rows, :], [zero] * len(refs))
        first = 8 * count + 8 * part
        out_ref[first : first + 8, :] = jnp.abs(found[0])
        out_ref[first + count : first + count + 8, :] = jnp.where(found[0] > 0, 1.0, 0.0)
        if pick_ref is not None:
            pick_ref[rows, :] = found[1].astype(I32)


def apply_incoming(field_ref, flag_ref, inverse_ref, in_ref, new_field_ref, new_flag_ref, flag_in_ref):
    tile_rows = flag_ref.shape[0]
    count = flag_in_ref.shape[0]
    base = 8 * count
    density_in = in_ref[base : base + count, :]
    flag_in_ref[...] = jnp.where(in_ref[base + count : base + 2 * count, :] > 0.5, density_in, -density_in)

    def body(row, carry):
        where = pl.ds(aligned(row * LANES, LANES), LANES)
        slot = inverse_ref[pl.ds(row, 1), :].astype(I32) - 1
        new_field_ref[:, where] = pick_fields(row_blocks(in_ref, count), slot, field_ref[:, where])
        return carry

    lax.fori_loop(0, tile_rows, body, 0, unroll=16)
    for part in range(tile_rows // 8):
        rows = slice(8 * part, 8 * part + 8)
        slot = inverse_ref[rows, :].astype(I32) - 1
        new_flag_ref[rows, :] = pick_rows([flag_in_ref], slot, [flag_ref[rows, :]])[0]


def first_kernel(particle_ref, flag_ref, send_in_ref, field_ref, out_ref, send_ref, index_ref):
    stage_index(send_in_ref, 0, index_ref)
    gather_outgoing(particle_ref, flag_ref, index_ref, out_ref)
    field_ref[...] = particle_ref[...]
    send_ref[...] = send_in_ref[...]


def inverse_kernel(count_ref, send_ref, *inverse_refs):
    slots = send_ref.shape[1]
    slot = iota((1, slots), 1)
    for level, inverse_ref in enumerate(inverse_refs):
        tile_rows = inverse_ref.shape[0]
        rows = send_ref[level : level + 1, :]
        taken = slot < count_ref[level]
        high = jnp.where(taken, rows >> 7, -1)
        low = rows & 127
        number = slot + 1
        hit = spread(high, tile_rows) == iota((tile_rows, slots), 0)
        coarse = jnp.where(hit, spread((number >> 6).astype(F32), tile_rows), 0.0)
        fine = jnp.where(hit, spread((number & 63).astype(F32), tile_rows), 0.0)
        left = jnp.concatenate([coarse, fine], axis=0).astype(jnp.bfloat16)
        right = jnp.where(spread(low, LANES) == iota((LANES, slots), 0), 1.0, 0.0).astype(jnp.bfloat16)
        both = lax.dot_general(left, right, (((1,), (1,)), ((), ())), preferred_element_type=F32)
        inverse_ref[...] = both[:tile_rows] * 64.0 + both[tile_rows:]


def ahead_first_kernel(field_ref, flag_ref, inverse_ref, send_ref, partial_ref, pick_ref, index_ref):
    stage_index(send_ref, 1, index_ref)
    gather_outgoing(field_ref, flag_ref, index_ref, partial_ref, inverse_ref, pick_ref)


def ahead_kernel(level, field_ref, flag_ref, before_ref, in_ref, inverse_ref, send_ref, new_field_ref, new_flag_ref, partial_ref, pick_ref, index_ref, flag_in_ref):
    apply_incoming(field_ref, flag_ref, before_ref, in_ref, new_field_ref, new_flag_ref, flag_in_ref)
    stage_index(send_ref, level + 1, index_ref)
    gather_outgoing(new_field_ref, new_flag_ref, index_ref, partial_ref, inverse_ref, pick_ref)


def fix_kernel(partial_ref, pick_ref, in_ref, out_ref):
    count = pick_ref.shape[0]

    def body(step, carry):
        where = pl.ds(aligned(step * 8), 8)
        slot = pick_ref[pl.ds(step, 1), :] - 1
        out_ref[where, :] = pick_fields(row_blocks(in_ref, count), slot, partial_ref[where, :])
        return carry

    lax.fori_loop(0, count, body, 0, unroll=True)
    base = 8 * count
    for part in range(count // 8):
        slot = pick_ref[8 * part : 8 * part + 8, :] - 1
        tables = [in_ref.at[pl.ds(base, count)], in_ref.at[pl.ds(base + count, count)]]
        places = [slice(base + n * count + 8 * part, base + n * count + 8 * part + 8) for n in range(2)]
        found = pick_rows(tables, slot, [partial_ref[place, :] for place in places])
        for place, value in zip(places, found):
            out_ref[place, :] = value


def apply_kernel(field_ref, flag_ref, inverse_ref, in_ref, new_field_ref, new_flag_ref, flag_in_ref):
    apply_incoming(field_ref, flag_ref, inverse_ref, in_ref, new_field_ref, new_flag_ref, flag_in_ref)


def gather_exports(field_ref, index_ref, first, count, out_ref):
    def body(step, carry):
        row = index_ref[pl.ds(first + step, 1), :]
        out_ref[pl.ds(aligned(step * 8), 8), :] = pick_fields(
            lane_blocks(field_ref), row, jnp.zeros((8, LANES), F32)
        )
        return carry

    lax.fori_loop(0, count, body, 0, unroll=8)


def last_kernel(field_ref, flag_ref, inverse_ref, in_ref, export_ref, new_field_ref, new_flag_ref, low_ref, high_ref, index_ref, flag_in_ref):
    blocks = export_ref.shape[1] // LANES
    for number in range(8):
        for block in range(blocks):
            at = number * blocks + block
            index_ref[at : at + 1, :] = export_ref[number : number + 1, LANES * block : LANES * (block + 1)]
    apply_incoming(field_ref, flag_ref, inverse_ref, in_ref, new_field_ref, new_flag_ref, flag_in_ref)
    gather_exports(new_field_ref, index_ref, 0, 3 * blocks, low_ref)
    gather_exports(new_field_ref, index_ref, 5 * blocks, 3 * blocks, high_ref)


def middle_kernel(field_ref, index_ref, out_ref):
    blocks = index_ref.shape[0] // 8
    gather_exports(field_ref, index_ref, 3 * blocks, 2 * blocks, out_ref)


EXPANDED = 8
NEAR_FIELDS = (0, 1, 2, 6)
SPEED_FIELDS = (3, 4, 5)
SLOPE_NORM = 0.375 * PARTICLE_MASS / math.pi


def derived(height):
    inverse = 1.0 / height
    square = inverse * inverse
    return inverse, SLOPE_NORM * (square * square)


def expand_targets(compact_ref, chunk, base, expanded_ref, fields=range(7), shift=0):
    groups = compact_ref.shape[0] // (4 * 32)
    region = (groups * 32 + 1) * 8
    half_base = jnp.where(iota((8, LANES), 1) < 64, 0, 64)
    for inner in range(8):
        for field in fields:
            index = half_base + (inner * 8 + field)
            for group in range(groups):
                for section in range(2):
                    for half in range(2):
                        place = ((group * 2 + section) * 2 + half) * 8
                        start = aligned(chunk * (groups * 32) + place)
                        tile = 2 * (group * 16 + section * 8 + inner) + half
                        value = lane_pick(compact_ref[pl.ds(start, 8), :], index)
                        first = base + (field - shift) * region + tile * 8
                        if field == 6:
                            inverse, norm = derived(value)
                            expanded_ref[pl.ds(aligned(first), 8), :] = inverse
                            expanded_ref[pl.ds(aligned(first + region), 8), :] = norm
                        else:
                            expanded_ref[pl.ds(aligned(first), 8), :] = value


def target_kernel(count_ref, field_ref, flag_ref, pair_ref,
                  compact_ref, rank_ref, order_ref, list_ref, length_ref, expanded_ref,
                  stack_ref):
    tile_rows = flag_ref.shape[0]
    groups = tile_rows // 16
    tile_count = 2 * tile_rows
    region = (tile_count + 1) * 8
    active = flag_ref[...] > 0
    ones = jnp.where(active, 1.0, 0.0).astype(jnp.bfloat16)
    a = iota((LANES, LANES), 0)
    b = iota((LANES, LANES), 1)
    same = (a >> 6) == (b >> 6)
    before = jnp.where(same & (a < b), 1.0, 0.0).astype(jnp.bfloat16)
    whole = jnp.where(same, 1.0, 0.0).astype(jnp.bfloat16)
    rank = jnp.dot(ones, before, preferred_element_type=F32).astype(I32)
    total = jnp.dot(ones, whole, preferred_element_type=F32)
    rank_ref[...] = rank
    lane = iota((tile_rows, LANES), 1)
    code = jnp.where(active, lane + 128 * ((lane & 63) - rank), -1)
    for bit in range(6):
        moved = pltpu.roll(code, LANES - (1 << bit), 1)
        take = (moved >= 0) & (((moved >> (7 + bit)) & 1) == 1)
        keep = (code >= 0) & (((code >> (7 + bit)) & 1) == 0)
        code = jnp.where(take, moved, jnp.where(keep, code, -1))
    order_ref[...] = jnp.where(code >= 0, code & 127, lane)
    left_half = iota((8, LANES), 1) < 64
    for group in range(groups):
        for inner in range(16):
            row = group * 16 + inner
            stack_ref[8 * inner : 8 * inner + 8, :] = lane_pick(
                field_ref[:, LANES * row : LANES * (row + 1)], spread(order_ref[row : row + 1, :])
            )
        turned = jnp.transpose(stack_ref[...])
        for half in range(2):
            for chunk in range(4):
                first = half * 64 + chunk * 16
                near, far = turned[first : first + 8], turned[first + 8 : first + 16]
                for section in range(2):
                    if section == 0:
                        mixed = jnp.where(left_half, near, pltpu.roll(far, 64, 1))
                    else:
                        mixed = jnp.where(left_half, pltpu.roll(near, 64, 1), far)
                    place = (((chunk * groups + group) * 2 + section) * 2 + half) * 8
                    compact_ref[place : place + 8, :] = mixed

    pairs = pair_ref.shape[1]
    slots = list_ref.shape[1]
    target, source = pair_ref[0:1, :], pair_ref[1:2, :]
    folded = jnp.where((lane & 63) == iota((tile_rows, LANES), 0), total, 0.0)
    totals = spread(jnp.sum(folded, axis=0, keepdims=True))
    place = spread((target & 1) * 64 + (target >> 1))
    need = jnp.concatenate(
        [lane_pick(totals, place[:, LANES * q : LANES * (q + 1)]) for q in range(pairs // LANES)], axis=1
    )
    sub = iota((8, pairs), 0)
    is_ghost = spread(source) >= tile_count
    member = (
        (iota((8, pairs), 1) < count_ref[0])
        & (need > (16 * (sub & 3)).astype(F32))
        & (is_ghost == (sub >= 4))
    )
    member_value = jnp.where(member, 1.0, 0.0)
    earlier = jnp.where(iota((pairs, pairs), 0) < iota((pairs, pairs), 1), 1.0, 0.0).astype(jnp.bfloat16)
    position = jnp.dot(member_value.astype(jnp.bfloat16), earlier, preferred_element_type=F32).astype(I32)
    length = jnp.broadcast_to(jnp.sum(member_value, axis=1, keepdims=True), (8, LANES)).astype(I32)
    length_ref[...] = length
    own_steps = ((length + (UNROLL - 1)) // UNROLL) * UNROLL
    base = jnp.where(iota((8, LANES), 0) >= 4, pltpu.roll(own_steps, 4, 0), 0)
    position = position + jnp.concatenate([base] * (pairs // LANES), axis=1)
    position = jnp.where(member, position, -1)
    local = jnp.where(source >= tile_count, source - tile_count, source)
    values = jnp.where(
        sub == 0, spread(target + 1), jnp.where(sub == 1, spread(local + 1), 0)
    ).astype(F32).astype(jnp.bfloat16)

    def make_list(chunk):
        row = jnp.maximum(position[chunk : chunk + 1, :], position[chunk + 4 : chunk + 5, :])
        hit = jnp.where(spread(row, slots) == iota((slots, pairs), 0), 1.0, 0.0).astype(jnp.bfloat16)
        found = lax.dot_general(
            values, hit, (((1,), (1,)), ((), ())), preferred_element_type=F32
        ).astype(I32)
        list_ref[chunk : chunk + 1, :] = jnp.where(found[0:1] > 0, found[0:1] - 1, tile_count) * 8
        list_ref[4 + chunk : 5 + chunk, :] = jnp.maximum(found[1:2] - 1, 0) * 8

    make_list(0)
    make_list(1)

    @pl.when(jnp.max(total) > 32.0)
    def _():
        make_list(2)
        make_list(3)

    def one_chunk(chunk, carry):
        expand_targets(compact_ref, chunk, aligned(chunk * (EXPANDED * region)), expanded_ref, NEAR_FIELDS)
        return carry

    lax.fori_loop(0, 2, one_chunk, 0)


def reduce_targets(sum_ref, first, tile_count, section, out_ref):
    blocks = tile_count // 16
    for block in range(blocks):
        start = first + block * LANES
        turned = jnp.transpose(sum_ref[start : start + LANES, :])
        for half in range(2):
            total = jnp.sum(turned[64 * half : 64 * half + 64], axis=0, keepdims=True)
            out_ref[pl.ds((section * 2 + half) * blocks + block, 1), :] = total


def place_results(red_ref, blocks, part, rank):
    row = iota((8, LANES), 0)
    half = iota((8, LANES), 1) >> 6
    index = (2 * row + half) * 8 + (rank & 7)
    which = rank >> 3
    found = jnp.zeros((8, LANES), F32)
    for section in range(8):
        table = spread(red_ref[section * blocks + part : section * blocks + part + 1, :])
        found = jnp.where(which == section, lane_pick(table, index), found)
    return found


def clear(sum_ref, first, rows):
    for at in range(0, rows, 8):
        sum_ref[first + at : first + at + 8, :] = jnp.zeros((8, LANES), F32)


def steps_of(length):
    return (length + (UNROLL - 1)) // UNROLL


def span(length_ref, chunk, ghost):
    own = steps_of(length_ref[chunk, 0])
    if not ghost:
        return 0, own
    return own, own + steps_of(length_ref[chunk + 4, 0])


def double_into(pool_ref, row, value):
    left = iota((8, LANES), 1) < 64
    other = pltpu.roll(value, 64, 1)
    pool_ref[16 * row : 16 * row + 8, :] = jnp.where(left, value, other)
    pool_ref[16 * row + 8 : 16 * row + 16, :] = jnp.where(left, other, value)


def density_pairs(list_ref, length_ref, chunk, ghost, expanded_ref, base, region, pool_ref, sum_ref, sum_base):
    def step(number, carry):
        results = []
        for u in range(UNROLL):
            target = list_ref[chunk, number * UNROLL + u]
            source = list_ref[chunk + 4, number * UNROLL + u]

            def at(field, target=target):
                return expanded_ref[pl.ds(aligned(target + (base + field * region)), 8), :]

            square = None
            for axis in range(3):
                gap = at(axis) - pool_ref[pl.ds(source + axis, 8, stride=0), :]
                gap = gap - jnp.floor(gap + 0.5)
                square = gap * gap if square is None else square + gap * gap
            safe = jnp.maximum(square, 1.2e-38)
            ratio = safe * lax.rsqrt(safe) * at(6)
            outer = jnp.maximum(2.0 - ratio, 0.0)
            inner = jnp.maximum(1.0 - ratio, 0.0)
            results.append((target, 0.25 * (outer * outer * outer) - inner * inner * inner))
        for target, value in results:
            sum_ref[pl.ds(aligned(target + sum_base), 8), :] += value
        return carry

    first, last = span(length_ref, chunk, ghost)
    lax.fori_loop(first, last, step, 0)


def density_own_kernel(list_ref, length_ref, field_ref, expanded_ref, compact_ref, pool_ref, sum_ref, speed_ref):
    tile_rows = field_ref.shape[1] // LANES
    region = (2 * tile_rows + 1) * 8
    for row in range(tile_rows):
        double_into(pool_ref, row, field_ref[:, LANES * row : LANES * (row + 1)])
    clear(sum_ref, 0, 2 * region)
    for chunk in range(2):
        density_pairs(
            list_ref, length_ref, chunk, False, expanded_ref, chunk * EXPANDED * region, region,
            pool_ref, sum_ref, chunk * region,
        )

    def one_chunk(chunk, carry):
        expand_targets(compact_ref, chunk, aligned(chunk * (3 * region)), speed_ref, SPEED_FIELDS, 3)
        return carry

    lax.fori_loop(0, 2, one_chunk, 0)


def density_kernel(list_ref, length_ref, compact_ref, expanded_ref, own_pool_ref, own_sum_ref, rank_ref, field_ref, flag_ref, low_ref, high_ref, down_ref, up_ref, export_ref,
                   density_ref, low_out, middle_out, high_out, pool_ref, sum_ref, result_ref,
                   red_ref, height_ref, spare_ref):
    tile_rows = flag_ref.shape[0]
    tile_count = 2 * tile_rows
    region = (tile_count + 1) * 8
    ghosts = (low_ref, high_ref, down_ref, up_ref)
    unit = low_ref.shape[0] // 3
    blocks = unit // 8
    for number, (which, start) in enumerate(ghost_place(unit)):
        for block in range(blocks):
            first = start + 8 * block
            double_into(pool_ref, number * blocks + block, ghosts[which][first : first + 8, :])
    for chunk in range(2):
        density_pairs(
            list_ref, length_ref, chunk, True, expanded_ref, chunk * EXPANDED * region, region,
            pool_ref, sum_ref, chunk * region,
        )
        reduce_targets(sum_ref, chunk * region, tile_count, chunk, red_ref)
    for row in range(4 * (tile_count // 16), 8 * (tile_count // 16), 8):
        red_ref[row : row + 8, :] = jnp.zeros((8, LANES), F32)

    def rare_chunk(chunk, carry):
        @pl.when(length_ref[chunk, 0] + length_ref[chunk + 4, 0] > 0)
        def _():
            expand_targets(compact_ref, chunk, 0, spare_ref)
            clear(sum_ref, 0, region)
            density_pairs(list_ref, length_ref, chunk, False, spare_ref, 0, region, own_pool_ref, sum_ref, 0)
            density_pairs(list_ref, length_ref, chunk, True, spare_ref, 0, region, pool_ref, sum_ref, 0)
            reduce_targets(sum_ref, 0, tile_count, chunk, red_ref)

        return carry

    lax.fori_loop(2, 4, rare_chunk, 0)
    for row in range(tile_rows):
        height_ref[row : row + 1, :] = field_ref[6:7, LANES * row : LANES * (row + 1)]
    for part in range(tile_rows // 8):
        rows = slice(8 * part, 8 * part + 8)
        found = place_results(red_ref, tile_count // 16, part, rank_ref[rows, :])
        height = height_ref[rows, :]
        flag = flag_ref[rows, :]
        norm = PARTICLE_MASS / (math.pi * height * height * height)
        density_ref[rows, :] = jnp.where(flag > 0, norm * (1.0 + found), jnp.abs(flag))
        result_ref[rows, :] = density_ref[rows, :]
    outs = (low_out, middle_out, high_out)
    zero = jnp.zeros((8, LANES), F32)
    for block in range(blocks):
        index = export_ref[:, LANES * block : LANES * (block + 1)]
        found = pick_rows([density_ref], index, [zero])[0]
        for number, (which, start) in enumerate(export_place(blocks)):
            outs[which][start + block : start + block + 1, :] = found[number : number + 1, :]


def source_tables(pool_ref, tile, first_ref, second_ref, density=None):
    sub = iota((8, LANES), 0)
    rows = slice(8 * tile, 8 * tile + 8)
    value = pool_ref[rows, :]
    inverse, norm = derived(value)
    press = (ADIABATIC - 1.0) * value
    if density is not None:
        press = press / density
    first_ref[rows, :] = jnp.where(sub == 7, press, jnp.where(sub == 6, inverse, value))
    second_ref[rows, :] = norm


def doubled_halves(row):
    left = iota((8, LANES), 1) < 64
    wide = spread(row)
    other = pltpu.roll(wide, 64, 1)
    return jnp.where(left, wide, other), jnp.where(left, other, wide)


def force_pairs(list_ref, length_ref, chunk, ghost, expanded_ref, base, speed_ref, speed_base, region, press_ref, press_base, first_ref, second_ref, sum_ref):
    def step(number, carry):
        results = []
        for u in range(UNROLL):
            target = list_ref[chunk, number * UNROLL + u]
            source = list_ref[chunk + 4, number * UNROLL + u]

            def at(field, target=target):
                return expanded_ref[pl.ds(aligned(target + (base + field * region)), 8), :]

            def speed(axis, target=target):
                return speed_ref[pl.ds(aligned(target + (speed_base + axis * region)), 8), :]

            def source_row(field, source=source):
                return first_ref[pl.ds(source + field, 8, stride=0), :]

            def source_more(field, source=source):
                return second_ref[pl.ds(source + field, 8, stride=0), :]

            gaps = []
            square = None
            approach = None
            for axis in range(3):
                gap = at(axis) - source_row(axis)
                gap = gap - jnp.floor(gap + 0.5)
                gaps.append(gap)
                square = gap * gap if square is None else square + gap * gap
                part = (speed(axis) - source_row(3 + axis)) * gap
                approach = part if approach is None else approach + part
            safe = jnp.maximum(square, 1.2e-38)
            inverse_distance = lax.rsqrt(safe)
            distance = safe * inverse_distance

            def slope(inverse_height, norm):
                ratio = distance * inverse_height
                outer = 2.0 - ratio
                inner = jnp.maximum(outer - ratio, 0.0)
                outer = jnp.maximum(outer, 0.0)
                return norm * (inner * inner - outer * outer)

            total = slope(at(6), at(7)) + slope(source_row(6), source_more(6))
            press = press_ref[pl.ds(aligned(target + press_base), 8), :] + source_row(7)
            weight = press * (total * inverse_distance)
            results.append((target, [weight * gap for gap in gaps] + [weight * approach]))
        for target, values in results:
            for quantity in range(4):
                sum_ref[pl.ds(aligned(target + quantity * region), 8), :] += values[quantity]
        return carry

    first, last = span(length_ref, chunk, ghost)
    lax.fori_loop(first, last, step, 0)


def expand_press(press_compact_ref, chunk, tile_rows, press_ref, base):
    half_base = jnp.where(iota((8, LANES), 1) < 64, 0, 64)
    for row in range(tile_rows):
        for half in range(2):
            start = aligned(chunk * 16 + half * 8)
            first = base + (2 * row + half) * 8
            press_ref[first : first + 8, :] = lane_pick(
                press_compact_ref[pl.ds(start, 8), :], half_base + row
            )


def force_own_kernel(list_ref, length_ref, density_ref, field_ref, order_ref, expanded_ref, speed_ref, pool_ref,
                     first_ref, second_ref, press_compact_ref, press_ref, sum_ref,
                     energy_ref, ordered_ref):
    tile_rows = density_ref.shape[0]
    tile_count = 2 * tile_rows
    region = (tile_count + 1) * 8
    left = iota((8, LANES), 1) < 64
    for row in range(tile_rows):
        near, far = doubled_halves(density_ref[row : row + 1, :])
        source_tables(pool_ref, 2 * row, first_ref, second_ref, near)
        source_tables(pool_ref, 2 * row + 1, first_ref, second_ref, far)
        energy_ref[row : row + 1, :] = field_ref[7:8, LANES * row : LANES * (row + 1)]
    for part in range(tile_rows // 8):
        rows = slice(8 * part, 8 * part + 8)
        press = (ADIABATIC - 1.0) * energy_ref[rows, :] / density_ref[rows, :]
        ordered_ref[rows, :] = lane_pick(press, order_ref[rows, :])
    ordered_ref[tile_rows:, :] = jnp.zeros((LANES - tile_rows, LANES), F32)
    turned = jnp.transpose(ordered_ref[...])
    for half in range(2):
        for chunk in range(4):
            first = half * 64 + chunk * 16
            near, far = turned[first : first + 8], turned[first + 8 : first + 16]
            place_at = (chunk * 2 + half) * 8
            press_compact_ref[place_at : place_at + 8, :] = jnp.where(left, near, pltpu.roll(far, 64, 1))
    for chunk in range(2):
        expand_press(press_compact_ref, chunk, tile_rows, press_ref, chunk * region)
    clear(sum_ref, 0, 4 * region)
    force_pairs(
        list_ref, length_ref, 0, False, expanded_ref, 0, speed_ref, 0, region, press_ref, 0, first_ref, second_ref, sum_ref,
    )


def force_own_more_kernel(list_ref, length_ref, expanded_ref, speed_ref, press_ref, own_first_ref, own_second_ref, pool_ref,
                          sum_ref, first_ref, second_ref):
    region = sum_ref.shape[0] // 4
    for tile in range(pool_ref.shape[0] // 8):
        source_tables(pool_ref, tile, first_ref, second_ref)
    clear(sum_ref, 0, 4 * region)
    force_pairs(
        list_ref, length_ref, 1, False, expanded_ref, EXPANDED * region, speed_ref, 3 * region, region, press_ref, region,
        own_first_ref, own_second_ref, sum_ref,
    )


def force_kernel(list_ref, length_ref, compact_ref, expanded_ref, speed_ref, press_compact_ref, press_ref, rank_ref, flag_ref, own_first_ref, own_second_ref, half_ref, second_ref, zero_sum_ref, one_sum_ref, low_ref, high_ref, down_ref, up_ref,
                 accel_ref, heat_ref, first_sum_ref, second_sum_ref,
                 first_ref, sum_ref, red_ref, spare_ref, spare_press_ref):
    tile_rows = flag_ref.shape[0]
    tile_count = 2 * tile_rows
    region = (tile_count + 1) * 8
    blocks = tile_count // 16
    is_press = iota((8, LANES), 0) == 7
    ghosts = (low_ref, high_ref, down_ref, up_ref)
    unit = low_ref.shape[0] // 3
    for number, (which, start) in enumerate(ghost_place(unit)):
        for block in range(unit):
            row = number * unit + block
            for half, density in enumerate(doubled_halves(ghosts[which][start + block : start + block + 1, :])):
                rows = slice(16 * row + 8 * half, 16 * row + 8 * half + 8)
                value = half_ref[rows, :]
                first_ref[rows, :] = jnp.where(is_press, value / density, value)
    for chunk in range(2):
        chunk_sum_ref = first_sum_ref if chunk == 0 else second_sum_ref
        force_pairs(
            list_ref, length_ref, chunk, True, expanded_ref, chunk * EXPANDED * region,
            speed_ref, chunk * 3 * region, region,
            press_ref, chunk * region, first_ref, second_ref, chunk_sum_ref,
        )
        for quantity in range(4):
            reduce_targets(chunk_sum_ref, quantity * region, tile_count, chunk + 4 * quantity, red_ref)
    for quantity in range(4):
        for row in range(4 * blocks, 8 * blocks, 8):
            at = quantity * 8 * blocks + row
            red_ref[at : at + 8, :] = jnp.zeros((8, LANES), F32)

    def rare_chunk(chunk, carry):
        @pl.when(length_ref[chunk, 0] + length_ref[chunk + 4, 0] > 0)
        def _():
            expand_targets(compact_ref, chunk, 0, spare_ref)
            expand_press(press_compact_ref, chunk, tile_rows, spare_press_ref, 0)
            clear(sum_ref, 0, 4 * region)
            force_pairs(
                list_ref, length_ref, chunk, False, spare_ref, 0, spare_ref, 3 * region, region, spare_press_ref, 0,
                own_first_ref, own_second_ref, sum_ref,
            )
            force_pairs(
                list_ref, length_ref, chunk, True, spare_ref, 0, spare_ref, 3 * region, region, spare_press_ref, 0,
                first_ref, second_ref, sum_ref,
            )
            for quantity in range(4):
                reduce_targets(sum_ref, quantity * region, tile_count, chunk + 4 * quantity, red_ref)

        return carry

    lax.fori_loop(2, 4, rare_chunk, 0)
    for part in range(tile_rows // 8):
        rank = rank_ref[8 * part : 8 * part + 8, :]
        flag = flag_ref[8 * part : 8 * part + 8, :]
        for quantity in range(4):
            found = place_results(red_ref.at[pl.ds(quantity * 8 * blocks, 8 * blocks)], blocks, part, rank)
            if quantity == 3:
                heat_ref[8 * part : 8 * part + 8, :] = jnp.where(flag > 0, 0.5 * found, 0.0)
            else:
                found = jnp.where(flag > 0, -found, 0.0)
                for row in range(8):
                    at = LANES * (8 * part + row)
                    accel_ref[quantity : quantity + 1, at : at + LANES] = found[row : row + 1, :]


def call(kernel, outs, scratch, operands, scalars=0, aliases=None):
    smem = pl.BlockSpec(memory_space=pltpu.SMEM)
    vmem = pl.BlockSpec(memory_space=pltpu.VMEM)
    return pl.pallas_call(
        kernel,
        out_shape=[jax.ShapeDtypeStruct(shape, dtype) for shape, dtype in outs],
        in_specs=[smem if i < scalars else vmem for i in range(len(operands))],
        out_specs=[vmem] * len(outs),
        scratch_shapes=[pltpu.VMEM(shape, dtype) for shape, dtype in scratch],
        input_output_aliases=aliases or {},
        compiler_params=pltpu.CompilerParams(vmem_limit_bytes=24 * 2**20),
    )(*operands)


def on_device(
    particles, old_density, active, send_rows, send_count, export_rows, pair_tiles, pair_count
):
    row_count = particles.shape[1]
    levels, slots = send_rows.shape
    ghosts = export_rows.shape[1]
    pair_total = pair_tiles.shape[1]
    tile_rows = row_count // LANES
    tile_count = 2 * tile_rows
    in_blocks = slots // LANES
    unit = 8 * (ghosts // LANES)
    dense_unit = ghosts // LANES
    region = (tile_count + 1) * 8
    list_slots = -(-(pair_total + 2 * UNROLL) // LANES) * LANES
    bits_x = lax.axis_size("gx").bit_length() - 1
    bits_y = lax.axis_size("gy").bit_length() - 1

    row = ((tile_rows, LANES), F32)
    whole = ((8, row_count), F32)
    offered = ((10 * in_blocks, LANES), F32)
    picked = ((in_blocks, LANES), I32)
    index_scratch = ((in_blocks, LANES), I32)
    flag_scratch = ((in_blocks, LANES), F32)
    exported = [((3 * unit, LANES), F32), ((2 * unit, LANES), F32), ((3 * unit, LANES), F32)]

    def swap(block, level):
        if level < 2:
            return from_partner(block, "gx", bits_x - 1 - level)
        return from_partner(block, "gy", bits_y + 1 - level)

    flag = jnp.where(active == 1, old_density, -old_density).reshape(tile_rows, LANES)
    fields, outgoing, send_rows = call(
        first_kernel,
        [whole, offered, (send_rows.shape, I32)],
        [index_scratch],
        [particles, flag, send_rows],
    )
    incoming = swap(outgoing, 0)
    inverse = call(inverse_kernel, [row] * levels, [], [send_count[:, 0], send_rows], scalars=1)
    partial, pick = call(
        ahead_first_kernel, [offered, picked], [index_scratch], [fields, flag, inverse[0], send_rows]
    )
    (outgoing,) = call(fix_kernel, [offered], [], [partial, pick, incoming])
    before = incoming
    incoming = swap(outgoing, 1)
    ahead = [whole, row, offered, picked]
    ahead_scratch = [index_scratch, flag_scratch]
    fields, flag, partial, pick = call(
        lambda *refs: ahead_kernel(1, *refs),
        ahead,
        ahead_scratch,
        [fields, flag, inverse[0], before, inverse[1], send_rows],
    )
    (outgoing,) = call(fix_kernel, [offered], [], [partial, pick, incoming])
    before = incoming
    incoming = swap(outgoing, 2)
    fields, flag, partial, pick = call(
        lambda *refs: ahead_kernel(2, *refs),
        ahead,
        ahead_scratch,
        [fields, flag, inverse[1], before, inverse[2], send_rows],
    )
    (outgoing,) = call(fix_kernel, [offered], [], [partial, pick, incoming])
    before = incoming
    incoming = swap(outgoing, 3)
    fields, flag = call(
        apply_kernel, [whole, row], [flag_scratch], [fields, flag, inverse[2], before]
    )
    fields, flag, low, high, export_index = call(
        last_kernel,
        [whole, row, exported[0], exported[2], ((8 * dense_unit, LANES), I32)],
        [flag_scratch],
        [fields, flag, inverse[3], incoming, export_rows],
    )
    low, high = along_x(low, high)
    (middle,) = call(middle_kernel, [exported[1]], [], [fields, export_index])
    compact, rank, order, lists, lengths, expanded = call(
        target_kernel,
        [
            ((8 * tile_rows, LANES), F32),
            ((tile_rows, LANES), I32),
            ((tile_rows, LANES), I32),
            ((8, list_slots), I32),
            ((8, LANES), I32),
            ((2 * EXPANDED * region, LANES), F32),
        ],
        [((LANES, LANES), F32)],
        [pair_count, fields, flag, pair_tiles],
        scalars=1,
    )
    low, high, lengths = lax.optimization_barrier((low, high, lengths))
    down, up = along_y(low, middle, high, unit)
    pool_shape = ((tile_count * 8, LANES), F32)
    ghost_pool_shape = ((2 * 8 * dense_unit * 8, LANES), F32)
    own_pool, own_sum, speed = call(
        density_own_kernel,
        [pool_shape, ((2 * region, LANES), F32), ((6 * region, LANES), F32)],
        [],
        [lists, lengths, fields, expanded, compact],
        scalars=2,
    )
    density, low_d, middle_d, high_d, ghost_pool, _, density_out = call(
        density_kernel,
        [
            row,
            ((3 * dense_unit, LANES), F32),
            ((2 * dense_unit, LANES), F32),
            ((3 * dense_unit, LANES), F32),
            ghost_pool_shape,
            ((2 * region, LANES), F32),
            row,
        ],
        [
            ((8 * (tile_count // 16), LANES), F32),
            row,
            ((EXPANDED * region, LANES), F32),
        ],
        [
            lists, lengths, compact, expanded, own_pool, own_sum,
            rank, fields, flag, low, high, down, up, export_rows,
        ],
        scalars=2,
        aliases={5: 5},
    )
    low_d, high_d = along_x(low_d, high_d)
    sums = ((4 * region, LANES), F32)
    own_first, own_second, press_compact, press, zero_sum = call(
        force_own_kernel,
        [pool_shape, pool_shape, ((64, LANES), F32), ((2 * region, LANES), F32), sums],
        [row, ((LANES, LANES), F32)],
        [lists, lengths, density, fields, order, expanded, speed, own_pool],
        scalars=2,
    )
    low_d, high_d, press = lax.optimization_barrier((low_d, high_d, press))
    down_d, up_d = along_y(low_d, middle_d, high_d, dense_unit)
    one_sum, ghost_first, ghost_second = call(
        force_own_more_kernel,
        [sums, ghost_pool_shape, ghost_pool_shape],
        [],
        [lists, lengths, expanded, speed, press, own_first, own_second, ghost_pool],
        scalars=2,
    )
    accel, heat, _, _ = call(
        force_kernel,
        [((3, row_count), F32), row, sums, sums],
        [
            ghost_pool_shape,
            sums,
            ((32 * (tile_count // 16), LANES), F32),
            ((EXPANDED * region, LANES), F32),
            ((region, LANES), F32),
        ],
        [
            lists, lengths, compact, expanded, speed, press_compact, press, rank, flag,
            own_first, own_second, ghost_first, ghost_second, zero_sum, one_sum,
            low_d, high_d, down_d, up_d,
        ],
        scalars=2,
        aliases={13: 2, 14: 3},
    )
    return (density_out.reshape(row_count), accel, heat.reshape(row_count))


def solution(mesh):
    in_specs = (
        P(None, ("gx", "gy")),
        P(("gx", "gy")),
        P(("gx", "gy")),
        P(None, ("gx", "gy")),
        P(None, ("gx", "gy")),
        P(None, ("gx", "gy")),
        P(None, ("gx", "gy")),
        P(("gx", "gy")),
    )
    out_specs = (P(("gx", "gy")), P(None, ("gx", "gy")), P(("gx", "gy")))
    return jax.shard_map(
        on_device, mesh=mesh, in_specs=in_specs, out_specs=out_specs, check_vma=False
    )
```

```python
import math

import jax
import jax.numpy as jnp
from jax import lax
from jax.experimental import pallas as pl
from jax.experimental.pallas import tpu as pltpu
from jax.sharding import PartitionSpec as P

TILE = 64
LANES = 128
UNROLL = 8

PARTICLE_MASS = 1.0 / 512.0
ADIABATIC = 5.0 / 3.0
F32 = jnp.float32
I32 = jnp.int32


def from_behind(value, axis, steps):
    count = lax.axis_size(axis)
    pairs = [(source, (source + steps) % count) for source in range(count)]
    return lax.ppermute(value, axis, pairs)


def from_partner(block, axis, bit):
    count = lax.axis_size(axis)
    route = []
    for low in range(count):
        high = low | 1 << bit
        if high != low and high < count:
            route += [(low, high), (high, low)]
    return lax.ppermute(block, axis, route)


def along_x(low, high):
    count = lax.axis_size("gx")
    if count % 2:
        return from_behind(low, "gx", -1), from_behind(high, "gx", 1)
    even = lax.axis_index("gx") % 2 == 0
    first = [(i, i ^ 1) for i in range(count)]
    second = [(i, (i + 1) % count if i % 2 else (i - 1) % count) for i in range(count)]
    after = lax.ppermute(jnp.where(even, high, low), "gx", first)
    before = lax.ppermute(jnp.where(even, low, high), "gx", second)
    return jnp.where(even, after, before), jnp.where(even, before, after)


def along_y(low, middle, high, unit):
    down = jnp.concatenate([low[:unit], middle[:unit], high[:unit]], axis=0)
    up = jnp.concatenate([low[2 * unit :], middle[unit:], high[2 * unit :]], axis=0)
    return from_behind(down, "gy", -1), from_behind(up, "gy", 1)


def ghost_place(unit):
    return ((2, 0), (0, unit), (3, 0), (2, unit), (3, unit), (2, 2 * unit), (1, unit), (3, 2 * unit))


def export_place(unit):
    return ((0, 0), (0, unit), (0, 2 * unit), (1, 0), (1, unit), (2, 0), (2, unit), (2, 2 * unit))


def lane_pick(table, index):
    return jnp.take_along_axis(table, index, axis=1, mode="promise_in_bounds")


def spread(row, rows=8):
    return jnp.broadcast_to(row, (rows, row.shape[1]))


def iota(shape, axis):
    return lax.broadcasted_iota(I32, shape, axis)


def aligned(value, size=8):
    return pl.multiple_of(value, size)


def pick_fields(tables, row, start):
    high, low = spread(row >> 7), spread(row & 127)
    found = start
    for block, table in enumerate(tables):
        found = jnp.where(high == block, lane_pick(table, low), found)
    return found


def pick_rows(table_refs, index, starts):
    high, low = index >> 7, index & 127
    found = list(starts)
    for block in range(table_refs[0].shape[0]):
        here = high == block
        for n, ref in enumerate(table_refs):
            found[n] = jnp.where(here, lane_pick(spread(ref[block : block + 1, :]), low), found[n])
    return found


def lane_blocks(ref):
    return [ref[:, LANES * b : LANES * (b + 1)] for b in range(ref.shape[1] // LANES)]


def row_blocks(ref, count):
    return [ref[8 * b : 8 * b + 8, :] for b in range(count)]


def stage_index(send_ref, level, index_ref):
    for j in range(index_ref.shape[0]):
        index_ref[j : j + 1, :] = send_ref[level : level + 1, LANES * j : LANES * (j + 1)]


def gather_outgoing(field_ref, flag_ref, index_ref, out_ref, inverse_ref=None, pick_ref=None):
    count = index_ref.shape[0]

    def body(step, carry):
        found = pick_fields(
            lane_blocks(field_ref), index_ref[pl.ds(step, 1), :], jnp.zeros((8, LANES), F32)
        )
        out_ref[pl.ds(aligned(step * 8), 8), :] = found
        return carry

    lax.fori_loop(0, count, body, 0, unroll=True)
    zero = jnp.zeros((8, LANES), F32)
    for part in range(count // 8):
        rows = slice(8 * part, 8 * part + 8)
        refs = [flag_ref] if inverse_ref is None else [flag_ref, inverse_ref]
        found = pick_rows(refs, index_ref[rows, :], [zero] * len(refs))
        first = 8 * count + 8 * part
        out_ref[first : first + 8, :] = jnp.abs(found[0])
        out_ref[first + count : first + count + 8, :] = jnp.where(found[0] > 0, 1.0, 0.0)
        if pick_ref is not None:
            pick_ref[rows, :] = found[1].astype(I32)


def apply_incoming(field_ref, flag_ref, inverse_ref, in_ref, new_field_ref, new_flag_ref, flag_in_ref):
    tile_rows = flag_ref.shape[0]
    count = flag_in_ref.shape[0]
    base = 8 * count
    density_in = in_ref[base : base + count, :]
    flag_in_ref[...] = jnp.where(in_ref[base + count : base + 2 * count, :] > 0.5, density_in, -density_in)

    def body(row, carry):
        where = pl.ds(aligned(row * LANES, LANES), LANES)
        slot = inverse_ref[pl.ds(row, 1), :].astype(I32) - 1
        new_field_ref[:, where] = pick_fields(row_blocks(in_ref, count), slot, field_ref[:, where])
        return carry

    lax.fori_loop(0, tile_rows, body, 0, unroll=16)
    for part in range(tile_rows // 8):
        rows = slice(8 * part, 8 * part + 8)
        slot = inverse_ref[rows, :].astype(I32) - 1
        new_flag_ref[rows, :] = pick_rows([flag_in_ref], slot, [flag_ref[rows, :]])[0]


def first_kernel(particle_ref, flag_ref, send_in_ref, field_ref, out_ref, send_ref, index_ref):
    stage_index(send_in_ref, 0, index_ref)
    gather_outgoing(particle_ref, flag_ref, index_ref, out_ref)
    field_ref[...] = particle_ref[...]
    send_ref[...] = send_in_ref[...]


def inverse_kernel(count_ref, send_ref, *inverse_refs):
    slots = send_ref.shape[1]
    slot = iota((1, slots), 1)
    for level, inverse_ref in enumerate(inverse_refs):
        tile_rows = inverse_ref.shape[0]
        rows = send_ref[level : level + 1, :]
        taken = slot < count_ref[level]
        high = jnp.where(taken, rows >> 7, -1)
        low = rows & 127
        number = slot + 1
        hit = spread(high, tile_rows) == iota((tile_rows, slots), 0)
        coarse = jnp.where(hit, spread((number >> 6).astype(F32), tile_rows), 0.0)
        fine = jnp.where(hit, spread((number & 63).astype(F32), tile_rows), 0.0)
        left = jnp.concatenate([coarse, fine], axis=0).astype(jnp.bfloat16)
        right = jnp.where(spread(low, LANES) == iota((LANES, slots), 0), 1.0, 0.0).astype(jnp.bfloat16)
        both = lax.dot_general(left, right, (((1,), (1,)), ((), ())), preferred_element_type=F32)
        inverse_ref[...] = both[:tile_rows] * 64.0 + both[tile_rows:]


EARLY = 16


def ahead_first_kernel(field_ref, flag_ref, inverse_ref, send_ref, last_ref, export_ref, partial_ref, pick_ref, export_index_ref, export_pick_ref, index_ref):
    stage_index(send_ref, 1, index_ref)
    gather_outgoing(field_ref, flag_ref, index_ref, partial_ref, inverse_ref, pick_ref)
    blocks = export_ref.shape[1] // LANES
    for number in range(8):
        for block in range(blocks):
            at = number * blocks + block
            export_index_ref[at : at + 1, :] = export_ref[number : number + 1, LANES * block : LANES * (block + 1)]
    zero = jnp.zeros((8, LANES), F32)
    for part in range(blocks):
        rows = slice(8 * part, 8 * part + 8)
        export_pick_ref[rows, :] = pick_rows([last_ref], export_index_ref[rows, :], [zero])[0].astype(I32)


def ahead_kernel(level, field_ref, flag_ref, before_ref, in_ref, inverse_ref, send_ref, new_field_ref, new_flag_ref, partial_ref, pick_ref, index_ref, flag_in_ref):
    apply_incoming(field_ref, flag_ref, before_ref, in_ref, new_field_ref, new_flag_ref, flag_in_ref)
    stage_index(send_ref, level + 1, index_ref)
    gather_outgoing(new_field_ref, new_flag_ref, index_ref, partial_ref, inverse_ref, pick_ref)


def fix_kernel(partial_ref, pick_ref, in_ref, out_ref):
    count = pick_ref.shape[0]

    def body(step, carry):
        where = pl.ds(aligned(step * 8), 8)
        slot = pick_ref[pl.ds(step, 1), :] - 1
        out_ref[where, :] = pick_fields(row_blocks(in_ref, count), slot, partial_ref[where, :])
        return carry

    lax.fori_loop(0, count, body, 0, unroll=True)
    base = 8 * count
    for part in range(count // 8):
        slot = pick_ref[8 * part : 8 * part + 8, :] - 1
        tables = [in_ref.at[pl.ds(base, count)], in_ref.at[pl.ds(base + count, count)]]
        places = [slice(base + n * count + 8 * part, base + n * count + 8 * part + 8) for n in range(2)]
        found = pick_rows(tables, slot, [partial_ref[place, :] for place in places])
        for place, value in zip(places, found):
            out_ref[place, :] = value


def ahead_last_kernel(field_ref, flag_ref, inverse_ref, in_ref, index_ref, new_field_ref, new_flag_ref, early_ref, flag_in_ref):
    apply_incoming(field_ref, flag_ref, inverse_ref, in_ref, new_field_ref, new_flag_ref, flag_in_ref)
    gather_exports(new_field_ref, index_ref, 0, EARLY, early_ref, 0)


def gather_exports(field_ref, index_ref, first, count, out_ref, skip, in_ref=None, pick_ref=None):
    def body(step, carry):
        row = index_ref[pl.ds(first + step, 1), :]
        found = pick_fields(lane_blocks(field_ref), row, jnp.zeros((8, LANES), F32))
        if in_ref is not None:
            slot = pick_ref[pl.ds(first + step, 1), :] - 1
            found = pick_fields(row_blocks(in_ref, in_ref.shape[0] // 10), slot, found)
        out_ref[pl.ds(aligned((skip + step) * 8), 8), :] = found
        return carry

    lax.fori_loop(0, count, body, 0, unroll=8)


def last_kernel(field_ref, in_ref, index_ref, early_ref, pick_ref, low_ref, high_ref):
    blocks = index_ref.shape[0] // 8

    def body(step, carry):
        where = pl.ds(aligned(step * 8), 8)
        slot = pick_ref[pl.ds(step, 1), :] - 1
        low_ref[where, :] = pick_fields(row_blocks(in_ref, in_ref.shape[0] // 10), slot, early_ref[where, :])
        return carry

    lax.fori_loop(0, EARLY, body, 0, unroll=True)
    gather_exports(field_ref, index_ref, EARLY, 3 * blocks - EARLY, low_ref, EARLY, in_ref, pick_ref)
    gather_exports(field_ref, index_ref, 5 * blocks, 3 * blocks, high_ref, 0, in_ref, pick_ref)


EXPANDED = 8
NEAR_FIELDS = (0, 1, 2, 6)
SPEED_FIELDS = (3, 4, 5)
SLOPE_NORM = 0.375 * PARTICLE_MASS / math.pi


def derived(height):
    inverse = 1.0 / height
    square = inverse * inverse
    return inverse, SLOPE_NORM * (square * square)


def expand_targets(compact_ref, chunk, base, expanded_ref, fields=range(7), shift=0):
    groups = compact_ref.shape[0] // (4 * 32)
    region = (groups * 32 + 1) * 8
    half_base = jnp.where(iota((8, LANES), 1) < 64, 0, 64)
    for inner in range(8):
        for field in fields:
            index = half_base + (inner * 8 + field)
            for group in range(groups):
                for section in range(2):
                    for half in range(2):
                        place = ((group * 2 + section) * 2 + half) * 8
                        start = aligned(chunk * (groups * 32) + place)
                        tile = 2 * (group * 16 + section * 8 + inner) + half
                        value = lane_pick(compact_ref[pl.ds(start, 8), :], index)
                        first = base + (field - shift) * region + tile * 8
                        if field == 6:
                            inverse, norm = derived(value)
                            expanded_ref[pl.ds(aligned(first), 8), :] = inverse
                            expanded_ref[pl.ds(aligned(first + region), 8), :] = norm
                        else:
                            expanded_ref[pl.ds(aligned(first), 8), :] = value


def target_kernel(count_ref, old_field_ref, old_flag_ref, inverse_ref, in_ref, index_ref, pair_ref,
                  field_ref, flag_ref, middle_ref, compact_ref, rank_ref, order_ref, list_ref, length_ref, expanded_ref,
                  flag_in_ref, stack_ref):
    apply_incoming(old_field_ref, old_flag_ref, inverse_ref, in_ref, field_ref, flag_ref, flag_in_ref)
    blocks = index_ref.shape[0] // 8
    gather_exports(field_ref, index_ref, 3 * blocks, 2 * blocks, middle_ref, 0)
    tile_rows = flag_ref.shape[0]
    groups = tile_rows // 16
    tile_count = 2 * tile_rows
    region = (tile_count + 1) * 8
    active = flag_ref[...] > 0
    ones = jnp.where(active, 1.0, 0.0).astype(jnp.bfloat16)
    a = iota((LANES, LANES), 0)
    b = iota((LANES, LANES), 1)
    same = (a >> 6) == (b >> 6)
    before = jnp.where(same & (a < b), 1.0, 0.0).astype(jnp.bfloat16)
    whole = jnp.where(same, 1.0, 0.0).astype(jnp.bfloat16)
    rank = jnp.dot(ones, before, preferred_element_type=F32).astype(I32)
    total = jnp.dot(ones, whole, preferred_element_type=F32)
    rank_ref[...] = rank
    lane = iota((tile_rows, LANES), 1)
    code = jnp.where(active, lane + 128 * ((lane & 63) - rank), -1)
    for bit in range(6):
        moved = pltpu.roll(code, LANES - (1 << bit), 1)
        take = (moved >= 0) & (((moved >> (7 + bit)) & 1) == 1)
        keep = (code >= 0) & (((code >> (7 + bit)) & 1) == 0)
        code = jnp.where(take, moved, jnp.where(keep, code, -1))
    order_ref[...] = jnp.where(code >= 0, code & 127, lane)
    left_half = iota((8, LANES), 1) < 64
    for group in range(groups):
        for inner in range(16):
            row = group * 16 + inner
            stack_ref[8 * inner : 8 * inner + 8, :] = lane_pick(
                field_ref[:, LANES * row : LANES * (row + 1)], spread(order_ref[row : row + 1, :])
            )
        turned = jnp.transpose(stack_ref[...])
        for half in range(2):
            for chunk in range(4):
                first = half * 64 + chunk * 16
                near, far = turned[first : first + 8], turned[first + 8 : first + 16]
                for section in range(2):
                    if section == 0:
                        mixed = jnp.where(left_half, near, pltpu.roll(far, 64, 1))
                    else:
                        mixed = jnp.where(left_half, pltpu.roll(near, 64, 1), far)
                    place = (((chunk * groups + group) * 2 + section) * 2 + half) * 8
                    compact_ref[place : place + 8, :] = mixed

    pairs = pair_ref.shape[1]
    slots = list_ref.shape[1]
    target, source = pair_ref[0:1, :], pair_ref[1:2, :]
    folded = jnp.where((lane & 63) == iota((tile_rows, LANES), 0), total, 0.0)
    totals = spread(jnp.sum(folded, axis=0, keepdims=True))
    place = spread((target & 1) * 64 + (target >> 1))
    need = jnp.concatenate(
        [lane_pick(totals, place[:, LANES * q : LANES * (q + 1)]) for q in range(pairs // LANES)], axis=1
    )
    sub = iota((8, pairs), 0)
    is_ghost = spread(source) >= tile_count
    member = (
        (iota((8, pairs), 1) < count_ref[0])
        & (need > (16 * (sub & 3)).astype(F32))
        & (is_ghost == (sub >= 4))
    )
    member_value = jnp.where(member, 1.0, 0.0)
    earlier = jnp.where(iota((pairs, pairs), 0) < iota((pairs, pairs), 1), 1.0, 0.0).astype(jnp.bfloat16)
    position = jnp.dot(member_value.astype(jnp.bfloat16), earlier, preferred_element_type=F32).astype(I32)
    length = jnp.broadcast_to(jnp.sum(member_value, axis=1, keepdims=True), (8, LANES)).astype(I32)
    length_ref[...] = length
    own_steps = ((length + (UNROLL - 1)) // UNROLL) * UNROLL
    base = jnp.where(iota((8, LANES), 0) >= 4, pltpu.roll(own_steps, 4, 0), 0)
    position = position + jnp.concatenate([base] * (pairs // LANES), axis=1)
    position = jnp.where(member, position, -1)
    local = jnp.where(source >= tile_count, source - tile_count, source)
    values = jnp.where(
        sub == 0, spread(target + 1), jnp.where(sub == 1, spread(local + 1), 0)
    ).astype(F32).astype(jnp.bfloat16)

    def make_list(chunk):
        row = jnp.maximum(position[chunk : chunk + 1, :], position[chunk + 4 : chunk + 5, :])
        hit = jnp.where(spread(row, slots) == iota((slots, pairs), 0), 1.0, 0.0).astype(jnp.bfloat16)
        found = lax.dot_general(
            values, hit, (((1,), (1,)), ((), ())), preferred_element_type=F32
        ).astype(I32)
        list_ref[chunk : chunk + 1, :] = jnp.where(found[0:1] > 0, found[0:1] - 1, tile_count) * 8
        list_ref[4 + chunk : 5 + chunk, :] = jnp.maximum(found[1:2] - 1, 0) * 8

    make_list(0)
    make_list(1)

    @pl.when(jnp.max(total) > 32.0)
    def _():
        make_list(2)
        make_list(3)

    def one_chunk(chunk, carry):
        expand_targets(compact_ref, chunk, aligned(chunk * (EXPANDED * region)), expanded_ref, NEAR_FIELDS)
        return carry

    lax.fori_loop(0, 2, one_chunk, 0)


def reduce_targets(sum_ref, first, tile_count, section, out_ref):
    blocks = tile_count // 16
    for block in range(blocks):
        start = first + block * LANES
        turned = jnp.transpose(sum_ref[start : start + LANES, :])
        for half in range(2):
            total = jnp.sum(turned[64 * half : 64 * half + 64], axis=0, keepdims=True)
            out_ref[pl.ds((section * 2 + half) * blocks + block, 1), :] = total


def place_results(red_ref, blocks, part, rank):
    row = iota((8, LANES), 0)
    half = iota((8, LANES), 1) >> 6
    index = (2 * row + half) * 8 + (rank & 7)
    which = rank >> 3
    found = jnp.zeros((8, LANES), F32)
    for section in range(8):
        table = spread(red_ref[section * blocks + part : section * blocks + part + 1, :])
        found = jnp.where(which == section, lane_pick(table, index), found)
    return found


def clear(sum_ref, first, rows):
    for at in range(0, rows, 8):
        sum_ref[first + at : first + at + 8, :] = jnp.zeros((8, LANES), F32)


def steps_of(length):
    return (length + (UNROLL - 1)) // UNROLL


def span(length_ref, chunk, ghost):
    own = steps_of(length_ref[chunk, 0])
    if not ghost:
        return 0, own
    return own, own + steps_of(length_ref[chunk + 4, 0])


def double_into(pool_ref, row, value):
    left = iota((8, LANES), 1) < 64
    other = pltpu.roll(value, 64, 1)
    pool_ref[16 * row : 16 * row + 8, :] = jnp.where(left, value, other)
    pool_ref[16 * row + 8 : 16 * row + 16, :] = jnp.where(left, other, value)


def density_pairs(list_ref, length_ref, chunk, ghost, expanded_ref, base, region, pool_ref, sum_ref, sum_base):
    def step(number, carry):
        results = []
        for u in range(UNROLL):
            target = list_ref[chunk, number * UNROLL + u]
            source = list_ref[chunk + 4, number * UNROLL + u]

            def at(field, target=target):
                return expanded_ref[pl.ds(aligned(target + (base + field * region)), 8), :]

            square = None
            for axis in range(3):
                gap = at(axis) - pool_ref[pl.ds(source + axis, 8, stride=0), :]
                gap = gap - jnp.floor(gap + 0.5)
                square = gap * gap if square is None else square + gap * gap
            safe = jnp.maximum(square, 1.2e-38)
            ratio = safe * lax.rsqrt(safe) * at(6)
            outer = jnp.maximum(2.0 - ratio, 0.0)
            inner = jnp.maximum(1.0 - ratio, 0.0)
            results.append((target, 0.25 * (outer * outer * outer) - inner * inner * inner))
        for target, value in results:
            sum_ref[pl.ds(aligned(target + sum_base), 8), :] += value
        return carry

    first, last = span(length_ref, chunk, ghost)
    lax.fori_loop(first, last, step, 0)


def density_own_kernel(list_ref, length_ref, field_ref, expanded_ref, compact_ref, pool_ref, sum_ref, speed_ref):
    tile_rows = field_ref.shape[1] // LANES
    region = (2 * tile_rows + 1) * 8
    for row in range(tile_rows):
        double_into(pool_ref, row, field_ref[:, LANES * row : LANES * (row + 1)])
    clear(sum_ref, 0, 2 * region)
    for chunk in range(2):
        density_pairs(
            list_ref, length_ref, chunk, False, expanded_ref, chunk * EXPANDED * region, region,
            pool_ref, sum_ref, chunk * region,
        )

    def one_chunk(chunk, carry):
        expand_targets(compact_ref, chunk, aligned(chunk * (3 * region)), speed_ref, SPEED_FIELDS, 3)
        return carry

    lax.fori_loop(0, 2, one_chunk, 0)


def density_kernel(list_ref, length_ref, compact_ref, expanded_ref, own_pool_ref, own_sum_ref, rank_ref, field_ref, flag_ref, low_ref, high_ref, down_ref, up_ref, export_ref,
                   density_ref, low_out, middle_out, high_out, pool_ref, sum_ref, result_ref,
                   red_ref, height_ref, spare_ref):
    tile_rows = flag_ref.shape[0]
    tile_count = 2 * tile_rows
    region = (tile_count + 1) * 8
    ghosts = (low_ref, high_ref, down_ref, up_ref)
    unit = low_ref.shape[0] // 3
    blocks = unit // 8
    for number, (which, start) in enumerate(ghost_place(unit)):
        for block in range(blocks):
            first = start + 8 * block
            double_into(pool_ref, number * blocks + block, ghosts[which][first : first + 8, :])
    for chunk in range(2):
        density_pairs(
            list_ref, length_ref, chunk, True, expanded_ref, chunk * EXPANDED * region, region,
            pool_ref, sum_ref, chunk * region,
        )
        reduce_targets(sum_ref, chunk * region, tile_count, chunk, red_ref)
    for row in range(4 * (tile_count // 16), 8 * (tile_count // 16), 8):
        red_ref[row : row + 8, :] = jnp.zeros((8, LANES), F32)

    def rare_chunk(chunk, carry):
        @pl.when(length_ref[chunk, 0] + length_ref[chunk + 4, 0] > 0)
        def _():
            expand_targets(compact_ref, chunk, 0, spare_ref)
            clear(sum_ref, 0, region)
            density_pairs(list_ref, length_ref, chunk, False, spare_ref, 0, region, own_pool_ref, sum_ref, 0)
            density_pairs(list_ref, length_ref, chunk, True, spare_ref, 0, region, pool_ref, sum_ref, 0)
            reduce_targets(sum_ref, 0, tile_count, chunk, red_ref)

        return carry

    lax.fori_loop(2, 4, rare_chunk, 0)
    for row in range(tile_rows):
        height_ref[row : row + 1, :] = field_ref[6:7, LANES * row : LANES * (row + 1)]
    for part in range(tile_rows // 8):
        rows = slice(8 * part, 8 * part + 8)
        found = place_results(red_ref, tile_count // 16, part, rank_ref[rows, :])
        height = height_ref[rows, :]
        flag = flag_ref[rows, :]
        norm = PARTICLE_MASS / (math.pi * height * height * height)
        density_ref[rows, :] = jnp.where(flag > 0, norm * (1.0 + found), jnp.abs(flag))
        result_ref[rows, :] = density_ref[rows, :]
    outs = (low_out, middle_out, high_out)
    zero = jnp.zeros((8, LANES), F32)
    for block in range(blocks):
        index = export_ref[:, LANES * block : LANES * (block + 1)]
        found = pick_rows([density_ref], index, [zero])[0]
        for number, (which, start) in enumerate(export_place(blocks)):
            outs[which][start + block : start + block + 1, :] = found[number : number + 1, :]


def source_tables(pool_ref, tile, first_ref, second_ref, density=None):
    sub = iota((8, LANES), 0)
    rows = slice(8 * tile, 8 * tile + 8)
    value = pool_ref[rows, :]
    inverse, norm = derived(value)
    press = (ADIABATIC - 1.0) * value
    if density is not None:
        press = press / density
    first_ref[rows, :] = jnp.where(sub == 7, press, jnp.where(sub == 6, inverse, value))
    second_ref[rows, :] = norm


def doubled_halves(row):
    left = iota((8, LANES), 1) < 64
    wide = spread(row)
    other = pltpu.roll(wide, 64, 1)
    return jnp.where(left, wide, other), jnp.where(left, other, wide)


def force_pairs(list_ref, length_ref, chunk, ghost, expanded_ref, base, speed_ref, speed_base, region, press_ref, press_base, first_ref, second_ref, sum_ref):
    def step(number, carry):
        results = []
        for u in range(UNROLL):
            target = list_ref[chunk, number * UNROLL + u]
            source = list_ref[chunk + 4, number * UNROLL + u]

            def at(field, target=target):
                return expanded_ref[pl.ds(aligned(target + (base + field * region)), 8), :]

            def speed(axis, target=target):
                return speed_ref[pl.ds(aligned(target + (speed_base + axis * region)), 8), :]

            def source_row(field, source=source):
                return first_ref[pl.ds(source + field, 8, stride=0), :]

            def source_more(field, source=source):
                return second_ref[pl.ds(source + field, 8, stride=0), :]

            gaps = []
            square = None
            approach = None
            for axis in range(3):
                gap = at(axis) - source_row(axis)
                gap = gap - jnp.floor(gap + 0.5)
                gaps.append(gap)
                square = gap * gap if square is None else square + gap * gap
                part = (speed(axis) - source_row(3 + axis)) * gap
                approach = part if approach is None else approach + part
            safe = jnp.maximum(square, 1.2e-38)
            inverse_distance = lax.rsqrt(safe)
            distance = safe * inverse_distance

            def slope(inverse_height, norm):
                ratio = distance * inverse_height
                outer = 2.0 - ratio
                inner = jnp.maximum(outer - ratio, 0.0)
                outer = jnp.maximum(outer, 0.0)
                return norm * (inner * inner - outer * outer)

            total = slope(at(6), at(7)) + slope(source_row(6), source_more(6))
            press = press_ref[pl.ds(aligned(target + press_base), 8), :] + source_row(7)
            weight = press * (total * inverse_distance)
            results.append((target, [weight * gap for gap in gaps] + [weight * approach]))
        for target, values in results:
            for quantity in range(4):
                sum_ref[pl.ds(aligned(target + quantity * region), 8), :] += values[quantity]
        return carry

    first, last = span(length_ref, chunk, ghost)
    lax.fori_loop(first, last, step, 0)


def expand_press(press_compact_ref, chunk, tile_rows, press_ref, base):
    half_base = jnp.where(iota((8, LANES), 1) < 64, 0, 64)
    for row in range(tile_rows):
        for half in range(2):
            start = aligned(chunk * 16 + half * 8)
            first = base + (2 * row + half) * 8
            press_ref[first : first + 8, :] = lane_pick(
                press_compact_ref[pl.ds(start, 8), :], half_base + row
            )


def force_own_kernel(list_ref, length_ref, density_ref, field_ref, order_ref, expanded_ref, speed_ref, pool_ref,
                     first_ref, second_ref, press_compact_ref, press_ref, sum_ref,
                     energy_ref, ordered_ref):
    tile_rows = density_ref.shape[0]
    tile_count = 2 * tile_rows
    region = (tile_count + 1) * 8
    left = iota((8, LANES), 1) < 64
    for row in range(tile_rows):
        near, far = doubled_halves(density_ref[row : row + 1, :])
        source_tables(pool_ref, 2 * row, first_ref, second_ref, near)
        source_tables(pool_ref, 2 * row + 1, first_ref, second_ref, far)
        energy_ref[row : row + 1, :] = field_ref[7:8, LANES * row : LANES * (row + 1)]
    for part in range(tile_rows // 8):
        rows = slice(8 * part, 8 * part + 8)
        press = (ADIABATIC - 1.0) * energy_ref[rows, :] / density_ref[rows, :]
        ordered_ref[rows, :] = lane_pick(press, order_ref[rows, :])
    ordered_ref[tile_rows:, :] = jnp.zeros((LANES - tile_rows, LANES), F32)
    turned = jnp.transpose(ordered_ref[...])
    for half in range(2):
        for chunk in range(4):
            first = half * 64 + chunk * 16
            near, far = turned[first : first + 8], turned[first + 8 : first + 16]
            place_at = (chunk * 2 + half) * 8
            press_compact_ref[place_at : place_at + 8, :] = jnp.where(left, near, pltpu.roll(far, 64, 1))
    for chunk in range(2):
        expand_press(press_compact_ref, chunk, tile_rows, press_ref, chunk * region)
    clear(sum_ref, 0, 4 * region)
    force_pairs(
        list_ref, length_ref, 0, False, expanded_ref, 0, speed_ref, 0, region, press_ref, 0, first_ref, second_ref, sum_ref,
    )


def force_own_more_kernel(list_ref, length_ref, expanded_ref, speed_ref, press_ref, own_first_ref, own_second_ref, pool_ref,
                          sum_ref, first_ref, second_ref):
    region = sum_ref.shape[0] // 4
    for tile in range(pool_ref.shape[0] // 8):
        source_tables(pool_ref, tile, first_ref, second_ref)
    clear(sum_ref, 0, 4 * region)
    force_pairs(
        list_ref, length_ref, 1, False, expanded_ref, EXPANDED * region, speed_ref, 3 * region, region, press_ref, region,
        own_first_ref, own_second_ref, sum_ref,
    )


def force_kernel(list_ref, length_ref, compact_ref, expanded_ref, speed_ref, press_compact_ref, press_ref, rank_ref, flag_ref, own_first_ref, own_second_ref, half_ref, second_ref, zero_sum_ref, one_sum_ref, low_ref, high_ref, down_ref, up_ref,
                 accel_ref, heat_ref, first_sum_ref, second_sum_ref,
                 first_ref, sum_ref, red_ref, spare_ref, spare_press_ref):
    tile_rows = flag_ref.shape[0]
    tile_count = 2 * tile_rows
    region = (tile_count + 1) * 8
    blocks = tile_count // 16
    is_press = iota((8, LANES), 0) == 7
    ghosts = (low_ref, high_ref, down_ref, up_ref)
    unit = low_ref.shape[0] // 3
    for number, (which, start) in enumerate(ghost_place(unit)):
        for block in range(unit):
            row = number * unit + block
            for half, density in enumerate(doubled_halves(ghosts[which][start + block : start + block + 1, :])):
                rows = slice(16 * row + 8 * half, 16 * row + 8 * half + 8)
                value = half_ref[rows, :]
                first_ref[rows, :] = jnp.where(is_press, value / density, value)
    for chunk in range(2):
        chunk_sum_ref = first_sum_ref if chunk == 0 else second_sum_ref
        force_pairs(
            list_ref, length_ref, chunk, True, expanded_ref, chunk * EXPANDED * region,
            speed_ref, chunk * 3 * region, region,
            press_ref, chunk * region, first_ref, second_ref, chunk_sum_ref,
        )
        for quantity in range(4):
            reduce_targets(chunk_sum_ref, quantity * region, tile_count, chunk + 4 * quantity, red_ref)
    for quantity in range(4):
        for row in range(4 * blocks, 8 * blocks, 8):
            at = quantity * 8 * blocks + row
            red_ref[at : at + 8, :] = jnp.zeros((8, LANES), F32)

    def rare_chunk(chunk, carry):
        @pl.when(length_ref[chunk, 0] + length_ref[chunk + 4, 0] > 0)
        def _():
            expand_targets(compact_ref, chunk, 0, spare_ref)
            expand_press(press_compact_ref, chunk, tile_rows, spare_press_ref, 0)
            clear(sum_ref, 0, 4 * region)
            force_pairs(
                list_ref, length_ref, chunk, False, spare_ref, 0, spare_ref, 3 * region, region, spare_press_ref, 0,
                own_first_ref, own_second_ref, sum_ref,
            )
            force_pairs(
                list_ref, length_ref, chunk, True, spare_ref, 0, spare_ref, 3 * region, region, spare_press_ref, 0,
                first_ref, second_ref, sum_ref,
            )
            for quantity in range(4):
                reduce_targets(sum_ref, quantity * region, tile_count, chunk + 4 * quantity, red_ref)

        return carry

    lax.fori_loop(2, 4, rare_chunk, 0)
    for part in range(tile_rows // 8):
        rank = rank_ref[8 * part : 8 * part + 8, :]
        flag = flag_ref[8 * part : 8 * part + 8, :]
        for quantity in range(4):
            found = place_results(red_ref.at[pl.ds(quantity * 8 * blocks, 8 * blocks)], blocks, part, rank)
            if quantity == 3:
                heat_ref[8 * part : 8 * part + 8, :] = jnp.where(flag > 0, 0.5 * found, 0.0)
            else:
                found = jnp.where(flag > 0, -found, 0.0)
                for row in range(8):
                    at = LANES * (8 * part + row)
                    accel_ref[quantity : quantity + 1, at : at + LANES] = found[row : row + 1, :]


def call(kernel, outs, scratch, operands, scalars=0, aliases=None):
    smem = pl.BlockSpec(memory_space=pltpu.SMEM)
    vmem = pl.BlockSpec(memory_space=pltpu.VMEM)
    return pl.pallas_call(
        kernel,
        out_shape=[jax.ShapeDtypeStruct(shape, dtype) for shape, dtype in outs],
        in_specs=[smem if i < scalars else vmem for i in range(len(operands))],
        out_specs=[vmem] * len(outs),
        scratch_shapes=[pltpu.VMEM(shape, dtype) for shape, dtype in scratch],
        input_output_aliases=aliases or {},
        compiler_params=pltpu.CompilerParams(vmem_limit_bytes=24 * 2**20),
    )(*operands)


def on_device(
    particles, old_density, active, send_rows, send_count, export_rows, pair_tiles, pair_count
):
    row_count = particles.shape[1]
    levels, slots = send_rows.shape
    ghosts = export_rows.shape[1]
    pair_total = pair_tiles.shape[1]
    tile_rows = row_count // LANES
    tile_count = 2 * tile_rows
    in_blocks = slots // LANES
    unit = 8 * (ghosts // LANES)
    dense_unit = ghosts // LANES
    region = (tile_count + 1) * 8
    list_slots = -(-(pair_total + 2 * UNROLL) // LANES) * LANES
    bits_x = lax.axis_size("gx").bit_length() - 1
    bits_y = lax.axis_size("gy").bit_length() - 1

    row = ((tile_rows, LANES), F32)
    whole = ((8, row_count), F32)
    offered = ((10 * in_blocks, LANES), F32)
    picked = ((in_blocks, LANES), I32)
    index_scratch = ((in_blocks, LANES), I32)
    flag_scratch = ((in_blocks, LANES), F32)
    exported = [((3 * unit, LANES), F32), ((2 * unit, LANES), F32), ((3 * unit, LANES), F32)]

    def swap(block, level):
        if level < 2:
            return from_partner(block, "gx", bits_x - 1 - level)
        return from_partner(block, "gy", bits_y + 1 - level)

    flag = jnp.where(active == 1, old_density, -old_density).reshape(tile_rows, LANES)
    fields, outgoing, send_rows = call(
        first_kernel,
        [whole, offered, (send_rows.shape, I32)],
        [index_scratch],
        [particles, flag, send_rows],
    )
    incoming = swap(outgoing, 0)
    inverse = call(inverse_kernel, [row] * levels, [], [send_count[:, 0], send_rows], scalars=1)
    export_rows_shape = ((8 * dense_unit, LANES), I32)
    partial, pick, export_index, export_pick = call(
        ahead_first_kernel,
        [offered, picked, export_rows_shape, export_rows_shape],
        [index_scratch],
        [fields, flag, inverse[0], send_rows, inverse[3], export_rows],
    )
    (outgoing,) = call(fix_kernel, [offered], [], [partial, pick, incoming])
    before = incoming
    incoming = swap(outgoing, 1)
    ahead = [whole, row, offered, picked]
    ahead_scratch = [index_scratch, flag_scratch]
    fields, flag, partial, pick = call(
        lambda *refs: ahead_kernel(1, *refs),
        ahead,
        ahead_scratch,
        [fields, flag, inverse[0], before, inverse[1], send_rows],
    )
    (outgoing,) = call(fix_kernel, [offered], [], [partial, pick, incoming])
    before = incoming
    incoming = swap(outgoing, 2)
    fields, flag, partial, pick = call(
        lambda *refs: ahead_kernel(2, *refs),
        ahead,
        ahead_scratch,
        [fields, flag, inverse[1], before, inverse[2], send_rows],
    )
    (outgoing,) = call(fix_kernel, [offered], [], [partial, pick, incoming])
    before = incoming
    incoming = swap(outgoing, 3)
    fields, flag, early = call(
        ahead_last_kernel,
        [whole, row, ((8 * EARLY, LANES), F32)],
        [flag_scratch],
        [fields, flag, inverse[2], before, export_index],
    )
    low, high = call(
        last_kernel,
        [exported[0], exported[2]],
        [],
        [fields, incoming, export_index, early, export_pick],
    )
    low, high = along_x(low, high)
    fields, flag, middle, compact, rank, order, lists, lengths, expanded = call(
        target_kernel,
        [
            whole,
            row,
            exported[1],
            ((8 * tile_rows, LANES), F32),
            ((tile_rows, LANES), I32),
            ((tile_rows, LANES), I32),
            ((8, list_slots), I32),
            ((8, LANES), I32),
            ((2 * EXPANDED * region, LANES), F32),
        ],
        [flag_scratch, ((LANES, LANES), F32)],
        [pair_count, fields, flag, inverse[3], incoming, export_index, pair_tiles],
        scalars=1,
    )
    low, high, lengths = lax.optimization_barrier((low, high, lengths))
    down, up = along_y(low, middle, high, unit)
    pool_shape = ((tile_count * 8, LANES), F32)
    ghost_pool_shape = ((2 * 8 * dense_unit * 8, LANES), F32)
    own_pool, own_sum, speed = call(
        density_own_kernel,
        [pool_shape, ((2 * region, LANES), F32), ((6 * region, LANES), F32)],
        [],
        [lists, lengths, fields, expanded, compact],
        scalars=2,
    )
    density, low_d, middle_d, high_d, ghost_pool, _, density_out = call(
        density_kernel,
        [
            row,
            ((3 * dense_unit, LANES), F32),
            ((2 * dense_unit, LANES), F32),
            ((3 * dense_unit, LANES), F32),
            ghost_pool_shape,
            ((2 * region, LANES), F32),
            row,
        ],
        [
            ((8 * (tile_count // 16), LANES), F32),
            row,
            ((EXPANDED * region, LANES), F32),
        ],
        [
            lists, lengths, compact, expanded, own_pool, own_sum,
            rank, fields, flag, low, high, down, up, export_rows,
        ],
        scalars=2,
        aliases={5: 5},
    )
    low_d, high_d = along_x(low_d, high_d)
    sums = ((4 * region, LANES), F32)
    own_first, own_second, press_compact, press, zero_sum = call(
        force_own_kernel,
        [pool_shape, pool_shape, ((64, LANES), F32), ((2 * region, LANES), F32), sums],
        [row, ((LANES, LANES), F32)],
        [lists, lengths, density, fields, order, expanded, speed, own_pool],
        scalars=2,
    )
    low_d, high_d, press = lax.optimization_barrier((low_d, high_d, press))
    down_d, up_d = along_y(low_d, middle_d, high_d, dense_unit)
    one_sum, ghost_first, ghost_second = call(
        force_own_more_kernel,
        [sums, ghost_pool_shape, ghost_pool_shape],
        [],
        [lists, lengths, expanded, speed, press, own_first, own_second, ghost_pool],
        scalars=2,
    )
    accel, heat, _, _ = call(
        force_kernel,
        [((3, row_count), F32), row, sums, sums],
        [
            ghost_pool_shape,
            sums,
            ((32 * (tile_count // 16), LANES), F32),
            ((EXPANDED * region, LANES), F32),
            ((region, LANES), F32),
        ],
        [
            lists, lengths, compact, expanded, speed, press_compact, press, rank, flag,
            own_first, own_second, ghost_first, ghost_second, zero_sum, one_sum,
            low_d, high_d, down_d, up_d,
        ],
        scalars=2,
        aliases={13: 2, 14: 3},
    )
    return (density_out.reshape(row_count), accel, heat.reshape(row_count))


def solution(mesh):
    in_specs = (
        P(None, ("gx", "gy")),
        P(("gx", "gy")),
        P(("gx", "gy")),
        P(None, ("gx", "gy")),
        P(None, ("gx", "gy")),
        P(None, ("gx", "gy")),
        P(None, ("gx", "gy")),
        P(("gx", "gy")),
    )
    out_specs = (P(("gx", "gy")), P(None, ("gx", "gy")), P(("gx", "gy")))
    return jax.shard_map(
        on_device, mesh=mesh, in_specs=in_specs, out_specs=out_specs, check_vma=False
    )
```

```python
import math

import jax
import jax.numpy as jnp
from jax import lax
from jax.experimental import pallas as pl
from jax.experimental.pallas import tpu as pltpu
from jax.sharding import PartitionSpec as P

TILE = 64
LANES = 128
UNROLL = 8

PARTICLE_MASS = 1.0 / 512.0
ADIABATIC = 5.0 / 3.0
F32 = jnp.float32
I32 = jnp.int32


def from_behind(value, axis, steps):
    count = lax.axis_size(axis)
    pairs = [(source, (source + steps) % count) for source in range(count)]
    return lax.ppermute(value, axis, pairs)


def from_partner(block, axis, bit):
    count = lax.axis_size(axis)
    route = []
    for low in range(count):
        high = low | 1 << bit
        if high != low and high < count:
            route += [(low, high), (high, low)]
    return lax.ppermute(block, axis, route)


def along_x(low, high):
    count = lax.axis_size("gx")
    if count % 2:
        return from_behind(low, "gx", -1), from_behind(high, "gx", 1)
    even = lax.axis_index("gx") % 2 == 0
    first = [(i, i ^ 1) for i in range(count)]
    second = [(i, (i + 1) % count if i % 2 else (i - 1) % count) for i in range(count)]
    after = lax.ppermute(jnp.where(even, high, low), "gx", first)
    before = lax.ppermute(jnp.where(even, low, high), "gx", second)
    return jnp.where(even, after, before), jnp.where(even, before, after)


def along_y(low, middle, high, unit):
    down = jnp.concatenate([low[:unit], middle[:unit], high[:unit]], axis=0)
    up = jnp.concatenate([low[2 * unit :], middle[unit:], high[2 * unit :]], axis=0)
    return from_behind(down, "gy", -1), from_behind(up, "gy", 1)


def ghost_place(unit):
    return ((2, 0), (0, unit), (3, 0), (2, unit), (3, unit), (2, 2 * unit), (1, unit), (3, 2 * unit))


def export_place(unit):
    return ((0, 0), (0, unit), (0, 2 * unit), (1, 0), (1, unit), (2, 0), (2, unit), (2, 2 * unit))


def lane_pick(table, index):
    return jnp.take_along_axis(table, index, axis=1, mode="promise_in_bounds")


def spread(row, rows=8):
    return jnp.broadcast_to(row, (rows, row.shape[1]))


def iota(shape, axis):
    return lax.broadcasted_iota(I32, shape, axis)


def aligned(value, size=8):
    return pl.multiple_of(value, size)


def pick_fields(tables, row, start):
    high, low = spread(row >> 7), spread(row & 127)
    found = start
    for block, table in enumerate(tables):
        found = jnp.where(high == block, lane_pick(table, low), found)
    return found


def pick_rows(table_refs, index, starts):
    high, low = index >> 7, index & 127
    found = list(starts)
    for block in range(table_refs[0].shape[0]):
        here = high == block
        for n, ref in enumerate(table_refs):
            found[n] = jnp.where(here, lane_pick(spread(ref[block : block + 1, :]), low), found[n])
    return found


def lane_blocks(ref):
    return [ref[:, LANES * b : LANES * (b + 1)] for b in range(ref.shape[1] // LANES)]


def row_blocks(ref, count):
    return [ref[8 * b : 8 * b + 8, :] for b in range(count)]


def stage_index(send_ref, level, index_ref):
    for j in range(index_ref.shape[0]):
        index_ref[j : j + 1, :] = send_ref[level : level + 1, LANES * j : LANES * (j + 1)]


def gather_outgoing(field_ref, flag_ref, index_ref, out_ref, inverse_ref=None, pick_ref=None):
    count = index_ref.shape[0]

    def body(step, carry):
        found = pick_fields(
            lane_blocks(field_ref), index_ref[pl.ds(step, 1), :], jnp.zeros((8, LANES), F32)
        )
        out_ref[pl.ds(aligned(step * 8), 8), :] = found
        return carry

    lax.fori_loop(0, count, body, 0, unroll=True)
    zero = jnp.zeros((8, LANES), F32)
    for part in range(count // 8):
        rows = slice(8 * part, 8 * part + 8)
        refs = [flag_ref] if inverse_ref is None else [flag_ref, inverse_ref]
        found = pick_rows(refs, index_ref[rows, :], [zero] * len(refs))
        first = 8 * count + 8 * part
        out_ref[first : first + 8, :] = jnp.abs(found[0])
        out_ref[first + count : first + count + 8, :] = jnp.where(found[0] > 0, 1.0, 0.0)
        if pick_ref is not None:
            pick_ref[rows, :] = found[1].astype(I32)


def apply_incoming(field_ref, flag_ref, inverse_ref, in_ref, new_field_ref, new_flag_ref, flag_in_ref):
    tile_rows = flag_ref.shape[0]
    count = flag_in_ref.shape[0]
    base = 8 * count
    density_in = in_ref[base : base + count, :]
    flag_in_ref[...] = jnp.where(in_ref[base + count : base + 2 * count, :] > 0.5, density_in, -density_in)

    def body(row, carry):
        where = pl.ds(aligned(row * LANES, LANES), LANES)
        slot = inverse_ref[pl.ds(row, 1), :].astype(I32) - 1
        new_field_ref[:, where] = pick_fields(row_blocks(in_ref, count), slot, field_ref[:, where])
        return carry

    lax.fori_loop(0, tile_rows, body, 0, unroll=16)
    for part in range(tile_rows // 8):
        rows = slice(8 * part, 8 * part + 8)
        slot = inverse_ref[rows, :].astype(I32) - 1
        new_flag_ref[rows, :] = pick_rows([flag_in_ref], slot, [flag_ref[rows, :]])[0]


def first_kernel(particle_ref, flag_ref, send_in_ref, field_ref, out_ref, send_ref, index_ref):
    stage_index(send_in_ref, 0, index_ref)
    gather_outgoing(particle_ref, flag_ref, index_ref, out_ref)
    field_ref[...] = particle_ref[...]
    send_ref[...] = send_in_ref[...]


def inverse_kernel(count_ref, send_ref, *inverse_refs):
    slots = send_ref.shape[1]
    slot = iota((1, slots), 1)
    for level, inverse_ref in enumerate(inverse_refs):
        tile_rows = inverse_ref.shape[0]
        rows = send_ref[level : level + 1, :]
        taken = slot < count_ref[level]
        high = jnp.where(taken, rows >> 7, -1)
        low = rows & 127
        number = slot + 1
        hit = spread(high, tile_rows) == iota((tile_rows, slots), 0)
        coarse = jnp.where(hit, spread((number >> 6).astype(F32), tile_rows), 0.0)
        fine = jnp.where(hit, spread((number & 63).astype(F32), tile_rows), 0.0)
        left = jnp.concatenate([coarse, fine], axis=0).astype(jnp.bfloat16)
        right = jnp.where(spread(low, LANES) == iota((LANES, slots), 0), 1.0, 0.0).astype(jnp.bfloat16)
        both = lax.dot_general(left, right, (((1,), (1,)), ((), ())), preferred_element_type=F32)
        inverse_ref[...] = both[:tile_rows] * 64.0 + both[tile_rows:]


EARLY = 16


def ahead_first_kernel(field_ref, flag_ref, inverse_ref, send_ref, last_ref, export_ref, partial_ref, pick_ref, export_index_ref, export_pick_ref, index_ref):
    stage_index(send_ref, 1, index_ref)
    gather_outgoing(field_ref, flag_ref, index_ref, partial_ref, inverse_ref, pick_ref)
    blocks = export_ref.shape[1] // LANES
    for number in range(8):
        for block in range(blocks):
            at = number * blocks + block
            export_index_ref[at : at + 1, :] = export_ref[number : number + 1, LANES * block : LANES * (block + 1)]
    zero = jnp.zeros((8, LANES), F32)
    for part in range(blocks):
        rows = slice(8 * part, 8 * part + 8)
        export_pick_ref[rows, :] = pick_rows([last_ref], export_index_ref[rows, :], [zero])[0].astype(I32)


def ahead_kernel(level, field_ref, flag_ref, before_ref, in_ref, inverse_ref, send_ref, new_field_ref, new_flag_ref, partial_ref, pick_ref, index_ref, flag_in_ref):
    apply_incoming(field_ref, flag_ref, before_ref, in_ref, new_field_ref, new_flag_ref, flag_in_ref)
    stage_index(send_ref, level + 1, index_ref)
    gather_outgoing(new_field_ref, new_flag_ref, index_ref, partial_ref, inverse_ref, pick_ref)


def fix_kernel(partial_ref, pick_ref, in_ref, out_ref):
    count = pick_ref.shape[0]

    def body(step, carry):
        where = pl.ds(aligned(step * 8), 8)
        slot = pick_ref[pl.ds(step, 1), :] - 1
        out_ref[where, :] = pick_fields(row_blocks(in_ref, count), slot, partial_ref[where, :])
        return carry

    lax.fori_loop(0, count, body, 0, unroll=True)
    base = 8 * count
    for part in range(count // 8):
        slot = pick_ref[8 * part : 8 * part + 8, :] - 1
        tables = [in_ref.at[pl.ds(base, count)], in_ref.at[pl.ds(base + count, count)]]
        places = [slice(base + n * count + 8 * part, base + n * count + 8 * part + 8) for n in range(2)]
        found = pick_rows(tables, slot, [partial_ref[place, :] for place in places])
        for place, value in zip(places, found):
            out_ref[place, :] = value


def ahead_last_kernel(field_ref, flag_ref, inverse_ref, in_ref, index_ref, new_field_ref, new_flag_ref, early_ref, flag_in_ref):
    apply_incoming(field_ref, flag_ref, inverse_ref, in_ref, new_field_ref, new_flag_ref, flag_in_ref)
    gather_exports(new_field_ref, index_ref, 0, EARLY, early_ref, 0)


def gather_exports(field_ref, index_ref, first, count, out_ref, skip, in_ref=None, pick_ref=None):
    def body(step, carry):
        row = index_ref[pl.ds(first + step, 1), :]
        found = pick_fields(lane_blocks(field_ref), row, jnp.zeros((8, LANES), F32))
        if in_ref is not None:
            slot = pick_ref[pl.ds(first + step, 1), :] - 1
            found = pick_fields(row_blocks(in_ref, in_ref.shape[0] // 10), slot, found)
        out_ref[pl.ds(aligned((skip + step) * 8), 8), :] = found
        return carry

    lax.fori_loop(0, count, body, 0, unroll=8)


def last_kernel(field_ref, in_ref, index_ref, early_ref, pick_ref, low_ref, high_ref):
    blocks = index_ref.shape[0] // 8

    def body(step, carry):
        where = pl.ds(aligned(step * 8), 8)
        slot = pick_ref[pl.ds(step, 1), :] - 1
        low_ref[where, :] = pick_fields(row_blocks(in_ref, in_ref.shape[0] // 10), slot, early_ref[where, :])
        return carry

    lax.fori_loop(0, EARLY, body, 0, unroll=True)
    gather_exports(field_ref, index_ref, EARLY, 3 * blocks - EARLY, low_ref, EARLY, in_ref, pick_ref)
    gather_exports(field_ref, index_ref, 5 * blocks, 3 * blocks, high_ref, 0, in_ref, pick_ref)


EXPANDED = 8
NEAR_FIELDS = (0, 1, 2, 6)
SPEED_FIELDS = (3, 4, 5)
SLOPE_NORM = 0.375 * PARTICLE_MASS / math.pi


def derived(height):
    inverse = 1.0 / height
    square = inverse * inverse
    return inverse, SLOPE_NORM * (square * square)


def expand_targets(compact_ref, chunk, base, expanded_ref, fields=range(7), shift=0):
    groups = compact_ref.shape[0] // (4 * 32)
    region = (groups * 32 + 1) * 8
    half_base = jnp.where(iota((8, LANES), 1) < 64, 0, 64)
    for inner in range(8):
        for field in fields:
            index = half_base + (inner * 8 + field)
            for group in range(groups):
                for section in range(2):
                    for half in range(2):
                        place = ((group * 2 + section) * 2 + half) * 8
                        start = aligned(chunk * (groups * 32) + place)
                        tile = 2 * (group * 16 + section * 8 + inner) + half
                        value = lane_pick(compact_ref[pl.ds(start, 8), :], index)
                        first = base + (field - shift) * region + tile * 8
                        if field == 6:
                            inverse, norm = derived(value)
                            expanded_ref[pl.ds(aligned(first), 8), :] = inverse
                            expanded_ref[pl.ds(aligned(first + region), 8), :] = norm
                        else:
                            expanded_ref[pl.ds(aligned(first), 8), :] = value


def target_kernel(count_ref, old_field_ref, old_flag_ref, inverse_ref, in_ref, index_ref, pair_ref,
                  field_ref, flag_ref, middle_ref, compact_ref, rank_ref, order_ref, list_ref, length_ref, expanded_ref,
                  flag_in_ref, stack_ref):
    apply_incoming(old_field_ref, old_flag_ref, inverse_ref, in_ref, field_ref, flag_ref, flag_in_ref)
    blocks = index_ref.shape[0] // 8
    gather_exports(field_ref, index_ref, 3 * blocks, 2 * blocks, middle_ref, 0)
    tile_rows = flag_ref.shape[0]
    groups = tile_rows // 16
    tile_count = 2 * tile_rows
    region = (tile_count + 1) * 8
    active = flag_ref[...] > 0
    ones = jnp.where(active, 1.0, 0.0).astype(jnp.bfloat16)
    a = iota((LANES, LANES), 0)
    b = iota((LANES, LANES), 1)
    same = (a >> 6) == (b >> 6)
    before = jnp.where(same & (a < b), 1.0, 0.0).astype(jnp.bfloat16)
    whole = jnp.where(same, 1.0, 0.0).astype(jnp.bfloat16)
    rank = jnp.dot(ones, before, preferred_element_type=F32).astype(I32)
    total = jnp.dot(ones, whole, preferred_element_type=F32)
    rank_ref[...] = rank
    lane = iota((tile_rows, LANES), 1)
    code = jnp.where(active, lane + 128 * ((lane & 63) - rank), -1)
    for bit in range(6):
        moved = pltpu.roll(code, LANES - (1 << bit), 1)
        take = (moved >= 0) & (((moved >> (7 + bit)) & 1) == 1)
        keep = (code >= 0) & (((code >> (7 + bit)) & 1) == 0)
        code = jnp.where(take, moved, jnp.where(keep, code, -1))
    order_ref[...] = jnp.where(code >= 0, code & 127, lane)
    left_half = iota((8, LANES), 1) < 64
    for group in range(groups):
        for inner in range(16):
            row = group * 16 + inner
            stack_ref[8 * inner : 8 * inner + 8, :] = lane_pick(
                field_ref[:, LANES * row : LANES * (row + 1)], spread(order_ref[row : row + 1, :])
            )
        turned = jnp.transpose(stack_ref[...])
        for half in range(2):
            for chunk in range(4):
                first = half * 64 + chunk * 16
                near, far = turned[first : first + 8], turned[first + 8 : first + 16]
                for section in range(2):
                    if section == 0:
                        mixed = jnp.where(left_half, near, pltpu.roll(far, 64, 1))
                    else:
                        mixed = jnp.where(left_half, pltpu.roll(near, 64, 1), far)
                    place = (((chunk * groups + group) * 2 + section) * 2 + half) * 8
                    compact_ref[place : place + 8, :] = mixed

    pairs = pair_ref.shape[1]
    slots = list_ref.shape[1]
    target, source = pair_ref[0:1, :], pair_ref[1:2, :]
    folded = jnp.where((lane & 63) == iota((tile_rows, LANES), 0), total, 0.0)
    totals = spread(jnp.sum(folded, axis=0, keepdims=True))
    place = spread((target & 1) * 64 + (target >> 1))
    need = jnp.concatenate(
        [lane_pick(totals, place[:, LANES * q : LANES * (q + 1)]) for q in range(pairs // LANES)], axis=1
    )
    sub = iota((8, pairs), 0)
    is_ghost = spread(source) >= tile_count
    member = (
        (iota((8, pairs), 1) < count_ref[0])
        & (need > (16 * (sub & 3)).astype(F32))
        & (is_ghost == (sub >= 4))
    )
    member_value = jnp.where(member, 1.0, 0.0)
    earlier = jnp.where(iota((pairs, pairs), 0) < iota((pairs, pairs), 1), 1.0, 0.0).astype(jnp.bfloat16)
    position = jnp.dot(member_value.astype(jnp.bfloat16), earlier, preferred_element_type=F32).astype(I32)
    length = jnp.broadcast_to(jnp.sum(member_value, axis=1, keepdims=True), (8, LANES)).astype(I32)
    length_ref[...] = length
    own_steps = ((length + (UNROLL - 1)) // UNROLL) * UNROLL
    base = jnp.where(iota((8, LANES), 0) >= 4, pltpu.roll(own_steps, 4, 0), 0)
    position = position + jnp.concatenate([base] * (pairs // LANES), axis=1)
    position = jnp.where(member, position, -1)
    local = jnp.where(source >= tile_count, source - tile_count, source)
    values = jnp.where(
        sub == 0, spread(target + 1), jnp.where(sub == 1, spread(local + 1), 0)
    ).astype(F32).astype(jnp.bfloat16)

    def make_list(chunk):
        row = jnp.maximum(position[chunk : chunk + 1, :], position[chunk + 4 : chunk + 5, :])
        hit = jnp.where(spread(row, slots) == iota((slots, pairs), 0), 1.0, 0.0).astype(jnp.bfloat16)
        found = lax.dot_general(
            values, hit, (((1,), (1,)), ((), ())), preferred_element_type=F32
        ).astype(I32)
        list_ref[chunk : chunk + 1, :] = jnp.where(found[0:1] > 0, found[0:1] - 1, tile_count) * 8
        list_ref[4 + chunk : 5 + chunk, :] = jnp.maximum(found[1:2] - 1, 0) * 8

    make_list(0)
    make_list(1)

    @pl.when(jnp.max(total) > 32.0)
    def _():
        make_list(2)
        make_list(3)

    def one_chunk(chunk, carry):
        expand_targets(compact_ref, chunk, aligned(chunk * (EXPANDED * region)), expanded_ref, NEAR_FIELDS)
        return carry

    lax.fori_loop(0, 2, one_chunk, 0)


def reduce_targets(sum_ref, first, tile_count, section, out_ref):
    blocks = tile_count // 16
    for block in range(blocks):
        start = first + block * LANES
        turned = jnp.transpose(sum_ref[start : start + LANES, :])
        for half in range(2):
            total = jnp.sum(turned[64 * half : 64 * half + 64], axis=0, keepdims=True)
            out_ref[pl.ds((section * 2 + half) * blocks + block, 1), :] = total


def place_results(red_ref, blocks, part, rank):
    row = iota((8, LANES), 0)
    half = iota((8, LANES), 1) >> 6
    index = (2 * row + half) * 8 + (rank & 7)
    which = rank >> 3
    found = jnp.zeros((8, LANES), F32)
    for section in range(8):
        table = spread(red_ref[section * blocks + part : section * blocks + part + 1, :])
        found = jnp.where(which == section, lane_pick(table, index), found)
    return found


def clear(sum_ref, first, rows):
    for at in range(0, rows, 8):
        sum_ref[first + at : first + at + 8, :] = jnp.zeros((8, LANES), F32)


def steps_of(length):
    return (length + (UNROLL - 1)) // UNROLL


def span(length_ref, chunk, ghost):
    own = steps_of(length_ref[chunk, 0])
    if not ghost:
        return 0, own
    return own, own + steps_of(length_ref[chunk + 4, 0])


def double_into(pool_ref, row, value):
    left = iota((8, LANES), 1) < 64
    other = pltpu.roll(value, 64, 1)
    pool_ref[16 * row : 16 * row + 8, :] = jnp.where(left, value, other)
    pool_ref[16 * row + 8 : 16 * row + 16, :] = jnp.where(left, other, value)


def density_pairs(list_ref, length_ref, chunk, ghost, expanded_ref, base, region, pool_ref, sum_ref, sum_base):
    def step(number, carry):
        results = []
        for u in range(UNROLL):
            target = list_ref[chunk, number * UNROLL + u]
            source = list_ref[chunk + 4, number * UNROLL + u]

            def at(field, target=target):
                return expanded_ref[pl.ds(aligned(target + (base + field * region)), 8), :]

            square = None
            for axis in range(3):
                gap = at(axis) - pool_ref[pl.ds(source + axis, 8, stride=0), :]
                gap = gap - jnp.floor(gap + 0.5)
                square = gap * gap if square is None else square + gap * gap
            safe = jnp.maximum(square, 1.2e-38)
            ratio = safe * lax.rsqrt(safe) * at(6)
            outer = jnp.maximum(2.0 - ratio, 0.0)
            inner = jnp.maximum(1.0 - ratio, 0.0)
            results.append((target, 0.25 * (outer * outer * outer) - inner * inner * inner))
        for target, value in results:
            sum_ref[pl.ds(aligned(target + sum_base), 8), :] += value
        return carry

    first, last = span(length_ref, chunk, ghost)
    lax.fori_loop(first, last, step, 0)


def density_own_kernel(list_ref, length_ref, field_ref, expanded_ref, compact_ref, pool_ref, sum_ref, speed_ref):
    tile_rows = field_ref.shape[1] // LANES
    region = (2 * tile_rows + 1) * 8
    for row in range(tile_rows):
        double_into(pool_ref, row, field_ref[:, LANES * row : LANES * (row + 1)])
    clear(sum_ref, 0, 2 * region)
    for chunk in range(2):
        density_pairs(
            list_ref, length_ref, chunk, False, expanded_ref, chunk * EXPANDED * region, region,
            pool_ref, sum_ref, chunk * region,
        )

    def one_chunk(chunk, carry):
        expand_targets(compact_ref, chunk, aligned(chunk * (3 * region)), speed_ref, SPEED_FIELDS, 3)
        return carry

    lax.fori_loop(0, 2, one_chunk, 0)


def density_kernel(list_ref, length_ref, compact_ref, expanded_ref, own_pool_ref, own_sum_ref, rank_ref, field_ref, flag_ref, low_ref, high_ref, down_ref, up_ref, export_ref,
                   density_ref, low_out, middle_out, high_out, pool_ref, sum_ref, result_ref,
                   red_ref, height_ref, spare_ref):
    tile_rows = flag_ref.shape[0]
    tile_count = 2 * tile_rows
    region = (tile_count + 1) * 8
    ghosts = (low_ref, high_ref, down_ref, up_ref)
    unit = low_ref.shape[0] // 3
    blocks = unit // 8
    for number, (which, start) in enumerate(ghost_place(unit)):
        for block in range(blocks):
            first = start + 8 * block
            double_into(pool_ref, number * blocks + block, ghosts[which][first : first + 8, :])
    for chunk in range(2):
        density_pairs(
            list_ref, length_ref, chunk, True, expanded_ref, chunk * EXPANDED * region, region,
            pool_ref, sum_ref, chunk * region,
        )
        reduce_targets(sum_ref, chunk * region, tile_count, chunk, red_ref)
    for row in range(4 * (tile_count // 16), 8 * (tile_count // 16), 8):
        red_ref[row : row + 8, :] = jnp.zeros((8, LANES), F32)

    def rare_chunk(chunk, carry):
        @pl.when(length_ref[chunk, 0] + length_ref[chunk + 4, 0] > 0)
        def _():
            expand_targets(compact_ref, chunk, 0, spare_ref)
            clear(sum_ref, 0, region)
            density_pairs(list_ref, length_ref, chunk, False, spare_ref, 0, region, own_pool_ref, sum_ref, 0)
            density_pairs(list_ref, length_ref, chunk, True, spare_ref, 0, region, pool_ref, sum_ref, 0)
            reduce_targets(sum_ref, 0, tile_count, chunk, red_ref)

        return carry

    lax.fori_loop(2, 4, rare_chunk, 0)
    for row in range(tile_rows):
        height_ref[row : row + 1, :] = field_ref[6:7, LANES * row : LANES * (row + 1)]
    for part in range(tile_rows // 8):
        rows = slice(8 * part, 8 * part + 8)
        found = place_results(red_ref, tile_count // 16, part, rank_ref[rows, :])
        height = height_ref[rows, :]
        flag = flag_ref[rows, :]
        norm = PARTICLE_MASS / (math.pi * height * height * height)
        density_ref[rows, :] = jnp.where(flag > 0, norm * (1.0 + found), jnp.abs(flag))
        result_ref[rows, :] = density_ref[rows, :]
    outs = (low_out, middle_out, high_out)
    zero = jnp.zeros((8, LANES), F32)
    for block in range(blocks):
        index = export_ref[:, LANES * block : LANES * (block + 1)]
        found = pick_rows([density_ref], index, [zero])[0]
        for number, (which, start) in enumerate(export_place(blocks)):
            outs[which][start + block : start + block + 1, :] = found[number : number + 1, :]


def source_tables(pool_ref, tile, first_ref, second_ref, density=None):
    sub = iota((8, LANES), 0)
    rows = slice(8 * tile, 8 * tile + 8)
    value = pool_ref[rows, :]
    inverse, norm = derived(value)
    press = (ADIABATIC - 1.0) * value
    if density is not None:
        press = press / density
    first_ref[rows, :] = jnp.where(sub == 7, press, jnp.where(sub == 6, inverse, value))
    second_ref[rows, :] = norm


def doubled_halves(row):
    left = iota((8, LANES), 1) < 64
    wide = spread(row)
    other = pltpu.roll(wide, 64, 1)
    return jnp.where(left, wide, other), jnp.where(left, other, wide)


def force_pairs(list_ref, length_ref, chunk, ghost, expanded_ref, base, speed_ref, speed_base, region, press_ref, press_base, first_ref, second_ref, sum_ref):
    def step(number, carry):
        results = []
        for u in range(UNROLL):
            target = list_ref[chunk, number * UNROLL + u]
            source = list_ref[chunk + 4, number * UNROLL + u]

            def at(field, target=target):
                return expanded_ref[pl.ds(aligned(target + (base + field * region)), 8), :]

            def speed(axis, target=target):
                return speed_ref[pl.ds(aligned(target + (speed_base + axis * region)), 8), :]

            def source_row(field, source=source):
                return first_ref[pl.ds(source + field, 8, stride=0), :]

            def source_more(field, source=source):
                return second_ref[pl.ds(source + field, 8, stride=0), :]

            gaps = []
            square = None
            approach = None
            for axis in range(3):
                gap = at(axis) - source_row(axis)
                gap = gap - jnp.floor(gap + 0.5)
                gaps.append(gap)
                square = gap * gap if square is None else square + gap * gap
                part = (speed(axis) - source_row(3 + axis)) * gap
                approach = part if approach is None else approach + part
            safe = jnp.maximum(square, 1.2e-38)
            inverse_distance = lax.rsqrt(safe)
            distance = safe * inverse_distance

            def slope(inverse_height, norm):
                ratio = distance * inverse_height
                outer = 2.0 - ratio
                inner = jnp.maximum(outer - ratio, 0.0)
                outer = jnp.maximum(outer, 0.0)
                return norm * (inner * inner - outer * outer)

            total = slope(at(6), at(7)) + slope(source_row(6), source_more(6))
            press = press_ref[pl.ds(aligned(target + press_base), 8), :] + source_row(7)
            weight = press * (total * inverse_distance)
            results.append((target, [weight * gap for gap in gaps] + [weight * approach]))
        for target, values in results:
            for quantity in range(4):
                sum_ref[pl.ds(aligned(target + quantity * region), 8), :] += values[quantity]
        return carry

    first, last = span(length_ref, chunk, ghost)
    lax.fori_loop(first, last, step, 0)


def expand_press(press_compact_ref, chunk, tile_rows, press_ref, base):
    half_base = jnp.where(iota((8, LANES), 1) < 64, 0, 64)
    for row in range(tile_rows):
        for half in range(2):
            start = aligned(chunk * 16 + half * 8)
            first = base + (2 * row + half) * 8
            press_ref[first : first + 8, :] = lane_pick(
                press_compact_ref[pl.ds(start, 8), :], half_base + row
            )


def force_own_kernel(list_ref, length_ref, density_ref, field_ref, order_ref, expanded_ref, speed_ref, pool_ref,
                     first_ref, second_ref, press_compact_ref, press_ref, sum_ref,
                     energy_ref, ordered_ref):
    tile_rows = density_ref.shape[0]
    tile_count = 2 * tile_rows
    region = (tile_count + 1) * 8
    left = iota((8, LANES), 1) < 64
    for row in range(tile_rows):
        near, far = doubled_halves(density_ref[row : row + 1, :])
        source_tables(pool_ref, 2 * row, first_ref, second_ref, near)
        source_tables(pool_ref, 2 * row + 1, first_ref, second_ref, far)
        energy_ref[row : row + 1, :] = field_ref[7:8, LANES * row : LANES * (row + 1)]
    for part in range(tile_rows // 8):
        rows = slice(8 * part, 8 * part + 8)
        press = (ADIABATIC - 1.0) * energy_ref[rows, :] / density_ref[rows, :]
        ordered_ref[rows, :] = lane_pick(press, order_ref[rows, :])
    ordered_ref[tile_rows:, :] = jnp.zeros((LANES - tile_rows, LANES), F32)
    turned = jnp.transpose(ordered_ref[...])
    for half in range(2):
        for chunk in range(4):
            first = half * 64 + chunk * 16
            near, far = turned[first : first + 8], turned[first + 8 : first + 16]
            place_at = (chunk * 2 + half) * 8
            press_compact_ref[place_at : place_at + 8, :] = jnp.where(left, near, pltpu.roll(far, 64, 1))
    for chunk in range(2):
        expand_press(press_compact_ref, chunk, tile_rows, press_ref, chunk * region)
    clear(sum_ref, 0, 4 * region)
    force_pairs(
        list_ref, length_ref, 0, False, expanded_ref, 0, speed_ref, 0, region, press_ref, 0, first_ref, second_ref, sum_ref,
    )


def force_own_more_kernel(list_ref, length_ref, expanded_ref, speed_ref, press_ref, own_first_ref, own_second_ref, pool_ref,
                          sum_ref, first_ref, second_ref):
    region = sum_ref.shape[0] // 4
    for tile in range(pool_ref.shape[0] // 8):
        source_tables(pool_ref, tile, first_ref, second_ref)
    clear(sum_ref, 0, 4 * region)
    force_pairs(
        list_ref, length_ref, 1, False, expanded_ref, EXPANDED * region, speed_ref, 3 * region, region, press_ref, region,
        own_first_ref, own_second_ref, sum_ref,
    )


def force_kernel(list_ref, length_ref, compact_ref, expanded_ref, speed_ref, press_compact_ref, press_ref, rank_ref, flag_ref, own_first_ref, own_second_ref, half_ref, second_ref, zero_sum_ref, one_sum_ref, low_ref, high_ref, down_ref, up_ref,
                 accel_ref, heat_ref, first_sum_ref, second_sum_ref,
                 first_ref, sum_ref, red_ref, spare_ref, spare_press_ref):
    tile_rows = flag_ref.shape[0]
    tile_count = 2 * tile_rows
    region = (tile_count + 1) * 8
    blocks = tile_count // 16
    is_press = iota((8, LANES), 0) == 7
    ghosts = (low_ref, high_ref, down_ref, up_ref)
    unit = low_ref.shape[0] // 3
    for number, (which, start) in enumerate(ghost_place(unit)):
        for block in range(unit):
            row = number * unit + block
            for half, density in enumerate(doubled_halves(ghosts[which][start + block : start + block + 1, :])):
                rows = slice(16 * row + 8 * half, 16 * row + 8 * half + 8)
                value = half_ref[rows, :]
                first_ref[rows, :] = jnp.where(is_press, value / density, value)
    for chunk in range(2):
        chunk_sum_ref = first_sum_ref if chunk == 0 else second_sum_ref
        force_pairs(
            list_ref, length_ref, chunk, True, expanded_ref, chunk * EXPANDED * region,
            speed_ref, chunk * 3 * region, region,
            press_ref, chunk * region, first_ref, second_ref, chunk_sum_ref,
        )
        for quantity in range(4):
            reduce_targets(chunk_sum_ref, quantity * region, tile_count, chunk + 4 * quantity, red_ref)
    for quantity in range(4):
        for row in range(4 * blocks, 8 * blocks, 8):
            at = quantity * 8 * blocks + row
            red_ref[at : at + 8, :] = jnp.zeros((8, LANES), F32)

    def rare_chunk(chunk, carry):
        @pl.when(length_ref[chunk, 0] + length_ref[chunk + 4, 0] > 0)
        def _():
            expand_targets(compact_ref, chunk, 0, spare_ref)
            expand_press(press_compact_ref, chunk, tile_rows, spare_press_ref, 0)
            clear(sum_ref, 0, 4 * region)
            force_pairs(
                list_ref, length_ref, chunk, False, spare_ref, 0, spare_ref, 3 * region, region, spare_press_ref, 0,
                own_first_ref, own_second_ref, sum_ref,
            )
            force_pairs(
                list_ref, length_ref, chunk, True, spare_ref, 0, spare_ref, 3 * region, region, spare_press_ref, 0,
                first_ref, second_ref, sum_ref,
            )
            for quantity in range(4):
                reduce_targets(sum_ref, quantity * region, tile_count, chunk + 4 * quantity, red_ref)

        return carry

    lax.fori_loop(2, 4, rare_chunk, 0)
    for part in range(tile_rows // 8):
        rank = rank_ref[8 * part : 8 * part + 8, :]
        flag = flag_ref[8 * part : 8 * part + 8, :]
        for quantity in range(4):
            found = place_results(red_ref.at[pl.ds(quantity * 8 * blocks, 8 * blocks)], blocks, part, rank)
            if quantity == 3:
                heat_ref[8 * part : 8 * part + 8, :] = jnp.where(flag > 0, 0.5 * found, 0.0)
            else:
                found = jnp.where(flag > 0, -found, 0.0)
                for row in range(8):
                    at = LANES * (8 * part + row)
                    accel_ref[quantity : quantity + 1, at : at + LANES] = found[row : row + 1, :]


def call(kernel, outs, scratch, operands, scalars=0, aliases=None):
    smem = pl.BlockSpec(memory_space=pltpu.SMEM)
    vmem = pl.BlockSpec(memory_space=pltpu.VMEM)
    return pl.pallas_call(
        kernel,
        out_shape=[jax.ShapeDtypeStruct(shape, dtype) for shape, dtype in outs],
        in_specs=[smem if i < scalars else vmem for i in range(len(operands))],
        out_specs=[vmem] * len(outs),
        scratch_shapes=[pltpu.VMEM(shape, dtype) for shape, dtype in scratch],
        input_output_aliases=aliases or {},
        compiler_params=pltpu.CompilerParams(vmem_limit_bytes=24 * 2**20),
    )(*operands)


def on_device(
    particles, old_density, active, send_rows, send_count, export_rows, pair_tiles, pair_count
):
    row_count = particles.shape[1]
    levels, slots = send_rows.shape
    ghosts = export_rows.shape[1]
    pair_total = pair_tiles.shape[1]
    tile_rows = row_count // LANES
    tile_count = 2 * tile_rows
    in_blocks = slots // LANES
    unit = 8 * (ghosts // LANES)
    dense_unit = ghosts // LANES
    region = (tile_count + 1) * 8
    list_slots = -(-(pair_total + 2 * UNROLL) // LANES) * LANES
    bits_x = lax.axis_size("gx").bit_length() - 1
    bits_y = lax.axis_size("gy").bit_length() - 1

    row = ((tile_rows, LANES), F32)
    whole = ((8, row_count), F32)
    offered = ((10 * in_blocks, LANES), F32)
    picked = ((in_blocks, LANES), I32)
    index_scratch = ((in_blocks, LANES), I32)
    flag_scratch = ((in_blocks, LANES), F32)
    exported = [((3 * unit, LANES), F32), ((2 * unit, LANES), F32), ((3 * unit, LANES), F32)]

    def swap(block, level):
        if level < 2:
            return from_partner(block, "gx", bits_x - 1 - level)
        return from_partner(block, "gy", bits_y + 1 - level)

    flag = jnp.where(active == 1, old_density, -old_density).reshape(tile_rows, LANES)
    fields, outgoing, send_rows = call(
        first_kernel,
        [whole, offered, (send_rows.shape, I32)],
        [index_scratch],
        [particles, flag, send_rows],
    )
    incoming = swap(outgoing, 0)
    inverse = call(inverse_kernel, [row] * levels, [], [send_count[:, 0], send_rows], scalars=1)
    export_rows_shape = ((8 * dense_unit, LANES), I32)
    partial, pick, export_index, export_pick = call(
        ahead_first_kernel,
        [offered, picked, export_rows_shape, export_rows_shape],
        [index_scratch],
        [fields, flag, inverse[0], send_rows, inverse[3], export_rows],
    )
    (outgoing,) = call(fix_kernel, [offered], [], [partial, pick, incoming])
    before = incoming
    incoming = swap(outgoing, 1)
    ahead = [whole, row, offered, picked]
    ahead_scratch = [index_scratch, flag_scratch]
    fields, flag, partial, pick = call(
        lambda *refs: ahead_kernel(1, *refs),
        ahead,
        ahead_scratch,
        [fields, flag, inverse[0], before, inverse[1], send_rows],
    )
    (outgoing,) = call(fix_kernel, [offered], [], [partial, pick, incoming])
    before = incoming
    incoming = swap(outgoing, 2)
    fields, flag, partial, pick = call(
        lambda *refs: ahead_kernel(2, *refs),
        ahead,
        ahead_scratch,
        [fields, flag, inverse[1], before, inverse[2], send_rows],
    )
    (outgoing,) = call(fix_kernel, [offered], [], [partial, pick, incoming])
    before = incoming
    incoming = swap(outgoing, 3)
    fields, flag, early = call(
        ahead_last_kernel,
        [whole, row, ((8 * EARLY, LANES), F32)],
        [flag_scratch],
        [fields, flag, inverse[2], before, export_index],
    )
    low, high = call(
        last_kernel,
        [exported[0], exported[2]],
        [],
        [fields, incoming, export_index, early, export_pick],
    )
    low, high = along_x(low, high)
    fields, flag, middle, compact, rank, order, lists, lengths, expanded = call(
        target_kernel,
        [
            whole,
            row,
            exported[1],
            ((8 * tile_rows, LANES), F32),
            ((tile_rows, LANES), I32),
            ((tile_rows, LANES), I32),
            ((8, list_slots), I32),
            ((8, LANES), I32),
            ((2 * EXPANDED * region, LANES), F32),
        ],
        [flag_scratch, ((LANES, LANES), F32)],
        [pair_count, fields, flag, inverse[3], incoming, export_index, pair_tiles],
        scalars=1,
    )
    low, high, lengths = lax.optimization_barrier((low, high, lengths))
    down, up = along_y(low, middle, high, unit)
    pool_shape = ((tile_count * 8 + 8, LANES), F32)
    ghost_pool_shape = ((2 * 8 * dense_unit * 8 + 8, LANES), F32)
    own_pool, own_sum, speed = call(
        density_own_kernel,
        [pool_shape, ((2 * region, LANES), F32), ((6 * region, LANES), F32)],
        [],
        [lists, lengths, fields, expanded, compact],
        scalars=2,
    )
    density, low_d, middle_d, high_d, ghost_pool, _, density_out = call(
        density_kernel,
        [
            row,
            ((3 * dense_unit, LANES), F32),
            ((2 * dense_unit, LANES), F32),
            ((3 * dense_unit, LANES), F32),
            ghost_pool_shape,
            ((2 * region, LANES), F32),
            row,
        ],
        [
            ((8 * (tile_count // 16), LANES), F32),
            row,
            ((EXPANDED * region, LANES), F32),
        ],
        [
            lists, lengths, compact, expanded, own_pool, own_sum,
            rank, fields, flag, low, high, down, up, export_rows,
        ],
        scalars=2,
        aliases={5: 5},
    )
    low_d, high_d = along_x(low_d, high_d)
    sums = ((4 * region, LANES), F32)
    own_first, own_second, press_compact, press, zero_sum = call(
        force_own_kernel,
        [pool_shape, pool_shape, ((64, LANES), F32), ((2 * region, LANES), F32), sums],
        [row, ((LANES, LANES), F32)],
        [lists, lengths, density, fields, order, expanded, speed, own_pool],
        scalars=2,
    )
    low_d, high_d, press = lax.optimization_barrier((low_d, high_d, press))
    down_d, up_d = along_y(low_d, middle_d, high_d, dense_unit)
    one_sum, ghost_first, ghost_second = call(
        force_own_more_kernel,
        [sums, ghost_pool_shape, ghost_pool_shape],
        [],
        [lists, lengths, expanded, speed, press, own_first, own_second, ghost_pool],
        scalars=2,
    )
    accel, heat, _, _ = call(
        force_kernel,
        [((3, row_count), F32), row, sums, sums],
        [
            ghost_pool_shape,
            sums,
            ((32 * (tile_count // 16), LANES), F32),
            ((EXPANDED * region, LANES), F32),
            ((region, LANES), F32),
        ],
        [
            lists, lengths, compact, expanded, speed, press_compact, press, rank, flag,
            own_first, own_second, ghost_first, ghost_second, zero_sum, one_sum,
            low_d, high_d, down_d, up_d,
        ],
        scalars=2,
        aliases={13: 2, 14: 3},
    )
    return (density_out.reshape(row_count), accel, heat.reshape(row_count))


def solution(mesh):
    in_specs = (
        P(None, ("gx", "gy")),
        P(("gx", "gy")),
        P(("gx", "gy")),
        P(None, ("gx", "gy")),
        P(None, ("gx", "gy")),
        P(None, ("gx", "gy")),
        P(None, ("gx", "gy")),
        P(("gx", "gy")),
    )
    out_specs = (P(("gx", "gy")), P(None, ("gx", "gy")), P(("gx", "gy")))
    return jax.shard_map(
        on_device, mesh=mesh, in_specs=in_specs, out_specs=out_specs, check_vma=False
    )
```
